32 devices in a mesh: seq: 2 (over x), tensor: 4 (over z), dp: 4 (over y, core).
Axes of the slice: x: 2, y: 2, z: 4, core: 2. Of those that a mesh axis runs over, the one named last changes fastest.
Arguments:
- span_act: bfloat16 [2048, 8192], P(('seq', 'dp'), 'tensor'), may hold values from -6 to 6
- q_weight: bfloat16 [8192, 4096], P(('seq', 'dp'), 'tensor'), may hold values from -0.0625 to 0.0625
- out_grad: bfloat16 [2048, 4096], P(('seq', 'dp'), 'tensor'), may hold values from -6 to 6
- neighbour_kv: bfloat16 [64, 2, 256, 4096], P(('seq', 'dp'), None, None, 'tensor'), may hold values from -210 to 210
- neighbour_ids: int32 [64, 256], P(('seq', 'dp')), may hold values from 0 to 255999, as said below
- owner: int32 [32], replicated, may hold values from 0 to 1, as said below
Outputs:
- act_grad: bfloat16 [2048, 8192], P(('seq', 'dp'), 'tensor')
- weight_grad: float32 [8192, 4096], P(('seq', 'dp'), 'tensor')
- kv_grad: bfloat16 [64, 2, 256, 4096], P(('seq', 'dp'), None, None, 'tensor')
The draws below stay inside these ranges and needn't reach their ends.
Inputs may be any that keep to these rules, and one draw needn't show every extreme that they name: owner[c] is the owner's index along seq within span c's own dp group. Of the 4 spans of one home block at most 4 name the same owner, and in each dp group some owner is named by 4 spans of every home block. `neighbour_ids`: each of the 2 neighbours of a slot takes 128 consecutive positions; its ids are positive on a leading run of 32 to 128 positions and 0 (padding) after it. Slots that no span names are never read.
All inputs are finite; a program needn't handle non-finite values.
Results may differ from the reference program's by a relative error of at most 0.022.
The reference program's roundings to bfloat16 on the way count: a program that leaves them out, or rounds other values in their place, can miss the bound.
Values may be sent and summed in bfloat16 or wider, within the bound.
No kernel may reach another device: no remote copies, remote signals or barrier semaphores. Data moves between devices by JAX's collectives and lax.ppermute only.
A program may use at most 128 MiB of HBM per device.

```python
import jax
import jax.numpy as jnp
from jax import lax

D = 8192
HD = 128
SPAN = 64
NEIGH = 2
NLEN = 128
VOCAB = 256000
CH_DEV = 4
PAIR = 4
CAP = 8
KEYS = 256
HW = 4096
TOK_DEV = 256
TOKENS = 2048
SPANS = 32
SLOTS = 64
N_SEQ = 2
N_TENSOR = 4
N_DP = 4


def draw_neighbour_kv(key, part):
    key = jax.random.fold_in(key, 33)
    shape = (SLOTS, 2, KEYS, HW)
    base = jax.random.normal(jax.random.fold_in(key, 1), shape, jnp.float32)
    return base.astype(jnp.bfloat16)


def draw_neighbour_ids(key, part):
    key = jax.random.fold_in(key, 22)
    lengths = jax.random.randint(jax.random.fold_in(key, 1), (SLOTS, NEIGH), NLEN // 4, NLEN + 1)
    lengths = lengths.at[0, NEIGH - 1].set(NLEN // 4)
    position = jnp.arange(NLEN)
    alive = position[None, None, :] < lengths[:, :, None]
    tokens = jax.random.randint(jax.random.fold_in(key, 2), (SLOTS, NEIGH, NLEN), 1, VOCAB)
    tokens = jnp.where(alive, tokens, 0).reshape(SLOTS, KEYS)
    tokens = tokens.at[0, 0].set(VOCAB - 1)
    return tokens.astype(jnp.int32)


def draw_owner(key, part):
    key = jax.random.fold_in(key, 11)
    blocks = N_SEQ * N_DP
    hottest = jax.random.randint(jax.random.fold_in(key, 1), (N_DP,), 0, N_SEQ)

    def one_block(block):
        sub = jax.random.fold_in(key, block + 100)
        chosen = hottest[block % N_DP]
        others = (chosen + 1 + jnp.arange((N_SEQ - 1) * PAIR) // PAIR) % N_SEQ
        others = jax.random.permutation(jax.random.fold_in(sub, 1), others)
        picks = jnp.concatenate([jnp.full((PAIR,), chosen), others[:CH_DEV - PAIR]])
        order = jax.random.permutation(jax.random.fold_in(sub, 2), CH_DEV)
        return picks[order]
    return jax.vmap(one_block)(jnp.arange(blocks)).reshape(-1).astype(jnp.int32)


def raised(result, key, source, target, shards_of, factor):
    owner, partner = [(jnp.arange(result.shape[axis_at]) // (result.shape[axis_at] // shards_of)).reshape([-1 if axis == axis_at else 1 for axis in range(result.ndim)]) for axis_at in (source, target)]
    chosen = jax.random.permutation(key, shards_of)[partner]
    strong = (owner == chosen) | (owner == (partner + shards_of // 2) % shards_of)
    return jnp.where(strong, factor * result, result)


def block_scale(rng, shape, shards, smallest, top_value):
    factor_of, own = 1.0, jax.random.fold_in(rng, 6)
    for dim, parts in shards:
        draws = jnp.exp(jax.random.uniform(jax.random.fold_in(own, dim), (parts,), jnp.float32, smallest / len(shards), top_value / len(shards)))
        factor_of = factor_of * jnp.repeat(draws, shape[dim] // parts).reshape([-1 if axis == dim else 1 for axis in range(len(shape))])
    return factor_of


def gaussian(rng, shape, scale, most, pieces=(), kind=jnp.bfloat16):
    drawn = jax.random.normal(rng, shape, jnp.float32) * scale
    if len(pieces) > 0:
        drawn = block_scale(rng, shape, pieces, -0.22, 0.18) * drawn
    return jnp.clip(drawn, min=-most, max=most).astype(kind)


def noise_with(rng, dims, scale, bound, cuts, heavy, kind=jnp.bfloat16):
    drawn = scale * jax.random.normal(rng, dims, jnp.float32)
    if cuts:
        drawn = drawn * block_scale(rng, dims, cuts, -0.22, 0.18)
    return jnp.clip(raised(drawn, jax.random.fold_in(rng, 3), *heavy), -bound, bound).astype(kind)


def setup_inputs(seed: int = 0) -> dict:
    arg_keys = jax.random.split(jax.random.key(seed), 7)
    return {
        "span_act": noise_with(arg_keys[0], (TOKENS, D), 1.0, 6.0, ((0, 8), (1, 4)), (0, 1, 8, 2.0)),
        "q_weight": gaussian(arg_keys[1], (D, HW), D ** -0.5, 0.0625, ((0, 8), (1, 4))),
        "out_grad": gaussian(arg_keys[2], (TOKENS, HW), 1.0, 6.0, ((0, 8), (1, 4))),
        "neighbour_kv": draw_neighbour_kv(jax.random.fold_in(arg_keys[6], 71), 0),
        "neighbour_ids": draw_neighbour_ids(jax.random.fold_in(arg_keys[6], 71), 0),
        "owner": draw_owner(jax.random.fold_in(arg_keys[6], 71), 0),
    }


def settle(values):
    return lax.optimization_barrier(values.astype(jnp.bfloat16)).astype(jnp.float32)


def attend_back(queries, grads, pair_kv, live):
    rows, width = queries.shape
    heads = width // HD
    scale = HD ** -0.5
    query_heads = queries.astype(jnp.float32).reshape(rows, heads, HD)
    grad_heads = grads.astype(jnp.float32).reshape(rows, heads, HD)
    key_heads = pair_kv[0].astype(jnp.float32).reshape(-1, heads, HD)
    value_heads = pair_kv[1].astype(jnp.float32).reshape(-1, heads, HD)
    scores = jnp.einsum('qhd,khd->hqk', query_heads, key_heads) * scale
    scores = jnp.where(live[None, None, :], scores, -1e30)
    top = jnp.max(scores, axis=-1, keepdims=True)
    expo = jnp.exp(scores - top)
    probs = expo / jnp.sum(expo, axis=-1, keepdims=True)
    value_grad = jnp.einsum('hqk,qhd->khd', settle(probs), grad_heads)
    prob_grad = jnp.einsum('qhd,khd->hqk', grad_heads, value_heads)
    center = jnp.sum(probs * prob_grad, axis=-1, keepdims=True)
    score_grad = settle(probs * (prob_grad - center) * scale)
    query_grad = jnp.einsum('hqk,khd->qhd', score_grad, key_heads)
    key_grad = jnp.einsum('hqk,qhd->khd', score_grad, query_heads)
    both = jnp.stack([key_grad, value_grad], axis=0).reshape(2, -1, width)
    return query_grad.reshape(rows, width).astype(jnp.bfloat16), both.astype(jnp.bfloat16)


def reference(span_act, q_weight, out_grad, neighbour_kv, neighbour_ids, owner):
    queries = jnp.dot(span_act, q_weight, preferred_element_type=jnp.float32).astype(jnp.bfloat16)
    blocks = N_SEQ * N_DP
    groups = owner.reshape(blocks, CH_DEV)
    position = jnp.arange(CH_DEV)
    same = groups[:, :, None] == groups[:, None, :]
    before = position[None, :] < position[:, None]
    rank = jnp.sum(same & before[None, :, :], axis=2).astype(jnp.int32)
    block_id = jnp.arange(blocks).astype(jnp.int32)[:, None]
    slot = ((groups * N_DP + block_id % N_DP) * CAP + (block_id // N_DP) * PAIR + rank).reshape(-1).astype(jnp.int32)
    q_spans = queries.reshape(SPANS, SPAN, HW)
    g_spans = out_grad.reshape(SPANS, SPAN, HW)
    live = neighbour_ids != 0

    def one(index):
        where = slot[index]
        return attend_back(q_spans[index], g_spans[index], neighbour_kv[where], live[where])

    span_qgrad, span_kv = lax.map(one, jnp.arange(SPANS).astype(jnp.int32))
    kv_grad = jnp.zeros(neighbour_kv.shape, jnp.bfloat16).at[slot].set(span_kv)
    query_grad = span_qgrad.reshape(TOKENS, HW)
    group_width = HW // N_TENSOR
    act_total = jnp.zeros((TOKENS, D), jnp.float32)
    for group in range(N_TENSOR):
        left = query_grad[:, group * group_width:(group + 1) * group_width]
        right = q_weight[:, group * group_width:(group + 1) * group_width]
        part = lax.dot_general(left, right, (((1,), (1,)), ((), ())), preferred_element_type=jnp.float32)
        act_total = act_total + settle(part)
    act_grad = act_total.astype(jnp.bfloat16)
    weight_total = jnp.zeros((D, HW), jnp.float32)
    for index in range(blocks):
        rows_act = span_act[index * TOK_DEV:(index + 1) * TOK_DEV]
        rows_grad = query_grad[index * TOK_DEV:(index + 1) * TOK_DEV]
        part = lax.dot_general(rows_act, rows_grad, (((0,), (0,)), ((), ())), preferred_element_type=jnp.float32)
        weight_total = weight_total + settle(part)
    return act_grad, weight_total, kv_grad
```

```python
import functools

import jax
import jax.numpy as jnp
from jax import lax
from jax.experimental import pallas as pl
from jax.experimental.pallas import tpu as pltpu
from jax.sharding import PartitionSpec as P

HD = 128
SPAN = 64
KEYS = 256
F32 = jnp.float32
BF16 = jnp.bfloat16


def dot(a, b, contract):
    return lax.dot_general(a, b, (contract, ((), ())), preferred_element_type=F32)


def shift(value, axis, step=1):
    if axis == "seq":
        size = lax.axis_size("seq")
        return lax.ppermute(value, "seq", [(i, (i + step) % size) for i in range(size)])
    size = lax.axis_size("dp")
    return lax.ppermute(value, "dp", [(i, (i + 2 * step) % size) for i in range(size)])


def swap(value):
    return lax.ppermute(value, "dp", [(i, i ^ 1) for i in range(lax.axis_size("dp"))])


def ring_gather(block, axis, size):
    blocks = [block]
    for _ in range(size - 1):
        blocks.append(shift(blocks[-1], axis))
    return blocks


def ring_reduce(blocks, axis):
    total = blocks[-1] if len(blocks) > 1 else blocks[0]
    size = len(blocks)
    for k in range(size - 1, 0, -1):
        total = shift(total.astype(BF16), axis, -1).astype(F32) + blocks[k - 1]
    return total


def attend_kernel(index_ref, named_ref, q_ref, g_ref, kv_ref, live_ref, *rest):
    dq_ref, grad_ref = rest[-2:]
    named = named_ref[pl.program_id(0)]
    heads = q_ref.shape[-1] // HD
    scale = HD ** (-0.5)

    @pl.when(named == 0)
    def _():
        dq_ref[...] = jnp.zeros_like(dq_ref)
        grad_ref[...] = jnp.zeros_like(grad_ref)

    @pl.when(named != 0)
    def _():
        live = live_ref[0] > 0.5
        zero = jnp.zeros((SPAN, HD), BF16)

        def diagonal(ref, start):
            one = ref[0, :, start:start + HD]
            two = ref[0, :, start + HD:start + 2 * HD]
            return jnp.concatenate(
                [jnp.concatenate([one, zero], axis=1), jnp.concatenate([zero, two], axis=1)], axis=0
            )

        for pair in range(heads // 2):
            start = pair * 2 * HD
            columns = slice(start, start + 2 * HD)
            q_two = diagonal(q_ref, start)
            g_two = diagonal(g_ref, start)
            keys = kv_ref[0, 0, :, columns]
            values = kv_ref[0, 1, :, columns]
            scores = jnp.where(live, dot(keys, q_two, ((1,), (1,))) * scale, -1e30)
            top = jnp.max(scores, axis=0, keepdims=True)
            expo = jnp.exp(scores - top)
            probs = expo * (1.0 / jnp.sum(expo, axis=0, keepdims=True))
            grad_ref[0, 1, :, columns] = dot(probs.astype(BF16), g_two, ((1,), (0,))).astype(BF16)
            prob_grad = dot(values, g_two, ((1,), (1,)))
            center = jnp.sum(probs * prob_grad, axis=0, keepdims=True)
            score_grad = (probs * (prob_grad - center) * scale).astype(BF16)
            grad_ref[0, 0, :, columns] = dot(score_grad, q_two, ((1,), (0,))).astype(BF16)
            both = dot(score_grad, keys, ((0,), (0,)))
            dq_ref[0, :, columns] = jnp.concatenate(
                [both[:SPAN, :HD], both[SPAN:, HD:]], axis=1
            ).astype(BF16)


def attend(index, named, queries, grads, kv, live, source, pairs, before):
    capacity, _, keys, width = kv.shape
    table = jnp.concatenate([index, jnp.reshape(source * pairs, (1,))]).astype(jnp.int32)
    span_block = pl.BlockSpec((1, SPAN, width), lambda r, t, n: (t[r], 0, 0))
    kv_block = pl.BlockSpec((1, 2, keys, width), lambda r, t, n: (t[pairs] + r, 0, 0, 0))
    live_block = pl.BlockSpec((1, keys, HD), lambda r, t, n: (t[pairs] + r, 0, 0))
    in_specs = [span_block, span_block, kv_block, live_block]
    operands = [table, named.astype(jnp.int32), queries, grads, kv, live]
    aliases = {}
    if before is not None:
        in_specs.append(pl.BlockSpec(memory_space=pl.ANY))
        operands.append(before)
        aliases = {len(operands) - 1: 1}
    heads = width // HD
    return pl.pallas_call(
        attend_kernel,
        grid_spec=pltpu.PrefetchScalarGridSpec(
            num_scalar_prefetch=2,
            grid=(pairs,),
            in_specs=in_specs,
            out_specs=[span_block, kv_block],
        ),
        out_shape=[
            jax.ShapeDtypeStruct(queries.shape, BF16),
            jax.ShapeDtypeStruct(kv.shape, BF16),
        ],
        input_output_aliases=aliases,
        compiler_params=pltpu.CompilerParams(vmem_limit_bytes=32 * 1024 * 1024),
        cost_estimate=pl.CostEstimate(
            flops=pairs * heads * 5 * 2 * SPAN * keys * HD * 4,
            bytes_accessed=pairs * 4 * keys * width * 2,
            transcendentals=pairs * heads * SPAN * keys,
        ),
    )(*operands)


def on_device(span_act, q_weight, out_grad, neighbour_kv, neighbour_ids, owner):
    rows, width = out_grad.shape
    depth = q_weight.shape[0]
    seq_count = lax.axis_size("seq")
    dp_count = lax.axis_size("dp")
    tensor_count = lax.axis_size("tensor")
    couples = dp_count // 2
    seq_at = lax.axis_index("seq")
    dp_at = lax.axis_index("dp")
    core = dp_at % 2
    spans = rows // SPAN
    capacity = neighbour_kv.shape[0]
    pairs = capacity // seq_count
    per = span_act.shape[1] // depth // 2

    act = span_act.reshape(rows, per, 2, depth)
    act_mine = lax.dynamic_index_in_dim(act, core, 2, keepdims=False).reshape(rows, per * depth)
    act_other = lax.dynamic_index_in_dim(act, 1 - core, 2, keepdims=False).reshape(rows, per * depth)
    act_both = jnp.concatenate([act_mine, swap(act_other)], axis=0)
    acts = lax.all_gather(act_both, "tensor", axis=0)

    cut = depth // 2
    seq_first = [
        ring_gather(block, "dp", couples) for block in ring_gather(q_weight[:cut], "seq", seq_count)
    ]
    dp_first = [
        ring_gather(block, "seq", seq_count) for block in ring_gather(q_weight[cut:], "dp", couples)
    ]

    def block_at(i, j):
        block = ((seq_at - i) % seq_count) * dp_count + ((dp_at // 2 - j) % couples) * 2
        return block // (2 * per), (block % (2 * per)) // 2

    def act_block(i, j):
        at, inner = block_at(i, j)
        return lax.dynamic_slice(acts, (at, 0, inner * depth), (1, 2 * rows, depth))[0]

    places = [(i, j) for i in range(seq_count) for j in range(couples)]
    partial = jnp.zeros((2 * rows, width), F32)
    for i, j in places:
        block = act_block(i, j)
        partial = partial + dot(block[:, :cut], seq_first[i][j], ((1,), (0,)))
        partial = partial + dot(block[:, cut:], dp_first[j][i], ((1,), (0,)))
    queries = (partial[:rows] + swap(partial[rows:])).astype(BF16)

    groups = owner.reshape(seq_count, dp_count, spans)
    groups = lax.dynamic_index_in_dim(groups, dp_at, 1, keepdims=False)

    def order(group, target):
        names = (group == target).astype(jnp.int32)
        count = jnp.sum(names)
        place = jnp.where(
            names == 1, jnp.cumsum(names) - 1, count + jnp.cumsum(1 - names) - 1
        )
        at = jnp.arange(spans)
        index = jnp.sum(jnp.where(place[None, :] == at[:, None], at[None, :], 0), axis=1)
        return index[:pairs], (at < count)[:pairs]

    whole_blocks = pairs == spans
    live = jnp.broadcast_to(
        (neighbour_ids != 0).astype(F32)[:, :, None], (capacity, KEYS, HD)
    )
    mine = lax.dynamic_index_in_dim(groups, seq_at, 0, keepdims=False)

    def to_owner(value, step):
        value = value.reshape(spans, SPAN, width)
        if not whole_blocks:
            index, _ = order(mine, (seq_at + step) % seq_count)
            value = jnp.take(value, index, axis=0)
        return shift(value, "seq", step) if step else value

    kv_grad = None
    query_grad = jnp.zeros((spans, SPAN, width), BF16)
    for step in range(seq_count):
        source = (seq_at - step) % seq_count
        group = lax.dynamic_index_in_dim(groups, source, 0, keepdims=False)
        index, named = order(group, seq_at)
        if not whole_blocks:
            index = jnp.arange(pairs)
        back, kv_grad = attend(
            index,
            named,
            to_owner(queries, step),
            to_owner(out_grad, step),
            neighbour_kv,
            live,
            source,
            pairs,
            kv_grad,
        )
        if step:
            back = shift(back, "seq", -step)
        if not whole_blocks:
            index, named = order(mine, (seq_at + step) % seq_count)
            hit = (index[:, None] == jnp.arange(spans)[None, :]) & named[:, None]
            back = jnp.sum(
                jnp.where(hit[:, :, None, None], back[:, None], jnp.zeros((), BF16)), axis=0
            )
        query_grad = query_grad + back
    flat_grad = query_grad.reshape(rows, width)
    both_grad = jnp.concatenate([flat_grad, swap(flat_grad)], axis=0)

    act_parts = jnp.zeros((tensor_count, 2 * rows, per * depth), BF16)
    for i, j in places:
        at, inner = block_at(i, j)
        weights = jnp.concatenate([seq_first[i][j], dp_first[j][i]], axis=0)
        part = dot(both_grad, weights, ((1,), (1,))).astype(BF16)
        act_parts = lax.dynamic_update_slice(act_parts, part[None], (at, 0, inner * depth))
    act_sum = lax.psum_scatter(act_parts, "tensor", scatter_dimension=0, tiled=False)
    kept = act_sum[:rows].reshape(rows, per, depth)
    arrived = swap(act_sum[rows:]).reshape(rows, per, depth)
    even = jnp.where(core == 0, kept, arrived)
    odd = jnp.where(core == 0, arrived, kept)
    act_grad = jnp.stack([even, odd], axis=2).reshape(rows, span_act.shape[1])

    products = {}
    for i, j in reversed(places):
        products[i, j] = dot(act_block(i, j), both_grad, ((0,), (0,)))
    upper = ring_reduce(
        [
            ring_reduce([products[i, j][:cut] for j in range(couples)], "dp")
            for i in range(seq_count)
        ],
        "seq",
    )
    lower = ring_reduce(
        [
            ring_reduce([products[i, j][cut:] for i in range(seq_count)], "seq")
            for j in range(couples)
        ],
        "dp",
    )
    weight_grad = jnp.concatenate([upper, lower], axis=0)
    return (act_grad, weight_grad, kv_grad)


def solution(mesh):
    in_specs = (
        P(("seq", "dp"), "tensor"),
        P(("seq", "dp"), "tensor"),
        P(("seq", "dp"), "tensor"),
        P(("seq", "dp"), None, None, "tensor"),
        P(("seq", "dp"), None),
        P(),
    )
    out_specs = (
        P(("seq", "dp"), "tensor"),
        P(("seq", "dp"), "tensor"),
        P(("seq", "dp"), None, None, "tensor"),
    )
    return jax.shard_map(
        on_device, mesh=mesh, in_specs=in_specs, out_specs=out_specs, check_vma=False
    )
```

```python
import functools

import jax
import jax.numpy as jnp
from jax import lax
from jax.experimental import pallas as pl
from jax.experimental.pallas import tpu as pltpu
from jax.sharding import PartitionSpec as P

HD = 128
SPAN = 64
KEYS = 256
F32 = jnp.float32
BF16 = jnp.bfloat16


def dot(a, b, contract):
    return lax.dot_general(a, b, (contract, ((), ())), preferred_element_type=F32)


def shift(value, axis, step=1):
    stride = 2 if axis == "dp" else 1
    size = lax.axis_size(axis)
    return lax.ppermute(value, axis, [(i, (i + step * stride) % size) for i in range(size)])


def swap(value):
    return lax.ppermute(value, "dp", [(i, i ^ 1) for i in range(lax.axis_size("dp"))])


def ring_gather(block, axis, size):
    blocks = [block]
    for _ in range(size - 1):
        blocks.append(shift(blocks[-1], axis))
    return blocks


def ring_reduce(blocks, axis):
    total = blocks[-1].astype(F32)
    for block in blocks[-2::-1]:
        total = shift(total.astype(BF16), axis, -1).astype(F32) + block.astype(F32)
    return total


def product_kernel(count, table_ref, *refs):
    blocks, weight_ref, out_ref = refs[:count], refs[count], refs[count + 1]
    tile = min(256, out_ref.shape[1])

    @pl.loop(0, out_ref.shape[1] // tile)
    def _(step):
        columns = pl.ds(pl.multiple_of(step * tile, tile), tile)
        total = None
        for k in range(count):
            part = dot(blocks[k][...], weight_ref[table_ref[k], :, columns], ((1,), (0,)))
            total = part if total is None else total + part
        out_ref[:, columns] = total


def product(blocks, weights, table):
    count, (rows, depth), width = len(blocks), blocks[0].shape, weights.shape[2]
    return pl.pallas_call(
        functools.partial(product_kernel, count),
        out_shape=jax.ShapeDtypeStruct((rows, width), F32),
        in_specs=[pl.BlockSpec(memory_space=pltpu.SMEM)]
        + [pl.BlockSpec(memory_space=pltpu.VMEM)] * (count + 1),
        out_specs=pl.BlockSpec(memory_space=pltpu.VMEM),
        compiler_params=pltpu.CompilerParams(vmem_limit_bytes=24 * 1024 * 1024),
        cost_estimate=pl.CostEstimate(
            flops=2 * rows * count * depth * width,
            bytes_accessed=2 * count * depth * (rows + width) + 4 * rows * width,
            transcendentals=0,
        ),
    )(table, *blocks, weights)


def attend_kernel(table_ref, q_ref, g_ref, kv_ref, live_ref, *rest):
    dq_ref, grad_ref = rest[-2:]
    count = pl.num_programs(0)
    named = table_ref[count + pl.program_id(0)]
    pairs = q_ref.shape[-1] // HD // 2
    scale = HD ** (-0.5)

    @pl.when(named == 0)
    def _():
        dq_ref[...] = jnp.zeros_like(dq_ref)
        grad_ref[...] = jnp.zeros_like(grad_ref)

    @pl.when(named != 0)
    def _():
        live = live_ref[0] > 0.5
        zero = jnp.zeros((SPAN, HD), BF16)

        def diagonal(ref, start):
            one = ref[0, :, start:start + HD]
            two = ref[0, :, start + HD:start + 2 * HD]
            return jnp.concatenate(
                [jnp.concatenate([one, zero], axis=1), jnp.concatenate([zero, two], axis=1)], axis=0
            )

        def first(pair):
            start = pair * 2 * HD
            columns = slice(start, start + 2 * HD)
            scores = dot(kv_ref[0, 0, :, columns], diagonal(q_ref, start), ((1,), (1,)))
            prob_grad = dot(kv_ref[0, 1, :, columns], diagonal(g_ref, start), ((1,), (1,)))
            return scores, prob_grad

        ahead = first(0)
        for pair in range(pairs):
            scores, prob_grad = ahead
            if pair + 1 < pairs:
                ahead = first(pair + 1)
            start = pair * 2 * HD
            columns = slice(start, start + 2 * HD)
            scores = jnp.where(live, scores * scale, -1e30)
            expo = jnp.exp(scores - jnp.max(scores, axis=0, keepdims=True))
            probs = expo * (1.0 / jnp.sum(expo, axis=0, keepdims=True))
            center = jnp.sum(probs * prob_grad, axis=0, keepdims=True)
            score_grad = (probs * (prob_grad - center) * scale).astype(BF16)
            value_grad = dot(probs.astype(BF16), diagonal(g_ref, start), ((1,), (0,)))
            key_grad = dot(score_grad, diagonal(q_ref, start), ((1,), (0,)))
            both = dot(score_grad, kv_ref[0, 0, :, columns], ((0,), (0,)))
            grad_ref[0, 1, :, columns] = value_grad.astype(BF16)
            grad_ref[0, 0, :, columns] = key_grad.astype(BF16)
            dq_ref[0, :, columns] = jnp.concatenate(
                [both[:SPAN, :HD], both[SPAN:, HD:]], axis=1
            ).astype(BF16)


def attend(slots, named, queries, grads, kv, live, before):
    count, _, width = queries.shape
    keys = kv.shape[2]
    heads = width // HD
    table = jnp.concatenate([slots, named]).astype(jnp.int32)
    span_block = pl.BlockSpec((1, SPAN, width), lambda r, t: (r, 0, 0))
    kv_block = pl.BlockSpec((1, 2, keys, width), lambda r, t: (t[r], 0, 0, 0))
    live_block = pl.BlockSpec((1, keys, HD), lambda r, t: (t[r], 0, 0))
    in_specs = [span_block, span_block, kv_block, live_block]
    operands = [table, queries, grads, kv, live]
    aliases = {}
    if before is not None:
        in_specs.append(pl.BlockSpec(memory_space=pl.ANY))
        operands.append(before)
        aliases = {len(operands) - 1: 1}
    return pl.pallas_call(
        attend_kernel,
        grid_spec=pltpu.PrefetchScalarGridSpec(
            num_scalar_prefetch=1,
            grid=(count,),
            in_specs=in_specs,
            out_specs=[span_block, kv_block],
        ),
        out_shape=[
            jax.ShapeDtypeStruct(queries.shape, BF16),
            jax.ShapeDtypeStruct(kv.shape, BF16),
        ],
        input_output_aliases=aliases,
        compiler_params=pltpu.CompilerParams(vmem_limit_bytes=40 * 1024 * 1024),
        cost_estimate=pl.CostEstimate(
            flops=count * heads * 5 * 2 * SPAN * keys * HD * 4,
            bytes_accessed=count * 4 * keys * width * 2,
            transcendentals=count * heads * SPAN * keys,
        ),
    )(*operands)


def on_device(span_act, q_weight, out_grad, neighbour_kv, neighbour_ids, owner):
    rows, width = out_grad.shape
    depth = q_weight.shape[0]
    seq_count = lax.axis_size("seq")
    dp_count = lax.axis_size("dp")
    tensor_count = lax.axis_size("tensor")
    couples = dp_count // 2
    seq_at = lax.axis_index("seq")
    dp_at = lax.axis_index("dp")
    tensor_at = lax.axis_index("tensor")
    core = dp_at % 2
    spans = rows // SPAN
    capacity = neighbour_kv.shape[0]
    pairs = capacity // seq_count
    whole_blocks = pairs == spans
    chunks = 2 if whole_blocks and spans % 2 == 0 else 1
    chunk_rows = rows // chunks
    per = span_act.shape[1] // depth // 2
    cut = depth // 2

    def chunk_of(value, chunk):
        return value[chunk * chunk_rows:(chunk + 1) * chunk_rows]

    def columns_of(which):
        return jnp.concatenate(
            [
                lax.dynamic_slice(span_act, (0, (2 * p + which) * depth), (rows, depth))
                for p in range(per)
            ],
            axis=1,
        )

    act_mine, act_other = columns_of(core), columns_of(1 - core)
    acts = []
    for chunk in range(chunks):
        both = jnp.concatenate(
            [chunk_of(act_mine, chunk), swap(chunk_of(act_other, chunk))], axis=0
        )
        acts.append(ring_gather(both, "tensor", tensor_count))
    depth_blocks = [(tensor_at - k) % tensor_count for k in range(tensor_count)]
    table = jnp.stack(depth_blocks).astype(jnp.int32)

    seq_first = [
        ring_gather(block, "dp", couples) for block in ring_gather(q_weight[:cut], "seq", seq_count)
    ]
    dp_first = [
        ring_gather(block, "seq", seq_count) for block in ring_gather(q_weight[cut:], "dp", couples)
    ]

    def block_at(i, j):
        block = ((seq_at - i) % seq_count) * dp_count + ((dp_at // 2 - j) % couples) * 2
        return block // (2 * per), (block % (2 * per)) // 2

    places = [(i, j) for i in range(seq_count) for j in range(couples)]
    weights = jnp.zeros((tensor_count, per * depth, width), BF16)
    for i, j in places:
        at, inner = block_at(i, j)
        for piece, start in ((seq_first[i][j], 0), (dp_first[j][i], cut)):
            weights = lax.dynamic_update_slice(weights, piece[None], (at, inner * depth + start, 0))

    groups = owner.reshape(seq_count, dp_count, spans)
    groups = lax.dynamic_index_in_dim(groups, dp_at, 1, keepdims=False)
    mine = lax.dynamic_index_in_dim(groups, seq_at, 0, keepdims=False)

    def order(group, target):
        names = group == target
        at = jnp.arange(spans)
        ahead = (names[None, :] & ~names[:, None]) | (
            (names[None, :] == names[:, None]) & (at[None, :] < at[:, None])
        )
        return jnp.sum(ahead.astype(jnp.int32), axis=1), names.astype(jnp.int32)

    def message(target):
        place, names = order(mine, target)
        hit = place[None, :] == jnp.arange(pairs)[:, None]
        return hit & (names[None, :] == 1)

    def to_owner(value, step):
        value = value.reshape(-1, SPAN, width)
        if not whole_blocks:
            hit = message((seq_at + step) % seq_count)
            value = jnp.sum(
                jnp.where(hit[:, :, None, None], value[None], jnp.zeros((), BF16)), axis=1
            )
        return shift(value, "seq", step) if step else value

    live = jnp.broadcast_to((neighbour_ids != 0).astype(F32)[:, :, None], (capacity, KEYS, HD))

    def slots_of(step):
        source = (seq_at - step) % seq_count
        group = lax.dynamic_index_in_dim(groups, source, 0, keepdims=False)
        place, names = order(group, seq_at)
        if not whole_blocks:
            place = jnp.arange(pairs)
            names = (place < jnp.sum(names)).astype(jnp.int32)
        return source * pairs + place, names

    sent_grads = [
        [to_owner(chunk_of(out_grad, chunk), step) for step in range(seq_count)]
        for chunk in range(chunks)
    ]

    sent_queries = []
    for chunk in range(chunks):
        partial = product(acts[chunk], weights, table)
        queries = (partial[:chunk_rows] + swap(partial[chunk_rows:])).astype(BF16)
        sent_queries.append([to_owner(queries, step) for step in range(seq_count)])

    kv_grad = None
    query_grads = [None] * chunks
    for step in range(seq_count):
        slots, names = slots_of(step)
        held = pairs // chunks
        for chunk in range(chunks):
            back, kv_grad = attend(
                slots[chunk * held:(chunk + 1) * held],
                names[chunk * held:(chunk + 1) * held],
                sent_queries[chunk][step],
                sent_grads[chunk][step],
                neighbour_kv,
                live,
                kv_grad,
            )
            if step:
                back = shift(back, "seq", -step)
            if not whole_blocks:
                hit = message((seq_at + step) % seq_count)
                back = jnp.sum(
                    jnp.where(hit[:, :, None, None], back[:, None], jnp.zeros((), BF16)), axis=0
                )
            back = back.reshape(chunk_rows, width)
            query_grads[chunk] = back if step == 0 else query_grads[chunk] + back
    both_grads = [jnp.concatenate([grad, swap(grad)], axis=0) for grad in query_grads]

    even, odd = [], []
    for chunk in range(chunks):
        parts = [None] * tensor_count
        for k in reversed(range(tensor_count)):
            block = lax.dynamic_index_in_dim(weights, depth_blocks[k], 0, keepdims=False)
            parts[k] = dot(both_grads[chunk], block, ((1,), (1,))).astype(BF16)
        total = ring_reduce(lax.optimization_barrier(parts), "tensor").astype(BF16)
        kept, arrived = total[:chunk_rows], swap(total[chunk_rows:])
        even.append(jnp.where(core == 0, kept, arrived))
        odd.append(jnp.where(core == 0, arrived, kept))
    even, odd = jnp.concatenate(even, axis=0), jnp.concatenate(odd, axis=0)
    act_grad = jnp.concatenate(
        [half[:, p * depth:(p + 1) * depth] for p in range(per) for half in (even, odd)], axis=1
    )

    act_whole = jnp.zeros((tensor_count, 2 * rows, per * depth), BF16)
    for chunk in range(chunks):
        for k in range(tensor_count):
            act_whole = lax.dynamic_update_slice(
                act_whole, acts[chunk][k][None], (depth_blocks[k], 2 * chunk * chunk_rows, 0)
            )
    grad_whole = jnp.concatenate(both_grads, axis=0)
    products = {}
    for i, j in reversed(places):
        at, inner = block_at(i, j)
        block = lax.dynamic_slice(act_whole, (at, 0, inner * depth), (1, 2 * rows, depth))[0]
        products[i, j] = dot(block, grad_whole, ((0,), (0,)))
        if (i, j) != (0, 0):
            products[i, j] = lax.optimization_barrier(products[i, j].astype(BF16))
    upper = ring_reduce(
        [
            ring_reduce([products[i, j][:cut] for j in range(couples)], "dp")
            for i in range(seq_count)
        ],
        "seq",
    )
    lower = ring_reduce(
        [
            ring_reduce([products[i, j][cut:] for i in range(seq_count)], "seq")
            for j in range(couples)
        ],
        "dp",
    )
    weight_grad = jnp.concatenate([upper, lower], axis=0)
    return (act_grad, weight_grad, kv_grad)


def solution(mesh):
    in_specs = (
        P(("seq", "dp"), "tensor"),
        P(("seq", "dp"), "tensor"),
        P(("seq", "dp"), "tensor"),
        P(("seq", "dp"), None, None, "tensor"),
        P(("seq", "dp"), None),
        P(),
    )
    out_specs = (
        P(("seq", "dp"), "tensor"),
        P(("seq", "dp"), "tensor"),
        P(("seq", "dp"), None, None, "tensor"),
    )
    return jax.shard_map(
        on_device, mesh=mesh, in_specs=in_specs, out_specs=out_specs, check_vma=False
    )
```

```python
import functools

import jax
import jax.numpy as jnp
from jax import lax
from jax.experimental import pallas as pl
from jax.experimental.pallas import tpu as pltpu
from jax.sharding import PartitionSpec as P

HD = 128
SPAN = 64
KEYS = 256
F32 = jnp.float32
BF16 = jnp.bfloat16


def dot(a, b, contract):
    return lax.dot_general(a, b, (contract, ((), ())), preferred_element_type=F32)


def shift(value, axis, step=1):
    stride = 2 if axis == "dp" else 1
    size = lax.axis_size(axis)
    return lax.ppermute(value, axis, [(i, (i + step * stride) % size) for i in range(size)])


def swap(value):
    return lax.ppermute(value, "dp", [(i, i ^ 1) for i in range(lax.axis_size("dp"))])


def shift_swap(value, step):
    tensor_count, dp_count = lax.axis_size("tensor"), lax.axis_size("dp")
    pairs = [
        (t * dp_count + d, (t + step) % tensor_count * dp_count + (d ^ 1))
        for t in range(tensor_count)
        for d in range(dp_count)
    ]
    return lax.ppermute(value, ("tensor", "dp"), pairs)


def after(value, *others):
    return lax.optimization_barrier((value, *others))[0]


def reaches(size, far_up):
    up = size // 2 if far_up else (size - 1) // 2
    return up, size - 1 - up


def gather_rings(streams, axis, size):
    held = [[block] + [None] * (size - 1) for block, _, _ in streams]
    for m in range(1, size // 2 + 1):
        came = {}
        for s, (_, far_up, hop) in enumerate(streams):
            for sign, count in zip((1, -1), reaches(size, far_up)):
                if m <= count:
                    first = hop is not None and m == 1
                    block = held[s][(sign * (m - 1)) % size]
                    came[s, (sign * m) % size] = hop(sign) if first else shift(block, axis, sign)
        for (s, k), block in zip(came, lax.optimization_barrier(tuple(came.values()))):
            held[s][k] = block
    return held


def reduce_rings(streams, axis):
    size = len(streams[0][0])
    found = [[blocks[0]] for blocks, _ in streams]
    came = {}
    for m in range(1, size // 2 + 1):
        sent = {}
        for s, (blocks, far_up) in enumerate(streams):
            for sign, count in zip((1, -1), reaches(size, far_up)):
                if m <= count:
                    block = blocks[(-sign * (count - m + 1)) % size]
                    if m > 1:
                        block = came[s, sign].astype(F32) + block.astype(F32)
                    sent[s, sign] = shift(block.astype(BF16), axis, sign)
        came = dict(zip(sent, lax.optimization_barrier(tuple(sent.values()))))
        for (s, sign), block in came.items():
            if m == reaches(size, streams[s][1])[0 if sign == 1 else 1]:
                found[s].append(block)
    return found


def total(values):
    return functools.reduce(lambda a, b: a + b, [value.astype(F32) for value in values])


def product_kernel(count, start, table_ref, *refs):
    blocks, weight_ref, out_ref = refs[:count], refs[count], refs[count + 1]
    tile = min(256, out_ref.shape[1])
    for at in range(0, out_ref.shape[1], tile):
        total = None
        for k in range(count):
            weight = weight_ref[table_ref[k], :, start + at:start + at + tile]
            part = dot(blocks[k][...], weight, ((1,), (0,)))
            total = part if total is None else total + part
        out_ref[:, at:at + tile] = total


def product(blocks, weights, table, start, width):
    count, (rows, depth) = len(blocks), blocks[0].shape
    return pl.pallas_call(
        functools.partial(product_kernel, count, start),
        out_shape=jax.ShapeDtypeStruct((rows, width), F32),
        in_specs=[pl.BlockSpec(memory_space=pltpu.SMEM)]
        + [pl.BlockSpec(memory_space=pltpu.VMEM)] * (count + 1),
        out_specs=pl.BlockSpec(memory_space=pltpu.VMEM),
        compiler_params=pltpu.CompilerParams(vmem_limit_bytes=32 * 1024 * 1024),
        cost_estimate=pl.CostEstimate(
            flops=2 * rows * count * depth * width,
            bytes_accessed=2 * count * depth * (rows + width) + 4 * rows * width,
            transcendentals=0,
        ),
    )(table, *blocks, weights)


def attend_kernel(table_ref, q_ref, g_ref, kv_ref, live_ref, *rest):
    dq_ref, grad_ref = rest[-2:]
    count = pl.num_programs(0)
    named = table_ref[count + pl.program_id(0)]
    pairs = q_ref.shape[-1] // HD // 2
    scale = HD ** (-0.5)

    @pl.when(named == 0)
    def _():
        dq_ref[...] = jnp.zeros_like(dq_ref)
        grad_ref[...] = jnp.zeros_like(grad_ref)

    @pl.when(named != 0)
    def _():
        live = live_ref[0] > 0.5
        zero = jnp.zeros((SPAN, HD), BF16)

        def diagonal(ref, start):
            one = ref[0, :, start:start + HD]
            two = ref[0, :, start + HD:start + 2 * HD]
            return jnp.concatenate(
                [jnp.concatenate([one, zero], axis=1), jnp.concatenate([zero, two], axis=1)], axis=0
            )

        def first(pair):
            start = pair * 2 * HD
            columns = slice(start, start + 2 * HD)
            scores = dot(kv_ref[0, 0, :, columns], diagonal(q_ref, start), ((1,), (1,)))
            prob_grad = dot(kv_ref[0, 1, :, columns], diagonal(g_ref, start), ((1,), (1,)))
            return scores, prob_grad

        ahead = first(0)
        for pair in range(pairs):
            scores, prob_grad = ahead
            if pair + 1 < pairs:
                ahead = first(pair + 1)
            start = pair * 2 * HD
            columns = slice(start, start + 2 * HD)
            scores = jnp.where(live, scores * scale, -1e30)
            expo = jnp.exp(scores - jnp.max(scores, axis=0, keepdims=True))
            probs = expo * (1.0 / jnp.sum(expo, axis=0, keepdims=True))
            center = jnp.sum(probs * prob_grad, axis=0, keepdims=True)
            score_grad = (probs * (prob_grad - center) * scale).astype(BF16)
            value_grad = dot(probs.astype(BF16), diagonal(g_ref, start), ((1,), (0,)))
            key_grad = dot(score_grad, diagonal(q_ref, start), ((1,), (0,)))
            both = dot(score_grad, kv_ref[0, 0, :, columns], ((0,), (0,)))
            grad_ref[0, 1, :, columns] = value_grad.astype(BF16)
            grad_ref[0, 0, :, columns] = key_grad.astype(BF16)
            dq_ref[0, :, columns] = jnp.concatenate(
                [both[:SPAN, :HD], both[SPAN:, HD:]], axis=1
            ).astype(BF16)


def attend(slots, named, queries, grads, kv, live, part, before):
    count, _, width = queries.shape
    keys = kv.shape[2]
    heads = width // HD
    table = jnp.concatenate([slots, named]).astype(jnp.int32)
    span_block = pl.BlockSpec((1, SPAN, width), lambda r, t: (r, 0, 0))
    part_block = pl.BlockSpec((1, SPAN, width), lambda r, t: (r, 0, part))
    kv_block = pl.BlockSpec((1, 2, keys, width), lambda r, t: (t[r], 0, 0, part))
    live_block = pl.BlockSpec((1, keys, HD), lambda r, t: (t[r], 0, 0))
    in_specs = [span_block, part_block, kv_block, live_block]
    operands = [table, queries, grads, kv, live]
    aliases = {}
    if before is not None:
        in_specs.append(pl.BlockSpec(memory_space=pl.ANY))
        operands.append(before)
        aliases = {len(operands) - 1: 1}
    return pl.pallas_call(
        attend_kernel,
        grid_spec=pltpu.PrefetchScalarGridSpec(
            num_scalar_prefetch=1,
            grid=(count,),
            in_specs=in_specs,
            out_specs=[span_block, kv_block],
        ),
        out_shape=[
            jax.ShapeDtypeStruct(queries.shape, BF16),
            jax.ShapeDtypeStruct(kv.shape, BF16),
        ],
        input_output_aliases=aliases,
        compiler_params=pltpu.CompilerParams(vmem_limit_bytes=40 * 1024 * 1024),
        cost_estimate=pl.CostEstimate(
            flops=count * heads * 5 * 2 * SPAN * keys * HD * 4,
            bytes_accessed=count * 4 * keys * width * 2,
            transcendentals=count * heads * SPAN * keys,
        ),
    )(*operands)


def on_device(span_act, q_weight, out_grad, neighbour_kv, neighbour_ids, owner):
    rows, width = out_grad.shape
    depth = q_weight.shape[0]
    seq_count = lax.axis_size("seq")
    dp_count = lax.axis_size("dp")
    tensor_count = lax.axis_size("tensor")
    couples = dp_count // 2
    seq_at = lax.axis_index("seq")
    dp_at = lax.axis_index("dp")
    tensor_at = lax.axis_index("tensor")
    core = dp_at % 2
    spans = rows // SPAN
    capacity = neighbour_kv.shape[0]
    pairs = capacity // seq_count
    whole_blocks = pairs == spans
    per = span_act.shape[1] // depth // 2
    half = width // 2

    along_seq = gather_rings([(q_weight, True, None)], "seq", seq_count)[0]
    along_dp = gather_rings([(q_weight, True, None)], "dp", couples)[0]
    along_seq, along_dp = lax.optimization_barrier((along_seq, along_dp))

    def columns_of(which):
        return jnp.concatenate(
            [
                lax.dynamic_slice(span_act, (0, (2 * p + which) * depth), (rows, depth))
                for p in range(per)
            ],
            axis=1,
        )

    act_mine, act_other = columns_of(core), columns_of(1 - core)
    own_other = swap(act_other)
    acts_mine, acts_other = gather_rings(
        [(act_mine, True, None), (own_other, False, functools.partial(shift_swap, act_other))],
        "tensor",
        tensor_count,
    )
    acts = [jnp.concatenate(both, axis=0) for both in zip(acts_mine, acts_other)]
    depth_blocks = [(tensor_at - k) % tensor_count for k in range(tensor_count)]
    table = jnp.stack(depth_blocks).astype(jnp.int32)

    cut = width * 5 // 8 // HD * HD
    corner_left = gather_rings(
        [(block[:, :cut], True, None) for block in along_seq[1:]], "dp", couples
    )
    corner_right = gather_rings(
        [(block[:, cut:], True, None) for block in along_dp[1:]], "seq", seq_count
    )

    def block_at(i, j):
        block = ((seq_at - i) % seq_count) * dp_count + ((dp_at // 2 - j) % couples) * 2
        return block // (2 * per), (block % (2 * per)) // 2

    places = [(i, j) for i in range(seq_count) for j in range(couples)]
    zero = after(jnp.zeros((), BF16), own_other)
    weights = jnp.broadcast_to(zero, (tensor_count, per * depth, width))
    for i, j in places:
        at, inner = block_at(i, j)
        if j == 0:
            pieces = [(along_seq[i], 0)]
        elif i == 0:
            pieces = [(along_dp[j], 0)]
        else:
            pieces = [(corner_left[i - 1][j], 0), (corner_right[j - 1][i], cut)]
        for piece, start in pieces:
            weights = lax.dynamic_update_slice(weights, piece[None], (at, inner * depth, start))

    groups = owner.reshape(seq_count, dp_count, spans)
    groups = lax.dynamic_index_in_dim(groups, dp_at, 1, keepdims=False)
    mine = lax.dynamic_index_in_dim(groups, seq_at, 0, keepdims=False)

    def order(group, target):
        names = group == target
        at = jnp.arange(spans)
        ahead = (names[None, :] & ~names[:, None]) | (
            (names[None, :] == names[:, None]) & (at[None, :] < at[:, None])
        )
        return jnp.sum(ahead.astype(jnp.int32), axis=1), names.astype(jnp.int32)

    def message(target):
        place, names = order(mine, target)
        hit = place[None, :] == jnp.arange(pairs)[:, None]
        return hit & (names[None, :] == 1)

    def to_owner(value, step):
        value = value.reshape(spans, SPAN, -1)
        if not whole_blocks:
            hit = message((seq_at + step) % seq_count)
            value = jnp.sum(
                jnp.where(hit[:, :, None, None], value[None], jnp.zeros((), BF16)), axis=1
            )
        return shift(value, "seq", step) if step else value

    def from_owner(value, step):
        value = shift(value, "seq", -step) if step else value
        if not whole_blocks:
            hit = message((seq_at + step) % seq_count)
            value = jnp.sum(
                jnp.where(hit[:, :, None, None], value[:, None], jnp.zeros((), BF16)), axis=0
            )
        return value.reshape(rows, -1)

    def slots_of(step):
        source = (seq_at - step) % seq_count
        group = lax.dynamic_index_in_dim(groups, source, 0, keepdims=False)
        place, names = order(group, seq_at)
        if not whole_blocks:
            place = jnp.arange(pairs)
            names = (place < jnp.sum(names)).astype(jnp.int32)
        return source * pairs + place, names

    live = jnp.broadcast_to((neighbour_ids != 0).astype(F32)[:, :, None], (capacity, KEYS, HD))
    slots = [slots_of(step) for step in range(seq_count)]
    grads = [to_owner(out_grad, step) for step in range(seq_count)]

    table = after(table, *grads)
    queries = []
    for part in range(2):
        partial = product(acts, weights, table, part * half, half)
        queries.append((partial[:rows] + swap(partial[rows:])).astype(BF16))
    asked = [[to_owner(value, step) for step in range(seq_count)] for value in queries]

    kv_grad = None
    both_grads, products = [], []
    for part in range(2):
        answers = []
        for step in range(seq_count):
            answer, kv_grad = attend(
                *slots[step], asked[part][step], grads[step], neighbour_kv, live, part, kv_grad
            )
            answers.append(from_owner(answer, step))
        if part:
            answers[-1] = after(answers[-1], products[0][places[-1]])
        grad = sum(answers[1:], answers[0])
        both_grads.append(jnp.concatenate([grad, swap(grad)], axis=0))
        if part == 0:
            act_whole = jnp.broadcast_to(zero, (tensor_count, 2 * rows, per * depth))
            for k in range(tensor_count):
                act_whole = lax.dynamic_update_slice(
                    act_whole, acts[k][None], (depth_blocks[k], 0, 0)
                )

        found = {}
        for i, j in reversed(places):
            at, inner = block_at(i, j)
            block = lax.dynamic_slice(act_whole, (at, 0, inner * depth), (1, 2 * rows, depth))[0]
            found[i, j] = dot(block, both_grads[part], ((0,), (0,)))
            if (i, j) != (0, 0):
                found[i, j] = lax.optimization_barrier(found[i, j].astype(BF16))
        products.append(found)

    both_grad = jnp.concatenate(both_grads, axis=1)
    parts = [None] * tensor_count
    for k in sorted(range(tensor_count), key=lambda k: -min(k, tensor_count - k)):
        block = lax.dynamic_index_in_dim(weights, depth_blocks[k], 0, keepdims=False)
        part = dot(both_grad, block, ((1,), (1,))).astype(BF16)
        parts[k] = lax.optimization_barrier(part)
    mine_parts, other_parts = reduce_rings(
        [([part[:rows] for part in parts], True), ([part[rows:] for part in parts], False)],
        "tensor",
    )
    arrived = swap(total(other_parts).astype(BF16))
    kept = total(mine_parts).astype(BF16)
    even = jnp.where(core == 0, kept, arrived)
    odd = jnp.where(core == 0, arrived, kept)
    act_grad = jnp.concatenate(
        [value[:, p * depth:(p + 1) * depth] for p in range(per) for value in (even, odd)], axis=1
    )

    left = reduce_rings(
        [([products[0][i, j] for j in range(couples)], True) for i in range(seq_count)], "dp"
    )
    right = reduce_rings(
        [([products[1][i, j] for i in range(seq_count)], True) for j in range(couples)], "seq"
    )
    left, right = lax.optimization_barrier((left, right))
    left = reduce_rings([([total(values) for values in left], True)], "seq")[0]
    right = reduce_rings([([total(values) for values in right], True)], "dp")[0]
    left, right = total(left), total(right)
    weight_grad = jnp.concatenate([left, right], axis=1)
    return (act_grad, weight_grad, kv_grad)


def solution(mesh):
    in_specs = (
        P(("seq", "dp"), "tensor"),
        P(("seq", "dp"), "tensor"),
        P(("seq", "dp"), "tensor"),
        P(("seq", "dp"), None, None, "tensor"),
        P(("seq", "dp"), None),
        P(),
    )
    out_specs = (
        P(("seq", "dp"), "tensor"),
        P(("seq", "dp"), "tensor"),
        P(("seq", "dp"), None, None, "tensor"),
    )
    return jax.shard_map(
        on_device, mesh=mesh, in_specs=in_specs, out_specs=out_specs, check_vma=False
    )
```

```python
import functools

import jax
import jax.numpy as jnp
from jax import lax
from jax.experimental import pallas as pl
from jax.experimental.pallas import tpu as pltpu
from jax.sharding import PartitionSpec as P

HD = 128
SPAN = 64
KEYS = 256
F32 = jnp.float32
BF16 = jnp.bfloat16


def dot(a, b, contract):
    return lax.dot_general(a, b, (contract, ((), ())), preferred_element_type=F32)


def shift(value, axis, step=1):
    stride = 2 if axis == "dp" else 1
    size = lax.axis_size(axis)
    return lax.ppermute(value, axis, [(i, (i + step * stride) % size) for i in range(size)])


def swap(value):
    return lax.ppermute(value, "dp", [(i, i ^ 1) for i in range(lax.axis_size("dp"))])


def after(value, *others):
    return lax.optimization_barrier((value, *others))[0]


def reaches(size, far_up):
    up = size // 2 if far_up else (size - 1) // 2
    return up, size - 1 - up


def gather_ring(block, axis, size, rounds=None):
    blocks = [block] + [None] * (size - 1)
    for m in range(1, (size // 2 if rounds is None else rounds) + 1):
        came = {}
        for sign, count in zip((1, -1), reaches(size, True)):
            if m <= count:
                came[(sign * m) % size] = shift(blocks[(sign * (m - 1)) % size], axis, sign)
        for k, value in zip(came, lax.optimization_barrier(tuple(came.values()))):
            blocks[k] = value
    return blocks


def reduce_rings(streams, axis):
    size = len(streams[0][0])
    found = [[blocks[0]] for blocks, _ in streams]
    came = {}
    for m in range(1, size // 2 + 1):
        sent = {}
        for s, (blocks, far_up) in enumerate(streams):
            for sign, count in zip((1, -1), reaches(size, far_up)):
                if m <= count:
                    block = blocks[(-sign * (count - m + 1)) % size]
                    if m > 1:
                        block = came[s, sign].astype(F32) + block.astype(F32)
                    sent[s, sign] = shift(block.astype(BF16), axis, sign)
        came = dict(zip(sent, lax.optimization_barrier(tuple(sent.values()))))
        for (s, sign), block in came.items():
            if m == reaches(size, streams[s][1])[0 if sign == 1 else 1]:
                found[s].append(block)
    return found


def total(values):
    return functools.reduce(lambda a, b: a + b, [value.astype(F32) for value in values])


def product_kernel(count, start, table_ref, *refs):
    blocks, weight_ref, out_ref = refs[:count], refs[count], refs[count + 1]
    tile = min(256, out_ref.shape[1])
    for at in range(0, out_ref.shape[1], tile):
        total = None
        for k in range(count):
            weight = weight_ref[table_ref[k], :, start + at:start + at + tile]
            part = dot(blocks[k][...], weight, ((1,), (0,)))
            total = part if total is None else total + part
        out_ref[:, at:at + tile] = total


def product(blocks, weights, table, start, width):
    count, (rows, depth) = len(blocks), blocks[0].shape
    return pl.pallas_call(
        functools.partial(product_kernel, count, start),
        out_shape=jax.ShapeDtypeStruct((rows, width), F32),
        in_specs=[pl.BlockSpec(memory_space=pltpu.SMEM)]
        + [pl.BlockSpec(memory_space=pltpu.VMEM)] * (count + 1),
        out_specs=pl.BlockSpec(memory_space=pltpu.VMEM),
        compiler_params=pltpu.CompilerParams(vmem_limit_bytes=32 * 1024 * 1024),
        cost_estimate=pl.CostEstimate(
            flops=2 * rows * count * depth * width,
            bytes_accessed=2 * count * depth * (rows + width) + 4 * rows * width,
            transcendentals=0,
        ),
    )(table, *blocks, weights)


def attend_kernel(table_ref, q_ref, g_ref, kv_ref, live_ref, *rest):
    dq_ref, grad_ref = rest[-2:]
    count = pl.num_programs(0)
    named = table_ref[count + pl.program_id(0)]
    pairs = q_ref.shape[-1] // HD // 2
    scale = HD ** (-0.5)

    @pl.when(named == 0)
    def _():
        dq_ref[...] = jnp.zeros_like(dq_ref)
        grad_ref[...] = jnp.zeros_like(grad_ref)

    @pl.when(named != 0)
    def _():
        live = live_ref[0] > 0.5
        zero = jnp.zeros((SPAN, HD), BF16)

        def diagonal(ref, start):
            one = ref[0, :, start:start + HD]
            two = ref[0, :, start + HD:start + 2 * HD]
            return jnp.concatenate(
                [jnp.concatenate([one, zero], axis=1), jnp.concatenate([zero, two], axis=1)], axis=0
            )

        def first(pair):
            start = pair * 2 * HD
            columns = slice(start, start + 2 * HD)
            scores = dot(kv_ref[0, 0, :, columns], diagonal(q_ref, start), ((1,), (1,)))
            prob_grad = dot(kv_ref[0, 1, :, columns], diagonal(g_ref, start), ((1,), (1,)))
            return scores, prob_grad

        ahead = first(0)
        for pair in range(pairs):
            scores, prob_grad = ahead
            if pair + 1 < pairs:
                ahead = first(pair + 1)
            start = pair * 2 * HD
            columns = slice(start, start + 2 * HD)
            scores = jnp.where(live, scores * scale, -1e30)
            expo = jnp.exp(scores - jnp.max(scores, axis=0, keepdims=True))
            probs = expo * (1.0 / jnp.sum(expo, axis=0, keepdims=True))
            center = jnp.sum(probs * prob_grad, axis=0, keepdims=True)
            score_grad = (probs * (prob_grad - center) * scale).astype(BF16)
            value_grad = dot(probs.astype(BF16), diagonal(g_ref, start), ((1,), (0,)))
            key_grad = dot(score_grad, diagonal(q_ref, start), ((1,), (0,)))
            both = dot(score_grad, kv_ref[0, 0, :, columns], ((0,), (0,)))
            grad_ref[0, 1, :, columns] = value_grad.astype(BF16)
            grad_ref[0, 0, :, columns] = key_grad.astype(BF16)
            dq_ref[0, :, columns] = jnp.concatenate(
                [both[:SPAN, :HD], both[SPAN:, HD:]], axis=1
            ).astype(BF16)


def attend(slots, named, queries, grads, kv, live, part, before):
    count, _, width = queries.shape
    keys = kv.shape[2]
    heads = width // HD
    table = jnp.concatenate([slots, named]).astype(jnp.int32)
    span_block = pl.BlockSpec((1, SPAN, width), lambda r, t: (r, 0, 0))
    part_block = pl.BlockSpec((1, SPAN, width), lambda r, t: (r, 0, part))
    kv_block = pl.BlockSpec((1, 2, keys, width), lambda r, t: (t[r], 0, 0, part))
    live_block = pl.BlockSpec((1, keys, HD), lambda r, t: (t[r], 0, 0))
    in_specs = [span_block, part_block, kv_block, live_block]
    operands = [table, queries, grads, kv, live]
    aliases = {}
    if before is not None:
        in_specs.append(pl.BlockSpec(memory_space=pl.ANY))
        operands.append(before)
        aliases = {len(operands) - 1: 1}
    return pl.pallas_call(
        attend_kernel,
        grid_spec=pltpu.PrefetchScalarGridSpec(
            num_scalar_prefetch=1,
            grid=(count,),
            in_specs=in_specs,
            out_specs=[span_block, kv_block],
        ),
        out_shape=[
            jax.ShapeDtypeStruct(queries.shape, BF16),
            jax.ShapeDtypeStruct(kv.shape, BF16),
        ],
        input_output_aliases=aliases,
        compiler_params=pltpu.CompilerParams(vmem_limit_bytes=40 * 1024 * 1024),
        cost_estimate=pl.CostEstimate(
            flops=count * heads * 5 * 2 * SPAN * keys * HD * 4,
            bytes_accessed=count * 4 * keys * width * 2,
            transcendentals=count * heads * SPAN * keys,
        ),
    )(*operands)


def on_device(span_act, q_weight, out_grad, neighbour_kv, neighbour_ids, owner):
    rows, width = out_grad.shape
    depth = q_weight.shape[0]
    seq_count = lax.axis_size("seq")
    dp_count = lax.axis_size("dp")
    tensor_count = lax.axis_size("tensor")
    couples = dp_count // 2
    seq_at = lax.axis_index("seq")
    dp_at = lax.axis_index("dp")
    tensor_at = lax.axis_index("tensor")
    core = dp_at % 2
    spans = rows // SPAN
    capacity = neighbour_kv.shape[0]
    pairs = capacity // seq_count
    whole_blocks = pairs == spans
    per = span_act.shape[1] // depth // 2
    half = width // 2
    opposite = tensor_count // 2

    def columns_of(which):
        return jnp.concatenate(
            [
                lax.dynamic_slice(span_act, (0, (2 * p + which) * depth), (rows, depth))
                for p in range(per)
            ],
            axis=1,
        )

    act_both = jnp.concatenate([columns_of(core), swap(columns_of(1 - core))], axis=0)

    acts = gather_ring(act_both, "tensor", tensor_count, opposite - 1)
    near = [act for act in acts if act is not None]
    along_seq = gather_ring(q_weight, "seq", seq_count)
    along_dp = gather_ring(q_weight, "dp", couples)
    near, along_seq, along_dp, grad_out = lax.optimization_barrier(
        (near, along_seq, along_dp, out_grad)
    )

    acts = near[:opposite] + [None] + near[opposite:]
    acts[opposite] = jnp.concatenate(
        [
            shift(acts[opposite - 1][:rows], "tensor", 1),
            shift(acts[opposite + 1][rows:], "tensor", -1),
        ],
        axis=0,
    )
    depth_blocks = [(tensor_at - k) % tensor_count for k in range(tensor_count)]
    table = jnp.stack(depth_blocks).astype(jnp.int32)

    cut = width * 5 // 8 // HD * HD
    corner_left = [gather_ring(block[:, :cut], "dp", couples) for block in along_seq[1:]]
    corner_right = [gather_ring(block[:, cut:], "seq", seq_count) for block in along_dp[1:]]

    def block_at(i, j):
        block = ((seq_at - i) % seq_count) * dp_count + ((dp_at // 2 - j) % couples) * 2
        return block // (2 * per), (block % (2 * per)) // 2

    places = [(i, j) for i in range(seq_count) for j in range(couples)]
    weights = jnp.zeros((tensor_count, per * depth, width), BF16)
    for i, j in places:
        at, inner = block_at(i, j)
        if j == 0:
            pieces = [(along_seq[i], 0)]
        elif i == 0:
            pieces = [(along_dp[j], 0)]
        else:
            pieces = [(corner_left[i - 1][j], 0), (corner_right[j - 1][i], cut)]
        for piece, start in pieces:
            weights = lax.dynamic_update_slice(weights, piece[None], (at, inner * depth, start))

    groups = owner.reshape(seq_count, dp_count, spans)
    groups = lax.dynamic_index_in_dim(groups, dp_at, 1, keepdims=False)
    mine = lax.dynamic_index_in_dim(groups, seq_at, 0, keepdims=False)

    def order(group, target):
        names = group == target
        at = jnp.arange(spans)
        ahead = (names[None, :] & ~names[:, None]) | (
            (names[None, :] == names[:, None]) & (at[None, :] < at[:, None])
        )
        return jnp.sum(ahead.astype(jnp.int32), axis=1), names.astype(jnp.int32)

    def message(target):
        place, names = order(mine, target)
        hit = place[None, :] == jnp.arange(pairs)[:, None]
        return hit & (names[None, :] == 1)

    def to_owner(value, step):
        value = value.reshape(spans, SPAN, -1)
        if not whole_blocks:
            hit = message((seq_at + step) % seq_count)
            value = jnp.sum(
                jnp.where(hit[:, :, None, None], value[None], jnp.zeros((), BF16)), axis=1
            )
        return shift(value, "seq", step) if step else value

    def from_owner(value, step):
        value = shift(value, "seq", -step) if step else value
        if not whole_blocks:
            hit = message((seq_at + step) % seq_count)
            value = jnp.sum(
                jnp.where(hit[:, :, None, None], value[:, None], jnp.zeros((), BF16)), axis=0
            )
        return value.reshape(rows, -1)

    def slots_of(step):
        source = (seq_at - step) % seq_count
        group = lax.dynamic_index_in_dim(groups, source, 0, keepdims=False)
        place, names = order(group, seq_at)
        if not whole_blocks:
            place = jnp.arange(pairs)
            names = (place < jnp.sum(names)).astype(jnp.int32)
        return source * pairs + place, names

    live = jnp.broadcast_to((neighbour_ids != 0).astype(F32)[:, :, None], (capacity, KEYS, HD))
    slots = [slots_of(step) for step in range(seq_count)]
    grads = [to_owner(grad_out, step) for step in range(seq_count)]

    table = after(table, *grads)
    queries = []
    for part in range(2):
        partial = product(acts, weights, table, part * half, half)
        queries.append((partial[:rows] + swap(partial[rows:])).astype(BF16))
    asked = [[to_owner(value, step) for step in range(seq_count)] for value in queries]

    stacked = jnp.stack(after(acts, queries[1]))

    def act_block(i, j):
        at, inner = block_at(i, j)
        k = (tensor_at - at) % tensor_count
        return lax.dynamic_slice(stacked, (k, 0, inner * depth), (1, 2 * rows, depth))[0]

    def weight_product(i, j, grad):
        found = dot(act_block(i, j), grad, ((0,), (0,)))
        return lax.optimization_barrier(found.astype(BF16))

    kv_grad = None
    both_grads, corners = [], []
    corner_places = [(i, j) for i in range(1, seq_count) for j in range(1, couples)]
    for part in range(2):
        answers = []
        for step in range(seq_count):
            answer, kv_grad = attend(
                *slots[step], asked[part][step], grads[step], neighbour_kv, live, part, kv_grad
            )
            answers.append(from_owner(answer, step))
        if part:
            answers[-1] = after(answers[-1], corners[0][corner_places[-1]])
        grad = sum(answers[1:], answers[0])
        both_grads.append(jnp.concatenate([grad, swap(grad)], axis=0))
        corners.append({at: weight_product(*at, both_grads[part]) for at in corner_places[::-1]})
    both_grad = jnp.concatenate(both_grads, axis=1)

    both_grad = after(both_grad, corners[1][corner_places[-1]])

    def act_product(k):
        block = lax.dynamic_index_in_dim(weights, depth_blocks[k], 0, keepdims=False)
        return lax.optimization_barrier(dot(both_grad, block, ((1,), (1,))).astype(BF16))

    far = act_product(opposite)
    up, down = shift(far[:rows], "tensor", 1), shift(far[rows:], "tensor", -1)

    left = [
        reduce_rings([([None] + [corners[0][i, j] for j in range(1, couples)], True)], "dp")[0][1:]
        for i in range(1, seq_count)
    ]
    right = [
        reduce_rings([([None] + [corners[1][i, j] for i in range(1, seq_count)], True)], "seq")[0][1:]
        for j in range(1, couples)
    ]
    act_parts = {k: act_product(k) for k in range(tensor_count) if k != opposite}
    beside_seq = [weight_product(i, 0, both_grad) for i in range(1, seq_count)]
    beside_dp = [weight_product(0, j, both_grad) for j in range(1, couples)]
    up, down, left, right, act_parts, beside_seq, beside_dp = lax.optimization_barrier(
        (up, down, left, right, act_parts, beside_seq, beside_dp)
    )

    for m in range(opposite - 1, 0, -1):
        block = act_parts[tensor_count - m]
        if up.shape[0] == rows:
            up = jnp.concatenate([total([block[:rows], up]).astype(BF16), block[rows:]], axis=0)
        else:
            up = total([block, up]).astype(BF16)
        block = act_parts[m]
        if down.shape[0] == rows:
            down = jnp.concatenate([block[:rows], total([block[rows:], down]).astype(BF16)], axis=0)
        else:
            down = total([block, down]).astype(BF16)
        up, down = shift(up, "tensor", 1), shift(down, "tensor", -1)
    beside_seq = [
        jnp.concatenate([total([block[:, :half]] + came).astype(BF16), block[:, half:]], axis=1)
        for block, came in zip(beside_seq, left)
    ]
    beside_dp = [
        jnp.concatenate([block[:, :half], total([block[:, half:]] + came).astype(BF16)], axis=1)
        for block, came in zip(beside_dp, right)
    ]
    from_seq = reduce_rings([([None] + beside_seq, True)], "seq")[0][1:]
    from_dp = reduce_rings([([None] + beside_dp, True)], "dp")[0][1:]

    act_sum = total([act_parts[0], up, down])
    kept, arrived = act_sum[:rows].astype(BF16), swap(act_sum[rows:].astype(BF16))
    even = jnp.where(core == 0, kept, arrived)
    odd = jnp.where(core == 0, arrived, kept)
    act_grad = jnp.concatenate(
        [value[:, p * depth:(p + 1) * depth] for p in range(per) for value in (even, odd)], axis=1
    )
    weight_grad = total([weight_product(0, 0, both_grad)] + from_seq + from_dp)
    return (act_grad, weight_grad, kv_grad)


def solution(mesh):
    in_specs = (
        P(("seq", "dp"), "tensor"),
        P(("seq", "dp"), "tensor"),
        P(("seq", "dp"), "tensor"),
        P(("seq", "dp"), None, None, "tensor"),
        P(("seq", "dp"), None),
        P(),
    )
    out_specs = (
        P(("seq", "dp"), "tensor"),
        P(("seq", "dp"), "tensor"),
        P(("seq", "dp"), None, None, "tensor"),
    )
    return jax.shard_map(
        on_device, mesh=mesh, in_specs=in_specs, out_specs=out_specs, check_vma=False
    )
```

```python
import functools

import jax
import jax.numpy as jnp
from jax import lax
from jax.experimental import pallas as pl
from jax.experimental.pallas import tpu as pltpu
from jax.sharding import PartitionSpec as P

HD = 128
SPAN = 64
KEYS = 256
F32 = jnp.float32
BF16 = jnp.bfloat16


def dot(a, b, contract):
    return lax.dot_general(a, b, (contract, ((), ())), preferred_element_type=F32)


def shift(value, axis, step=1):
    stride = 2 if axis == "dp" else 1
    size = lax.axis_size(axis)
    return lax.ppermute(value, axis, [(i, (i + step * stride) % size) for i in range(size)])


def swap(value):
    return lax.ppermute(value, "dp", [(i, i ^ 1) for i in range(lax.axis_size("dp"))])


def after(value, *others):
    return lax.optimization_barrier((value, *others))[0]


def reaches(size, far_up):
    up = size // 2 if far_up else (size - 1) // 2
    return up, size - 1 - up


def gather_ring(block, axis, size, rounds=None):
    blocks = [block] + [None] * (size - 1)
    for m in range(1, (size // 2 if rounds is None else rounds) + 1):
        came = {}
        for sign, count in zip((1, -1), reaches(size, True)):
            if m <= count:
                came[(sign * m) % size] = shift(blocks[(sign * (m - 1)) % size], axis, sign)
        for k, value in zip(came, lax.optimization_barrier(tuple(came.values()))):
            blocks[k] = value
    return blocks


def reduce_rings(streams, axis):
    size = len(streams[0][0])
    found = [[blocks[0]] for blocks, _ in streams]
    came = {}
    for m in range(1, size // 2 + 1):
        sent = {}
        for s, (blocks, far_up) in enumerate(streams):
            for sign, count in zip((1, -1), reaches(size, far_up)):
                if m <= count:
                    block = blocks[(-sign * (count - m + 1)) % size]
                    if m > 1:
                        block = came[s, sign].astype(F32) + block.astype(F32)
                    sent[s, sign] = shift(block.astype(BF16), axis, sign)
        came = dict(zip(sent, lax.optimization_barrier(tuple(sent.values()))))
        for (s, sign), block in came.items():
            if m == reaches(size, streams[s][1])[0 if sign == 1 else 1]:
                found[s].append(block)
    return found


def total(values):
    return functools.reduce(lambda a, b: a + b, [value.astype(F32) for value in values])


def product_kernel(count, start, table_ref, *refs):
    blocks, weight_ref, out_ref = refs[:count], refs[count], refs[count + 1]
    tile = min(256, out_ref.shape[1])
    for at in range(0, out_ref.shape[1], tile):
        total = None
        for k in range(count):
            weight = weight_ref[table_ref[k], :, start + at:start + at + tile]
            part = dot(blocks[k][...], weight, ((1,), (0,)))
            total = part if total is None else total + part
        out_ref[:, at:at + tile] = total


def product(blocks, weights, table, start, width):
    count, (rows, depth) = len(blocks), blocks[0].shape
    return pl.pallas_call(
        functools.partial(product_kernel, count, start),
        out_shape=jax.ShapeDtypeStruct((rows, width), F32),
        in_specs=[pl.BlockSpec(memory_space=pltpu.SMEM)]
        + [pl.BlockSpec(memory_space=pltpu.VMEM)] * (count + 1),
        out_specs=pl.BlockSpec(memory_space=pltpu.VMEM),
        compiler_params=pltpu.CompilerParams(vmem_limit_bytes=16 * 1024 * 1024),
        cost_estimate=pl.CostEstimate(
            flops=2 * rows * count * depth * width,
            bytes_accessed=2 * count * depth * (rows + width) + 4 * rows * width,
            transcendentals=0,
        ),
    )(table, *blocks, weights)


def attend_block(q_ref, g_ref, kv_ref, live_ref, dq_ref, grad_ref):
    pairs = q_ref.shape[-1] // HD // 2
    scale = HD ** (-0.5)
    live = live_ref[...] > 0.5
    zero = jnp.zeros((SPAN, HD), BF16)

    def diagonal(ref, start):
        one = ref[:, start:start + HD]
        two = ref[:, start + HD:start + 2 * HD]
        return jnp.concatenate(
            [jnp.concatenate([one, zero], axis=1), jnp.concatenate([zero, two], axis=1)], axis=0
        )

    def first(pair):
        start = pair * 2 * HD
        columns = slice(start, start + 2 * HD)
        scores = dot(kv_ref[0, :, columns], diagonal(q_ref, start), ((1,), (1,)))
        prob_grad = dot(kv_ref[1, :, columns], diagonal(g_ref, start), ((1,), (1,)))
        return scores, prob_grad

    ahead = first(0)
    for pair in range(pairs):
        scores, prob_grad = ahead
        if pair + 1 < pairs:
            ahead = first(pair + 1)
        start = pair * 2 * HD
        columns = slice(start, start + 2 * HD)
        scores = jnp.where(live, scores * scale, -1e30)
        expo = jnp.exp(scores - jnp.max(scores, axis=0, keepdims=True))
        probs = expo * (1.0 / jnp.sum(expo, axis=0, keepdims=True))
        center = jnp.sum(probs * prob_grad, axis=0, keepdims=True)
        score_grad = (probs * (prob_grad - center) * scale).astype(BF16)
        value_grad = dot(probs.astype(BF16), diagonal(g_ref, start), ((1,), (0,)))
        key_grad = dot(score_grad, diagonal(q_ref, start), ((1,), (0,)))
        both = dot(score_grad, kv_ref[0, :, columns], ((0,), (0,)))
        grad_ref[1, :, columns] = value_grad.astype(BF16)
        grad_ref[0, :, columns] = key_grad.astype(BF16)
        dq_ref[:, columns] = jnp.concatenate([both[:SPAN, :HD], both[SPAN:, HD:]], axis=1).astype(
            BF16
        )


def attend_kernel(part, table_ref, q_ref, g_ref, live_ref, kv_ref, *rest):
    dq_ref, grad_ref, kv_buf, grad_buf, in_sem, out_sem = rest[-6:]
    count, _, width = q_ref.shape
    columns = pl.ds(part * width, width)

    def copy_in(r):
        source = kv_ref.at[table_ref[r], :, :, columns]
        return pltpu.make_async_copy(source, kv_buf.at[r % 2], in_sem.at[r % 2])

    def copy_out(r):
        target = grad_ref.at[table_ref[r], :, :, columns]
        return pltpu.make_async_copy(grad_buf.at[r % 2], target, out_sem.at[r % 2])

    copy_in(0).start()

    @pl.loop(0, count)
    def _(r):
        @pl.when(r + 1 < count)
        def _():
            copy_in(r + 1).start()

        copy_in(r).wait()

        @pl.when(r >= 2)
        def _():
            copy_out(r - 2).wait()

        slot = r % 2

        @pl.when(table_ref[count + r] == 0)
        def _():
            dq_ref[r] = jnp.zeros(dq_ref.shape[1:], BF16)
            grad_buf[slot] = jnp.zeros(grad_buf.shape[1:], BF16)

        @pl.when(table_ref[count + r] != 0)
        def _():
            attend_block(
                q_ref.at[r],
                g_ref.at[r, :, columns],
                kv_buf.at[slot],
                live_ref.at[table_ref[r]],
                dq_ref.at[r],
                grad_buf.at[slot],
            )

        copy_out(r).start()

    for r in range(max(0, count - 2), count):
        copy_out(r).wait()


def attend(slots, named, queries, grads, kv, live, part, before):
    count, _, width = queries.shape
    keys = kv.shape[2]
    heads = width // HD
    table = jnp.concatenate([slots, named]).astype(jnp.int32)
    inside = pl.BlockSpec(memory_space=pltpu.VMEM)
    outside = pl.BlockSpec(memory_space=pltpu.HBM)
    in_specs = [pl.BlockSpec(memory_space=pltpu.SMEM), inside, inside, inside, outside]
    operands = [table, queries, grads, live, kv]
    aliases = {}
    if before is not None:
        in_specs.append(outside)
        operands.append(before)
        aliases = {len(operands) - 1: 1}
    return pl.pallas_call(
        functools.partial(attend_kernel, part),
        in_specs=in_specs,
        out_specs=[inside, outside],
        out_shape=[
            jax.ShapeDtypeStruct(queries.shape, BF16),
            jax.ShapeDtypeStruct(kv.shape, BF16),
        ],
        scratch_shapes=[
            pltpu.VMEM((2, 2, keys, width), BF16),
            pltpu.VMEM((2, 2, keys, width), BF16),
            pltpu.SemaphoreType.DMA((2,)),
            pltpu.SemaphoreType.DMA((2,)),
        ],
        input_output_aliases=aliases,
        compiler_params=pltpu.CompilerParams(vmem_limit_bytes=16 * 1024 * 1024),
        cost_estimate=pl.CostEstimate(
            flops=count * heads * 5 * 2 * SPAN * keys * HD * 4,
            bytes_accessed=count * 4 * keys * width * 2,
            transcendentals=count * heads * SPAN * keys,
        ),
    )(*operands)


def assemble_kernel(depth, core_ref, own_ref, up_ref, down_ref, arrived_ref, out_ref):
    kept = own_ref[...].astype(F32) + up_ref[...].astype(F32) + down_ref[...].astype(F32)
    kept = kept.astype(BF16)
    for p in range(kept.shape[1] // depth):
        columns = slice(p * depth, (p + 1) * depth)
        mine, other = 2 * p + core_ref[0], 2 * p + 1 - core_ref[0]
        out_ref[:, pl.ds(pl.multiple_of(mine * depth, depth), depth)] = kept[:, columns]
        out_ref[:, pl.ds(pl.multiple_of(other * depth, depth), depth)] = arrived_ref[:, columns]


def assemble(core, own, up, down, arrived, depth):
    rows, columns = arrived.shape
    tile = min(64, rows)
    block = pl.BlockSpec((tile, columns), lambda r: (r, 0))
    return pl.pallas_call(
        functools.partial(assemble_kernel, depth),
        grid=(rows // tile,),
        in_specs=[pl.BlockSpec(memory_space=pltpu.SMEM)] + [block] * 4,
        out_specs=pl.BlockSpec((tile, 2 * columns), lambda r: (r, 0)),
        out_shape=jax.ShapeDtypeStruct((rows, 2 * columns), BF16),
        compiler_params=pltpu.CompilerParams(vmem_limit_bytes=16 * 1024 * 1024),
        cost_estimate=pl.CostEstimate(
            flops=2 * rows * columns, bytes_accessed=12 * rows * columns, transcendentals=0
        ),
    )(jnp.reshape(core, (1,)).astype(jnp.int32), own, up, down, arrived)


def on_device(span_act, q_weight, out_grad, neighbour_kv, neighbour_ids, owner):
    rows, width = out_grad.shape
    depth = q_weight.shape[0]
    seq_count = lax.axis_size("seq")
    dp_count = lax.axis_size("dp")
    tensor_count = lax.axis_size("tensor")
    couples = dp_count // 2
    seq_at = lax.axis_index("seq")
    dp_at = lax.axis_index("dp")
    tensor_at = lax.axis_index("tensor")
    core = dp_at % 2
    spans = rows // SPAN
    capacity = neighbour_kv.shape[0]
    pairs = capacity // seq_count
    whole_blocks = pairs == spans
    per = span_act.shape[1] // depth // 2
    half = width // 2
    opposite = tensor_count // 2

    def columns_of(which):
        return jnp.concatenate(
            [
                lax.dynamic_slice(span_act, (0, (2 * p + which) * depth), (rows, depth))
                for p in range(per)
            ],
            axis=1,
        )

    act_mine, act_other = columns_of(core), columns_of(1 - core)
    act_both = jnp.concatenate([act_mine, swap(act_other)], axis=0)

    q_weight = after(q_weight, act_other)
    acts = gather_ring(act_both, "tensor", tensor_count, opposite - 1)
    along_seq = gather_ring(q_weight, "seq", seq_count)
    along_dp = gather_ring(q_weight, "dp", couples)

    cut = width * 5 // 8 // HD * HD
    left_from = [block[:, :cut] for block in along_seq[1:]]
    right_from = [block[:, cut:] for block in along_dp[1:]]
    left_from, right_from, grad_out = lax.optimization_barrier((left_from, right_from, out_grad))
    corner_left = [gather_ring(block, "dp", couples) for block in left_from]
    corner_right = [gather_ring(block, "seq", seq_count) for block in right_from]
    acts[opposite] = jnp.concatenate(
        [
            shift(acts[opposite - 1][:rows], "tensor", 1),
            shift(after(acts[opposite + 1][rows:], grad_out), "tensor", -1),
        ],
        axis=0,
    )
    depth_blocks = [(tensor_at - k) % tensor_count for k in range(tensor_count)]
    table = jnp.stack(depth_blocks).astype(jnp.int32)

    def block_at(i, j):
        block = ((seq_at - i) % seq_count) * dp_count + ((dp_at // 2 - j) % couples) * 2
        return block // (2 * per), (block % (2 * per)) // 2

    places = [(i, j) for i in range(seq_count) for j in range(couples)]
    weights = jnp.zeros((tensor_count, per * depth, width), BF16)
    for i, j in places:
        at, inner = block_at(i, j)
        if j == 0:
            pieces = [(along_seq[i], 0)]
        elif i == 0:
            pieces = [(along_dp[j], 0)]
        else:
            pieces = [(corner_left[i - 1][j], 0), (corner_right[j - 1][i], cut)]
        for piece, start in pieces:
            weights = lax.dynamic_update_slice(weights, piece[None], (at, inner * depth, start))

    groups = owner.reshape(seq_count, dp_count, spans)
    groups = lax.dynamic_index_in_dim(groups, dp_at, 1, keepdims=False)
    mine = lax.dynamic_index_in_dim(groups, seq_at, 0, keepdims=False)

    def order(group, target):
        names = group == target
        at = jnp.arange(spans)
        ahead = (names[None, :] & ~names[:, None]) | (
            (names[None, :] == names[:, None]) & (at[None, :] < at[:, None])
        )
        return jnp.sum(ahead.astype(jnp.int32), axis=1), names.astype(jnp.int32)

    def message(target):
        place, names = order(mine, target)
        hit = place[None, :] == jnp.arange(pairs)[:, None]
        return hit & (names[None, :] == 1)

    def to_owner(value, step):
        value = value.reshape(spans, SPAN, -1)
        if not whole_blocks:
            hit = message((seq_at + step) % seq_count)
            value = jnp.sum(
                jnp.where(hit[:, :, None, None], value[None], jnp.zeros((), BF16)), axis=1
            )
        return shift(value, "seq", step) if step else value

    def from_owner(value, step):
        value = shift(value, "seq", -step) if step else value
        if not whole_blocks:
            hit = message((seq_at + step) % seq_count)
            value = jnp.sum(
                jnp.where(hit[:, :, None, None], value[:, None], jnp.zeros((), BF16)), axis=0
            )
        return value.reshape(rows, -1)

    def slots_of(step):
        source = (seq_at - step) % seq_count
        group = lax.dynamic_index_in_dim(groups, source, 0, keepdims=False)
        place, names = order(group, seq_at)
        if not whole_blocks:
            place = jnp.arange(pairs)
            names = (place < jnp.sum(names)).astype(jnp.int32)
        return source * pairs + place, names

    live = jnp.broadcast_to((neighbour_ids != 0).astype(F32)[:, :, None], (capacity, KEYS, HD))
    slots = [slots_of(step) for step in range(seq_count)]
    grads = [to_owner(grad_out, step) for step in range(seq_count)]

    table = after(table, *grads)
    queries = []
    for part in range(2):
        partial = product(acts, weights, table, part * half, half)
        queries.append((partial[:rows] + swap(partial[rows:])).astype(BF16))
    asked = [[to_owner(value, step) for step in range(seq_count)] for value in queries]

    stacked = jnp.stack(after(acts, queries[1]))

    def act_block(i, j):
        at, inner = block_at(i, j)
        k = (tensor_at - at) % tensor_count
        return lax.dynamic_slice(stacked, (k, 0, inner * depth), (1, 2 * rows, depth))[0]

    def weight_product(i, j, grad):
        found = dot(act_block(i, j), grad, ((0,), (0,)))
        return lax.optimization_barrier(found.astype(BF16))

    kv_grad = None
    both_grads, corners = [], []
    corner_places = [(i, j) for i in range(1, seq_count) for j in range(1, couples)]
    for part in range(2):
        answers = []
        for step in range(seq_count):
            answer, kv_grad = attend(
                *slots[step], asked[part][step], grads[step], neighbour_kv, live, part, kv_grad
            )
            answers.append(from_owner(answer, step))
        if part:
            answers[-1] = after(answers[-1], corners[0][corner_places[-1]])
        grad = sum(answers[1:], answers[0])
        both_grads.append(jnp.concatenate([grad, swap(grad)], axis=0))
        if part == 0:
            corners.append({at: weight_product(*at, both_grads[0]) for at in corner_places[::-1]})
    both_grad = jnp.concatenate(both_grads, axis=1)

    def act_product(k):
        block = lax.dynamic_index_in_dim(weights, depth_blocks[k], 0, keepdims=False)
        return lax.optimization_barrier(dot(both_grad, block, ((1,), (1,))).astype(BF16))

    far = act_product(opposite)
    up, down = shift(far[:rows], "tensor", 1), shift(far[rows:], "tensor", -1)

    late_grad = after(both_grads[1], far)
    corners.append({at: weight_product(*at, late_grad) for at in corner_places[::-1]})
    left = [
        reduce_rings([([None] + [corners[0][i, j] for j in range(1, couples)], True)], "dp")[0][1:]
        for i in range(1, seq_count)
    ]
    right = [
        reduce_rings([([None] + [corners[1][i, j] for i in range(1, seq_count)], True)], "seq")[0][1:]
        for j in range(1, couples)
    ]
    act_parts = {k: act_product(k) for k in range(tensor_count) if k != opposite}
    own = weight_product(0, 0, both_grad)
    beside_seq = [weight_product(i, 0, both_grad) for i in range(1, seq_count)]
    beside_dp = [weight_product(0, j, both_grad) for j in range(1, couples)]
    up, down, left, right, act_parts, own, beside_seq, beside_dp = lax.optimization_barrier(
        (up, down, left, right, act_parts, own, beside_seq, beside_dp)
    )

    beside_seq = [
        lax.dynamic_update_slice(block, total([block[:, :half]] + came).astype(BF16), (0, 0))
        for block, came in zip(beside_seq, left)
    ]
    from_seq = reduce_rings([([None] + beside_seq, True)], "seq")[0][1:]
    for m in range(opposite - 1, 0, -1):
        block = act_parts[tensor_count - m]
        if up.shape[0] == rows:
            up = lax.dynamic_update_slice(block, total([block[:rows], up]).astype(BF16), (0, 0))
        else:
            up = total([block, up]).astype(BF16)
        block = act_parts[m]
        if down.shape[0] == rows:
            down = lax.dynamic_update_slice(
                block, total([block[rows:], down]).astype(BF16), (rows, 0)
            )
        else:
            down = total([block, down]).astype(BF16)
        up, down = shift(up, "tensor", 1), shift(down, "tensor", -1)
    beside_dp = [
        lax.dynamic_update_slice(block, total([block[:, half:]] + came).astype(BF16), (0, half))
        for block, came in zip(beside_dp, right)
    ]
    from_dp = reduce_rings([([None] + beside_dp, True)], "dp")[0][1:]

    arrived = swap(total([part[rows:] for part in (act_parts[0], up, down)]).astype(BF16))
    act_grad = assemble(core, act_parts[0], up, down, arrived, depth)
    weight_grad = total([own] + from_seq + from_dp)
    return (act_grad, weight_grad, kv_grad)


def solution(mesh):
    in_specs = (
        P(("seq", "dp"), "tensor"),
        P(("seq", "dp"), "tensor"),
        P(("seq", "dp"), "tensor"),
        P(("seq", "dp"), None, None, "tensor"),
        P(("seq", "dp"), None),
        P(),
    )
    out_specs = (
        P(("seq", "dp"), "tensor"),
        P(("seq", "dp"), "tensor"),
        P(("seq", "dp"), None, None, "tensor"),
    )
    return jax.shard_map(
        on_device, mesh=mesh, in_specs=in_specs, out_specs=out_specs, check_vma=False
    )
```

```python
import functools

import jax
import jax.numpy as jnp
from jax import lax
from jax.experimental import pallas as pl
from jax.experimental.pallas import tpu as pltpu
from jax.sharding import PartitionSpec as P

HD = 128
SPAN = 64
KEYS = 256
F32 = jnp.float32
BF16 = jnp.bfloat16


def dot(a, b, contract):
    return lax.dot_general(a, b, (contract, ((), ())), preferred_element_type=F32)


def shift(value, axis, step=1):
    stride = 2 if axis == "dp" else 1
    size = lax.axis_size(axis)
    return lax.ppermute(value, axis, [(i, (i + step * stride) % size) for i in range(size)])


def swap(value):
    return lax.ppermute(value, "dp", [(i, i ^ 1) for i in range(lax.axis_size("dp"))])


def after(value, *others):
    return lax.optimization_barrier((value, *others))[0]


def reaches(size, far_up):
    up = size // 2 if far_up else (size - 1) // 2
    return up, size - 1 - up


def gather_ring(block, axis, size, rounds=None):
    blocks = [block] + [None] * (size - 1)
    for m in range(1, (size // 2 if rounds is None else rounds) + 1):
        came = {}
        for sign, count in zip((1, -1), reaches(size, True)):
            if m <= count:
                came[(sign * m) % size] = shift(blocks[(sign * (m - 1)) % size], axis, sign)
        for k, value in zip(came, lax.optimization_barrier(tuple(came.values()))):
            blocks[k] = value
    return blocks


def reduce_rings(streams, axis):
    size = len(streams[0][0])
    found = [[blocks[0]] for blocks, _ in streams]
    came = {}
    for m in range(1, size // 2 + 1):
        sent = {}
        for s, (blocks, far_up) in enumerate(streams):
            for sign, count in zip((1, -1), reaches(size, far_up)):
                if m <= count:
                    block = blocks[(-sign * (count - m + 1)) % size]
                    if m > 1:
                        block = came[s, sign].astype(F32) + block.astype(F32)
                    sent[s, sign] = shift(block.astype(BF16), axis, sign)
        came = dict(zip(sent, lax.optimization_barrier(tuple(sent.values()))))
        for (s, sign), block in came.items():
            if m == reaches(size, streams[s][1])[0 if sign == 1 else 1]:
                found[s].append(block)
    return found


def total(values):
    return functools.reduce(lambda a, b: a + b, [value.astype(F32) for value in values])


def product_kernel(count, start, table_ref, *refs):
    blocks, weight_ref, out_ref = refs[:count], refs[count], refs[count + 1]
    tile = min(256, out_ref.shape[1])
    for at in range(0, out_ref.shape[1], tile):
        total = None
        for k in range(count):
            weight = weight_ref[table_ref[k], :, start + at:start + at + tile]
            part = dot(blocks[k][...], weight, ((1,), (0,)))
            total = part if total is None else total + part
        out_ref[:, at:at + tile] = total


def product(blocks, weights, table, start, width):
    count, (rows, depth) = len(blocks), blocks[0].shape
    return pl.pallas_call(
        functools.partial(product_kernel, count, start),
        out_shape=jax.ShapeDtypeStruct((rows, width), F32),
        in_specs=[pl.BlockSpec(memory_space=pltpu.SMEM)]
        + [pl.BlockSpec(memory_space=pltpu.VMEM)] * (count + 1),
        out_specs=pl.BlockSpec(memory_space=pltpu.VMEM),
        compiler_params=pltpu.CompilerParams(vmem_limit_bytes=16 * 1024 * 1024),
        cost_estimate=pl.CostEstimate(
            flops=2 * rows * count * depth * width,
            bytes_accessed=2 * count * depth * (rows + width) + 4 * rows * width,
            transcendentals=0,
        ),
    )(table, *blocks, weights)


def attend_block(q_ref, g_ref, kv_ref, live_ref, dq_ref, grad_ref):
    pairs = q_ref.shape[-1] // HD // 2
    scale = HD ** (-0.5)
    live = live_ref[...] > 0.5
    zero = jnp.zeros((SPAN, HD), BF16)

    def diagonal(ref, start):
        one = ref[:, start:start + HD]
        two = ref[:, start + HD:start + 2 * HD]
        return jnp.concatenate(
            [jnp.concatenate([one, zero], axis=1), jnp.concatenate([zero, two], axis=1)], axis=0
        )

    def first(pair):
        start = pair * 2 * HD
        columns = slice(start, start + 2 * HD)
        scores = dot(kv_ref[0, :, columns], diagonal(q_ref, start), ((1,), (1,)))
        prob_grad = dot(kv_ref[1, :, columns], diagonal(g_ref, start), ((1,), (1,)))
        return scores, prob_grad

    ahead = first(0)
    for pair in range(pairs):
        scores, prob_grad = ahead
        if pair + 1 < pairs:
            ahead = first(pair + 1)
        start = pair * 2 * HD
        columns = slice(start, start + 2 * HD)
        scores = jnp.where(live, scores * scale, -1e30)
        expo = jnp.exp(scores - jnp.max(scores, axis=0, keepdims=True))
        probs = expo * (1.0 / jnp.sum(expo, axis=0, keepdims=True))
        center = jnp.sum(probs * prob_grad, axis=0, keepdims=True)
        score_grad = (probs * (prob_grad - center) * scale).astype(BF16)
        value_grad = dot(probs.astype(BF16), diagonal(g_ref, start), ((1,), (0,)))
        key_grad = dot(score_grad, diagonal(q_ref, start), ((1,), (0,)))
        both = dot(score_grad, kv_ref[0, :, columns], ((0,), (0,)))
        grad_ref[1, :, columns] = value_grad.astype(BF16)
        grad_ref[0, :, columns] = key_grad.astype(BF16)
        dq_ref[:, columns] = jnp.concatenate([both[:SPAN, :HD], both[SPAN:, HD:]], axis=1).astype(
            BF16
        )


def attend_kernel(table_ref, q_ref, g_ref, live_ref, kv_ref, dq_ref, grad_ref):
    named = table_ref[pl.num_programs(0) + pl.program_id(0)]

    @pl.when(named == 0)
    def _():
        dq_ref[...] = jnp.zeros_like(dq_ref)
        grad_ref[...] = jnp.zeros_like(grad_ref)

    @pl.when(named != 0)
    def _():
        refs = (q_ref, g_ref, kv_ref, live_ref, dq_ref, grad_ref)
        attend_block(*(ref.at[0] for ref in refs))


def attend(slots, named, queries, grads, live, part, state):
    count, _, width = queries.shape
    keys = state.shape[2]
    heads = width // HD
    table = jnp.concatenate([slots, named]).astype(jnp.int32)
    span_block = pl.BlockSpec((1, SPAN, width), lambda r, t: (r, 0, 0))
    part_block = pl.BlockSpec((1, SPAN, width), lambda r, t: (r, 0, part))
    live_block = pl.BlockSpec((1, keys, HD), lambda r, t: (t[r], 0, 0))
    kv_block = pl.BlockSpec((1, 2, keys, width), lambda r, t: (t[r], 0, 0, part))
    return pl.pallas_call(
        attend_kernel,
        grid_spec=pltpu.PrefetchScalarGridSpec(
            num_scalar_prefetch=1,
            grid=(count,),
            in_specs=[span_block, part_block, live_block, kv_block],
            out_specs=[span_block, kv_block],
        ),
        out_shape=[
            jax.ShapeDtypeStruct(queries.shape, BF16),
            jax.ShapeDtypeStruct(state.shape, BF16),
        ],
        input_output_aliases={4: 1},
        compiler_params=pltpu.CompilerParams(vmem_limit_bytes=12 * 1024 * 1024),
        cost_estimate=pl.CostEstimate(
            flops=count * heads * 5 * 2 * SPAN * keys * HD * 4,
            bytes_accessed=count * 4 * keys * width * 2,
            transcendentals=count * heads * SPAN * keys,
        ),
    )(table, queries, grads, live, state)


def copy_kernel(in_ref, out_ref, sem):
    copy = pltpu.make_async_copy(in_ref, out_ref, sem)
    copy.start()
    copy.wait()


def copied(value):
    return pl.pallas_call(
        copy_kernel,
        in_specs=[pl.BlockSpec(memory_space=pltpu.HBM)],
        out_specs=pl.BlockSpec(memory_space=pltpu.HBM),
        out_shape=jax.ShapeDtypeStruct(value.shape, value.dtype),
        scratch_shapes=[pltpu.SemaphoreType.DMA],
        cost_estimate=pl.CostEstimate(
            flops=0, bytes_accessed=2 * value.size * 2, transcendentals=0
        ),
    )(value)


def assemble_kernel(depth, core_ref, own_ref, up_ref, down_ref, arrived_ref, out_ref):
    kept = own_ref[...].astype(F32) + up_ref[...].astype(F32) + down_ref[...].astype(F32)
    kept = kept.astype(BF16)
    for p in range(kept.shape[1] // depth):
        columns = slice(p * depth, (p + 1) * depth)
        mine, other = 2 * p + core_ref[0], 2 * p + 1 - core_ref[0]
        out_ref[:, pl.ds(pl.multiple_of(mine * depth, depth), depth)] = kept[:, columns]
        out_ref[:, pl.ds(pl.multiple_of(other * depth, depth), depth)] = arrived_ref[:, columns]


def assemble(core, own, up, down, arrived, depth):
    rows, columns = arrived.shape
    tile = min(64, rows)
    block = pl.BlockSpec((tile, columns), lambda r: (r, 0))
    return pl.pallas_call(
        functools.partial(assemble_kernel, depth),
        grid=(rows // tile,),
        in_specs=[pl.BlockSpec(memory_space=pltpu.SMEM)] + [block] * 4,
        out_specs=pl.BlockSpec((tile, 2 * columns), lambda r: (r, 0)),
        out_shape=jax.ShapeDtypeStruct((rows, 2 * columns), BF16),
        compiler_params=pltpu.CompilerParams(vmem_limit_bytes=16 * 1024 * 1024),
        cost_estimate=pl.CostEstimate(
            flops=2 * rows * columns, bytes_accessed=12 * rows * columns, transcendentals=0
        ),
    )(jnp.reshape(core, (1,)).astype(jnp.int32), own, up, down, arrived)


def on_device(span_act, q_weight, out_grad, neighbour_kv, neighbour_ids, owner):
    rows, width = out_grad.shape
    depth = q_weight.shape[0]
    seq_count = lax.axis_size("seq")
    dp_count = lax.axis_size("dp")
    tensor_count = lax.axis_size("tensor")
    couples = dp_count // 2
    seq_at = lax.axis_index("seq")
    dp_at = lax.axis_index("dp")
    tensor_at = lax.axis_index("tensor")
    core = dp_at % 2
    spans = rows // SPAN
    capacity = neighbour_kv.shape[0]
    pairs = capacity // seq_count
    whole_blocks = pairs == spans
    per = span_act.shape[1] // depth // 2
    half = width // 2
    opposite = tensor_count // 2

    raw = gather_ring(span_act, "tensor", tensor_count, opposite - 1)
    along_seq = gather_ring(q_weight, "seq", seq_count)
    along_dp = gather_ring(q_weight, "dp", couples)

    groups = owner.reshape(seq_count, dp_count, spans)
    groups = lax.dynamic_index_in_dim(groups, dp_at, 1, keepdims=False)
    mine = lax.dynamic_index_in_dim(groups, seq_at, 0, keepdims=False)

    def order(group, target):
        names = group == target
        at = jnp.arange(spans)
        ahead = (names[None, :] & ~names[:, None]) | (
            (names[None, :] == names[:, None]) & (at[None, :] < at[:, None])
        )
        return jnp.sum(ahead.astype(jnp.int32), axis=1), names.astype(jnp.int32)

    def message(target):
        place, names = order(mine, target)
        hit = place[None, :] == jnp.arange(pairs)[:, None]
        return hit & (names[None, :] == 1)

    def to_owner(value, step):
        value = value.reshape(spans, SPAN, -1)
        if not whole_blocks:
            hit = message((seq_at + step) % seq_count)
            value = jnp.sum(
                jnp.where(hit[:, :, None, None], value[None], jnp.zeros((), BF16)), axis=1
            )
        return shift(value, "seq", step) if step else value

    state = copied(neighbour_kv)
    left_from = [block[:, :half] for block in along_seq[1:]]
    right_from = [block[:, half:] for block in along_dp[1:]]
    left_from, right_from, state = lax.optimization_barrier((left_from, right_from, state))
    corner_left = [gather_ring(block, "dp", couples) for block in left_from]
    corner_right = [gather_ring(block, "seq", seq_count) for block in right_from]
    up_from, down_from = raw[opposite - 1][:rows // 2], raw[opposite + 1][rows // 2:]
    up_from, down_from = lax.optimization_barrier((up_from, down_from, left_from, right_from))[:2]
    raw[opposite] = jnp.concatenate(
        [shift(up_from, "tensor", 1), shift(down_from, "tensor", -1)], axis=0
    )
    grad_out = after(out_grad, corner_right)
    grads = [to_owner(grad_out, step) for step in range(seq_count)]

    def columns_of(block, which):
        return jnp.concatenate(
            [
                lax.dynamic_slice(block, (0, (2 * p + which) * depth), (block.shape[0], depth))
                for p in range(per)
            ],
            axis=1,
        )

    near = [k for k in range(tensor_count) if k != opposite]
    others = swap(jnp.concatenate([columns_of(raw[k], 1 - core) for k in near], axis=0))
    others = {k: others[n * rows:(n + 1) * rows] for n, k in enumerate(near)}
    others[opposite] = swap(after(columns_of(raw[opposite], 1 - core), others))
    acts = [
        jnp.concatenate([columns_of(raw[k], core), others[k]], axis=0) for k in range(tensor_count)
    ]
    depth_blocks = [(tensor_at - k) % tensor_count for k in range(tensor_count)]
    table = jnp.stack(depth_blocks).astype(jnp.int32)

    def block_at(i, j):
        block = ((seq_at - i) % seq_count) * dp_count + ((dp_at // 2 - j) % couples) * 2
        return block // (2 * per), (block % (2 * per)) // 2

    places = [(i, j) for i in range(seq_count) for j in range(couples)]
    weights = jnp.zeros((tensor_count, per * depth, width), BF16)
    for i, j in places:
        at, inner = block_at(i, j)
        if j == 0:
            pieces = [(along_seq[i], 0)]
        elif i == 0:
            pieces = [(along_dp[j], 0)]
        else:
            pieces = [(corner_left[i - 1][j], 0), (corner_right[j - 1][i], half)]
        for piece, start in pieces:
            weights = lax.dynamic_update_slice(weights, piece[None], (at, inner * depth, start))

    def from_owner(value, step):
        value = shift(value, "seq", -step) if step else value
        if not whole_blocks:
            hit = message((seq_at + step) % seq_count)
            value = jnp.sum(
                jnp.where(hit[:, :, None, None], value[:, None], jnp.zeros((), BF16)), axis=0
            )
        return value.reshape(rows, -1)

    def slots_of(step):
        source = (seq_at - step) % seq_count
        group = lax.dynamic_index_in_dim(groups, source, 0, keepdims=False)
        place, names = order(group, seq_at)
        if not whole_blocks:
            place = jnp.arange(pairs)
            names = (place < jnp.sum(names)).astype(jnp.int32)
        return source * pairs + place, names

    live = jnp.broadcast_to((neighbour_ids != 0).astype(F32)[:, :, None], (capacity, KEYS, HD))
    slots = [slots_of(step) for step in range(seq_count)]

    queries = []
    for part in range(2):
        partial = product(acts, weights, table, part * half, half)
        arrived = swap(partial[rows:])
        if part == 0:
            partial = after(partial, grads)
        queries.append((partial[:rows] + arrived).astype(BF16))
    asked = [[to_owner(value, step) for step in range(seq_count)] for value in queries]
    asked[0][0] = after(asked[0][0], queries[1])

    stacked = jnp.stack(after(acts, queries[1]))

    def act_block(i, j):
        at, inner = block_at(i, j)
        k = (tensor_at - at) % tensor_count
        return lax.dynamic_slice(stacked, (k, 0, inner * depth), (1, 2 * rows, depth))[0]

    def weight_product(i, j, grad):
        found = dot(act_block(i, j), grad, ((0,), (0,)))
        return lax.optimization_barrier(found.astype(BF16))

    both_grads, corners = [], []
    corner_places = [(i, j) for i in range(1, seq_count) for j in range(1, couples)]
    for part in range(2):
        answers = []
        for step in range(seq_count):
            answer, state = attend(
                *slots[step], asked[part][step], grads[step], live, part, state
            )
            answers.append(from_owner(answer, step))
        if part:
            answers[-1] = after(answers[-1], corners[0][corner_places[-1]])
        grad = sum(answers[1:], answers[0])
        both_grads.append(jnp.concatenate([grad, swap(grad)], axis=0))
        if part == 0:
            corners.append({at: weight_product(*at, both_grads[0]) for at in corner_places[::-1]})
    both_grad = jnp.concatenate(both_grads, axis=1)

    def act_product(k):
        block = lax.dynamic_index_in_dim(weights, depth_blocks[k], 0, keepdims=False)
        return lax.optimization_barrier(dot(both_grad, block, ((1,), (1,))).astype(BF16))

    far = act_product(opposite)
    up, down = shift(far[:rows], "tensor", 1), shift(far[rows:], "tensor", -1)

    late_grad = after(both_grads[1], far)
    corners.append({at: weight_product(*at, late_grad) for at in corner_places[::-1]})
    left = [
        reduce_rings([([None] + [corners[0][i, j] for j in range(1, couples)], True)], "dp")[0][1:]
        for i in range(1, seq_count)
    ]
    right = [
        reduce_rings([([None] + [corners[1][i, j] for i in range(1, seq_count)], True)], "seq")[0][1:]
        for j in range(1, couples)
    ]
    act_parts = {k: act_product(k) for k in range(tensor_count) if k != opposite}
    own = weight_product(0, 0, both_grad)
    beside_seq = [weight_product(i, 0, both_grad) for i in range(1, seq_count)]
    beside_dp = [weight_product(0, j, both_grad) for j in range(1, couples)]
    up, down, left, right, act_parts, own, beside_seq, beside_dp = lax.optimization_barrier(
        (up, down, left, right, act_parts, own, beside_seq, beside_dp)
    )

    beside_seq = [
        lax.dynamic_update_slice(block, total([block[:, :half]] + came).astype(BF16), (0, 0))
        for block, came in zip(beside_seq, left)
    ]
    from_seq = reduce_rings([([None] + beside_seq, True)], "seq")[0][1:]
    for m in range(opposite - 1, 0, -1):
        block = act_parts[tensor_count - m]
        if up.shape[0] == rows:
            up = lax.dynamic_update_slice(block, total([block[:rows], up]).astype(BF16), (0, 0))
        else:
            up = total([block, up]).astype(BF16)
        block = act_parts[m]
        if down.shape[0] == rows:
            down = lax.dynamic_update_slice(
                block, total([block[rows:], down]).astype(BF16), (rows, 0)
            )
        else:
            down = total([block, down]).astype(BF16)
        up, down = shift(up, "tensor", 1), shift(down, "tensor", -1)
    beside_dp = [
        lax.dynamic_update_slice(block, total([block[:, half:]] + came).astype(BF16), (0, half))
        for block, came in zip(beside_dp, right)
    ]
    from_dp = reduce_rings([([None] + beside_dp, True)], "dp")[0][1:]

    arrived = swap(total([part[rows:] for part in (act_parts[0], up, down)]).astype(BF16))
    act_grad = assemble(core, act_parts[0], up, down, arrived, depth)
    weight_grad = total([own] + from_seq + from_dp)
    return (act_grad, weight_grad, state)


def solution(mesh):
    in_specs = (
        P(("seq", "dp"), "tensor"),
        P(("seq", "dp"), "tensor"),
        P(("seq", "dp"), "tensor"),
        P(("seq", "dp"), None, None, "tensor"),
        P(("seq", "dp"), None),
        P(),
    )
    out_specs = (
        P(("seq", "dp"), "tensor"),
        P(("seq", "dp"), "tensor"),
        P(("seq", "dp"), None, None, "tensor"),
    )
    return jax.shard_map(
        on_device, mesh=mesh, in_specs=in_specs, out_specs=out_specs, check_vma=False
    )
```

```python
import functools

import jax
import jax.numpy as jnp
from jax import lax
from jax.experimental import pallas as pl
from jax.experimental.pallas import tpu as pltpu
from jax.sharding import PartitionSpec as P

HD = 128
SPAN = 64
KEYS = 256
F32 = jnp.float32
BF16 = jnp.bfloat16


def dot(a, b, contract):
    return lax.dot_general(a, b, (contract, ((), ())), preferred_element_type=F32)


def shift(value, axis, step=1):
    stride = 2 if axis == "dp" else 1
    size = lax.axis_size(axis)
    return lax.ppermute(value, axis, [(i, (i + step * stride) % size) for i in range(size)])


def swap(value):
    return lax.ppermute(value, "dp", [(i, i ^ 1) for i in range(lax.axis_size("dp"))])


def after(value, *others):
    return lax.optimization_barrier((value, *others))[0]


def reaches(size, far_up):
    up = size // 2 if far_up else (size - 1) // 2
    return up, size - 1 - up


def gather_ring(block, axis, size, rounds=None):
    blocks = [block] + [None] * (size - 1)
    for m in range(1, (size // 2 if rounds is None else rounds) + 1):
        came = {}
        for sign, count in zip((1, -1), reaches(size, True)):
            if m <= count:
                came[(sign * m) % size] = shift(blocks[(sign * (m - 1)) % size], axis, sign)
        for k, value in zip(came, lax.optimization_barrier(tuple(came.values()))):
            blocks[k] = value
    return blocks


def reduce_rings(streams, axis):
    size = len(streams[0][0])
    found = [[blocks[0]] for blocks, _ in streams]
    came = {}
    for m in range(1, size // 2 + 1):
        sent = {}
        for s, (blocks, far_up) in enumerate(streams):
            for sign, count in zip((1, -1), reaches(size, far_up)):
                if m <= count:
                    block = blocks[(-sign * (count - m + 1)) % size]
                    if m > 1:
                        block = came[s, sign].astype(F32) + block.astype(F32)
                    sent[s, sign] = shift(block.astype(BF16), axis, sign)
        came = dict(zip(sent, lax.optimization_barrier(tuple(sent.values()))))
        for (s, sign), block in came.items():
            if m == reaches(size, streams[s][1])[0 if sign == 1 else 1]:
                found[s].append(block)
    return found


def total(values):
    return functools.reduce(lambda a, b: a + b, [value.astype(F32) for value in values])


def product_kernel(count, start, table_ref, *refs):
    blocks, weight_ref, out_ref = refs[:count], refs[count], refs[count + 1]
    tile = min(256, out_ref.shape[1])
    for at in range(0, out_ref.shape[1], tile):
        total = None
        for k in range(count):
            weight = weight_ref[table_ref[k], :, start + at:start + at + tile]
            part = dot(blocks[k][...], weight, ((1,), (0,)))
            total = part if total is None else total + part
        out_ref[:, at:at + tile] = total


def product(blocks, weights, table, start, width):
    count, (rows, depth) = len(blocks), blocks[0].shape
    return pl.pallas_call(
        functools.partial(product_kernel, count, start),
        out_shape=jax.ShapeDtypeStruct((rows, width), F32),
        in_specs=[pl.BlockSpec(memory_space=pltpu.SMEM)]
        + [pl.BlockSpec(memory_space=pltpu.VMEM)] * (count + 1),
        out_specs=pl.BlockSpec(memory_space=pltpu.VMEM),
        compiler_params=pltpu.CompilerParams(vmem_limit_bytes=16 * 1024 * 1024),
        cost_estimate=pl.CostEstimate(
            flops=2 * rows * count * depth * width,
            bytes_accessed=2 * count * depth * (rows + width) + 4 * rows * width,
            transcendentals=0,
        ),
    )(table, *blocks, weights)


def attend_block(q_ref, g_ref, kv_ref, live_ref, dq_ref, grad_ref):
    pairs = q_ref.shape[-1] // HD // 2
    scale = HD ** (-0.5)
    live = live_ref[...] > 0.5
    zero = jnp.zeros((SPAN, HD), BF16)

    def diagonal(ref, start):
        one = ref[:, start:start + HD]
        two = ref[:, start + HD:start + 2 * HD]
        return jnp.concatenate(
            [jnp.concatenate([one, zero], axis=1), jnp.concatenate([zero, two], axis=1)], axis=0
        )

    def first(pair):
        start = pair * 2 * HD
        columns = slice(start, start + 2 * HD)
        scores = dot(kv_ref[0, :, columns], diagonal(q_ref, start), ((1,), (1,)))
        prob_grad = dot(kv_ref[1, :, columns], diagonal(g_ref, start), ((1,), (1,)))
        return scores, prob_grad

    ahead = first(0)
    for pair in range(pairs):
        scores, prob_grad = ahead
        if pair + 1 < pairs:
            ahead = first(pair + 1)
        start = pair * 2 * HD
        columns = slice(start, start + 2 * HD)
        scores = jnp.where(live, scores * scale, -1e30)
        expo = jnp.exp(scores - jnp.max(scores, axis=0, keepdims=True))
        probs = expo * (1.0 / jnp.sum(expo, axis=0, keepdims=True))
        center = jnp.sum(probs * prob_grad, axis=0, keepdims=True)
        score_grad = (probs * (prob_grad - center) * scale).astype(BF16)
        value_grad = dot(probs.astype(BF16), diagonal(g_ref, start), ((1,), (0,)))
        key_grad = dot(score_grad, diagonal(q_ref, start), ((1,), (0,)))
        both = dot(score_grad, kv_ref[0, :, columns], ((0,), (0,)))
        grad_ref[1, :, columns] = value_grad.astype(BF16)
        grad_ref[0, :, columns] = key_grad.astype(BF16)
        dq_ref[:, columns] = jnp.concatenate([both[:SPAN, :HD], both[SPAN:, HD:]], axis=1).astype(
            BF16
        )


def attend_kernel(table_ref, q_ref, g_ref, live_ref, kv_ref, *rest):
    dq_ref, grad_ref = rest[-2:]
    named = table_ref[pl.num_programs(0) + pl.program_id(0)]

    @pl.when(named == 0)
    def _():
        dq_ref[...] = jnp.zeros_like(dq_ref)
        grad_ref[...] = jnp.zeros_like(grad_ref)

    @pl.when(named != 0)
    def _():
        refs = (q_ref, g_ref, kv_ref, live_ref, dq_ref, grad_ref)
        attend_block(*(ref.at[0] for ref in refs))


def attend(place, named, source, queries, grads, kv, live, part, before):
    count, _, width = queries.shape
    capacity, keys, _ = live.shape
    heads = width // HD
    table = jnp.concatenate([place, named, source * count + place]).astype(jnp.int32)
    span_block = pl.BlockSpec((1, SPAN, width), lambda r, t: (r, 0, 0))
    part_block = pl.BlockSpec((1, SPAN, width), lambda r, t: (r, 0, part))
    live_block = pl.BlockSpec((1, keys, HD), lambda r, t: (t[2 * count + r], 0, 0))
    kv_block = pl.BlockSpec((1, 2, keys, width), lambda r, t: (t[r], 0, 0, 0))
    grad_block = pl.BlockSpec((1, 2, keys, width), lambda r, t: (t[2 * count + r], 0, 0, part))
    in_specs = [span_block, part_block, live_block, kv_block]
    operands = [table, queries, grads, live, kv]
    aliases = {}
    if before is not None:
        in_specs.append(pl.BlockSpec(memory_space=pl.ANY))
        operands.append(before)
        aliases = {len(operands) - 1: 1}
    return pl.pallas_call(
        attend_kernel,
        grid_spec=pltpu.PrefetchScalarGridSpec(
            num_scalar_prefetch=1,
            grid=(count,),
            in_specs=in_specs,
            out_specs=[span_block, grad_block],
        ),
        out_shape=[
            jax.ShapeDtypeStruct(queries.shape, BF16),
            jax.ShapeDtypeStruct((capacity, 2, keys, 2 * width), BF16),
        ],
        input_output_aliases=aliases,
        compiler_params=pltpu.CompilerParams(vmem_limit_bytes=12 * 1024 * 1024),
        cost_estimate=pl.CostEstimate(
            flops=count * heads * 5 * 2 * SPAN * keys * HD * 4,
            bytes_accessed=count * 4 * keys * width * 2,
            transcendentals=count * heads * SPAN * keys,
        ),
    )(*operands)


def stage_kernel(source_ref, kv_ref, left_ref, right_ref):
    width = left_ref.shape[-1]
    left_ref[...] = kv_ref[:, :, :, :width]
    right_ref[...] = kv_ref[:, :, :, width:]


def stage(kv, source, count):
    _, _, keys, width = kv.shape
    half_block = pl.BlockSpec((1, 2, keys, width // 2), lambda r, t: (r, 0, 0, 0))
    half_shape = jax.ShapeDtypeStruct((count, 2, keys, width // 2), kv.dtype)
    return pl.pallas_call(
        stage_kernel,
        grid_spec=pltpu.PrefetchScalarGridSpec(
            num_scalar_prefetch=1,
            grid=(count,),
            in_specs=[
                pl.BlockSpec((1, 2, keys, width), lambda r, t: (t[0] * count + r, 0, 0, 0))
            ],
            out_specs=[half_block, half_block],
        ),
        out_shape=[half_shape, half_shape],
        compiler_params=pltpu.CompilerParams(vmem_limit_bytes=12 * 1024 * 1024),
        cost_estimate=pl.CostEstimate(
            flops=0, bytes_accessed=8 * count * keys * width, transcendentals=0
        ),
    )(jnp.reshape(source, (1,)).astype(jnp.int32), kv)


def total_kernel(*refs):
    refs[-1][...] = total([ref[...] for ref in refs[:-1]])


def summed(values):
    rows, columns = values[0].shape
    tile = min(128, rows)
    block = pl.BlockSpec((tile, columns), lambda r: (r, 0))
    return pl.pallas_call(
        total_kernel,
        grid=(rows // tile,),
        in_specs=[block] * len(values),
        out_specs=block,
        out_shape=jax.ShapeDtypeStruct((rows, columns), F32),
        compiler_params=pltpu.CompilerParams(vmem_limit_bytes=16 * 1024 * 1024),
        cost_estimate=pl.CostEstimate(
            flops=len(values) * rows * columns,
            bytes_accessed=(2 * len(values) + 4) * rows * columns,
            transcendentals=0,
        ),
    )(*values)


def assemble_kernel(depth, core_ref, own_ref, up_ref, down_ref, arrived_ref, out_ref):
    kept = own_ref[...].astype(F32) + up_ref[...].astype(F32) + down_ref[...].astype(F32)
    kept = kept.astype(BF16)
    for p in range(kept.shape[1] // depth):
        columns = slice(p * depth, (p + 1) * depth)
        mine, other = 2 * p + core_ref[0], 2 * p + 1 - core_ref[0]
        out_ref[:, pl.ds(pl.multiple_of(mine * depth, depth), depth)] = kept[:, columns]
        out_ref[:, pl.ds(pl.multiple_of(other * depth, depth), depth)] = arrived_ref[:, columns]


def assemble(core, own, up, down, arrived, depth):
    rows, columns = arrived.shape
    tile = min(64, rows)
    block = pl.BlockSpec((tile, columns), lambda r: (r, 0))
    return pl.pallas_call(
        functools.partial(assemble_kernel, depth),
        grid=(rows // tile,),
        in_specs=[pl.BlockSpec(memory_space=pltpu.SMEM)] + [block] * 4,
        out_specs=pl.BlockSpec((tile, 2 * columns), lambda r: (r, 0)),
        out_shape=jax.ShapeDtypeStruct((rows, 2 * columns), BF16),
        compiler_params=pltpu.CompilerParams(vmem_limit_bytes=16 * 1024 * 1024),
        cost_estimate=pl.CostEstimate(
            flops=2 * rows * columns, bytes_accessed=12 * rows * columns, transcendentals=0
        ),
    )(jnp.reshape(core, (1,)).astype(jnp.int32), own, up, down, arrived)


def on_device(span_act, q_weight, out_grad, neighbour_kv, neighbour_ids, owner):
    rows, width = out_grad.shape
    depth = q_weight.shape[0]
    seq_count = lax.axis_size("seq")
    dp_count = lax.axis_size("dp")
    tensor_count = lax.axis_size("tensor")
    couples = dp_count // 2
    seq_at = lax.axis_index("seq")
    dp_at = lax.axis_index("dp")
    tensor_at = lax.axis_index("tensor")
    core = dp_at % 2
    spans = rows // SPAN
    capacity = neighbour_kv.shape[0]
    pairs = capacity // seq_count
    whole_blocks = pairs == spans
    per = span_act.shape[1] // depth // 2
    half = width // 2
    opposite = tensor_count // 2

    raw = gather_ring(span_act, "tensor", tensor_count, opposite - 1)
    along_seq = gather_ring(q_weight, "seq", seq_count)
    along_dp = gather_ring(q_weight, "dp", couples)

    groups = owner.reshape(seq_count, dp_count, spans)
    groups = lax.dynamic_index_in_dim(groups, dp_at, 1, keepdims=False)
    mine = lax.dynamic_index_in_dim(groups, seq_at, 0, keepdims=False)

    def order(group, target):
        names = group == target
        at = jnp.arange(spans)
        ahead = (names[None, :] & ~names[:, None]) | (
            (names[None, :] == names[:, None]) & (at[None, :] < at[:, None])
        )
        return jnp.sum(ahead.astype(jnp.int32), axis=1), names.astype(jnp.int32)

    def message(target):
        place, names = order(mine, target)
        hit = place[None, :] == jnp.arange(pairs)[:, None]
        return hit & (names[None, :] == 1)

    def to_owner(value, step):
        value = value.reshape(spans, SPAN, -1)
        if not whole_blocks:
            hit = message((seq_at + step) % seq_count)
            value = jnp.sum(
                jnp.where(hit[:, :, None, None], value[None], jnp.zeros((), BF16)), axis=1
            )
        return shift(value, "seq", step) if step else value

    cut = width * 5 // 8 // HD * HD
    sources = [(seq_at - step) % seq_count for step in range(seq_count)]
    staged = [stage(neighbour_kv, source, pairs) for source in sources]
    left_from = [block[:, :cut] for block in along_seq[1:]]
    right_from = [block[:, cut:] for block in along_dp[1:]]
    left_from, right_from, staged, grad_out = lax.optimization_barrier(
        (left_from, right_from, staged, out_grad)
    )
    corner_left = [gather_ring(block, "dp", couples) for block in left_from]
    corner_right = [gather_ring(block, "seq", seq_count) for block in right_from]
    def columns_of(block, which):
        return jnp.concatenate(
            [
                lax.dynamic_slice(block, (0, (2 * p + which) * depth), (block.shape[0], depth))
                for p in range(per)
            ],
            axis=1,
        )

    near = [k for k in range(tensor_count) if k != opposite]
    others = swap(jnp.concatenate([columns_of(raw[k], 1 - core) for k in near], axis=0))
    up_from, down_from = raw[opposite - 1][:rows // 2], raw[opposite + 1][rows // 2:]
    up_from, down_from = lax.optimization_barrier((up_from, down_from, left_from, right_from))[:2]
    up = shift(up_from, "tensor", 1)
    down_from, grad_out, others = lax.optimization_barrier((down_from, grad_out, others))
    down = shift(down_from, "tensor", -1)
    grads = [to_owner(grad_out, step) for step in range(seq_count)]
    raw[opposite] = jnp.concatenate([up, down], axis=0)
    others = {k: others[n * rows:(n + 1) * rows] for n, k in enumerate(near)}
    others[opposite] = swap(columns_of(raw[opposite], 1 - core))
    acts = [
        jnp.concatenate([columns_of(raw[k], core), others[k]], axis=0) for k in range(tensor_count)
    ]
    depth_blocks = [(tensor_at - k) % tensor_count for k in range(tensor_count)]
    table = after(jnp.stack(depth_blocks).astype(jnp.int32), grads)

    def block_at(i, j):
        block = ((seq_at - i) % seq_count) * dp_count + ((dp_at // 2 - j) % couples) * 2
        return block // (2 * per), (block % (2 * per)) // 2

    places = [(i, j) for i in range(seq_count) for j in range(couples)]
    weights = jnp.zeros((tensor_count, per * depth, width), BF16)
    for i, j in places:
        at, inner = block_at(i, j)
        if j == 0:
            pieces = [(along_seq[i], 0)]
        elif i == 0:
            pieces = [(along_dp[j], 0)]
        else:
            pieces = [(corner_left[i - 1][j], 0), (corner_right[j - 1][i], cut)]
        for piece, start in pieces:
            weights = lax.dynamic_update_slice(weights, piece[None], (at, inner * depth, start))

    def from_owner(value, step):
        value = shift(value, "seq", -step) if step else value
        if not whole_blocks:
            hit = message((seq_at + step) % seq_count)
            value = jnp.sum(
                jnp.where(hit[:, :, None, None], value[:, None], jnp.zeros((), BF16)), axis=0
            )
        return value.reshape(rows, -1)

    def slots_of(step):
        group = lax.dynamic_index_in_dim(groups, sources[step], 0, keepdims=False)
        place, names = order(group, seq_at)
        if not whole_blocks:
            place = jnp.arange(pairs)
            names = (place < jnp.sum(names)).astype(jnp.int32)
        return place, names, sources[step]

    live = jnp.broadcast_to((neighbour_ids != 0).astype(F32)[:, :, None], (capacity, KEYS, HD))
    slots = [slots_of(step) for step in range(seq_count)]

    queries = []
    for part in range(2):
        partial = product(acts, weights, table, part * half, half)
        arrived = swap(partial[rows:])
        queries.append((partial[:rows] + arrived).astype(BF16))
    asked = [[to_owner(value, step) for step in range(seq_count)] for value in queries]
    asked[0][0] = after(asked[0][0], queries[1])

    stacked = jnp.stack(after(acts, queries[1]))

    def act_block(i, j):
        at, inner = block_at(i, j)
        k = (tensor_at - at) % tensor_count
        return lax.dynamic_slice(stacked, (k, 0, inner * depth), (1, 2 * rows, depth))[0]

    def weight_product(i, j, grad):
        found = dot(act_block(i, j), grad, ((0,), (0,)))
        return lax.optimization_barrier(found.astype(BF16))

    kv_grad = None
    both_grads, corners = [], []
    corner_places = [(i, j) for i in range(1, seq_count) for j in range(1, couples)]
    for part in range(2):
        answers = []
        for step in range(seq_count):
            answer, kv_grad = attend(
                *slots[step],
                asked[part][step],
                grads[step],
                staged[step][part],
                live,
                part,
                kv_grad,
            )
            answers.append(from_owner(answer, step))
        if part:
            answers[-1] = after(answers[-1], corners[0][corner_places[-1]])
        grad = sum(answers[1:], answers[0])
        both_grads.append(jnp.concatenate([grad, swap(grad)], axis=0))
        if part == 0:
            corners.append({at: weight_product(*at, both_grads[0]) for at in corner_places[::-1]})
    both_grad = jnp.concatenate(both_grads, axis=1)

    def act_product(k):
        block = lax.dynamic_index_in_dim(weights, depth_blocks[k], 0, keepdims=False)
        return lax.optimization_barrier(dot(both_grad, block, ((1,), (1,))).astype(BF16))

    far = act_product(opposite)
    up, down = shift(far[:rows], "tensor", 1), shift(far[rows:], "tensor", -1)

    late_grad = after(both_grads[1], far)
    corners.append({at: weight_product(*at, late_grad) for at in corner_places[::-1]})
    left = [
        reduce_rings([([None] + [corners[0][i, j] for j in range(1, couples)], True)], "dp")[0][1:]
        for i in range(1, seq_count)
    ]
    right = [
        reduce_rings([([None] + [corners[1][i, j] for i in range(1, seq_count)], True)], "seq")[0][1:]
        for j in range(1, couples)
    ]
    act_parts = {k: act_product(k) for k in range(tensor_count) if k != opposite}
    own = weight_product(0, 0, both_grad)
    beside_seq = [weight_product(i, 0, both_grad) for i in range(1, seq_count)]
    beside_dp = [weight_product(0, j, both_grad) for j in range(1, couples)]
    up, down, left, right, act_parts, own, beside_seq, beside_dp = lax.optimization_barrier(
        (up, down, left, right, act_parts, own, beside_seq, beside_dp)
    )

    beside_seq = [
        lax.dynamic_update_slice(block, total([block[:, :half]] + came).astype(BF16), (0, 0))
        for block, came in zip(beside_seq, left)
    ]
    from_seq = reduce_rings([([None] + beside_seq, True)], "seq")[0][1:]
    for m in range(opposite - 1, 0, -1):
        block = act_parts[tensor_count - m]
        if up.shape[0] == rows:
            up = lax.dynamic_update_slice(block, total([block[:rows], up]).astype(BF16), (0, 0))
        else:
            up = total([block, up]).astype(BF16)
        block = act_parts[m]
        if down.shape[0] == rows:
            down = lax.dynamic_update_slice(
                block, total([block[rows:], down]).astype(BF16), (rows, 0)
            )
        else:
            down = total([block, down]).astype(BF16)
        up, down = shift(up, "tensor", 1), shift(down, "tensor", -1)
    beside_dp = [
        lax.dynamic_update_slice(block, total([block[:, half:]] + came).astype(BF16), (0, half))
        for block, came in zip(beside_dp, right)
    ]
    from_dp = reduce_rings([([None] + beside_dp, True)], "dp")[0][1:]

    arrived = swap(total([part[rows:] for part in (act_parts[0], up, down)]).astype(BF16))
    act_grad = assemble(core, act_parts[0], up, down, arrived, depth)
    weight_grad = summed([own] + from_seq + from_dp)
    return (act_grad, weight_grad, kv_grad)


def solution(mesh):
    in_specs = (
        P(("seq", "dp"), "tensor"),
        P(("seq", "dp"), "tensor"),
        P(("seq", "dp"), "tensor"),
        P(("seq", "dp"), None, None, "tensor"),
        P(("seq", "dp"), None),
        P(),
    )
    out_specs = (
        P(("seq", "dp"), "tensor"),
        P(("seq", "dp"), "tensor"),
        P(("seq", "dp"), None, None, "tensor"),
    )
    return jax.shard_map(
        on_device, mesh=mesh, in_specs=in_specs, out_specs=out_specs, check_vma=False
    )
```

```python
import functools

import jax
import jax.numpy as jnp
from jax import lax
from jax.experimental import pallas as pl
from jax.experimental.pallas import tpu as pltpu
from jax.sharding import PartitionSpec as P

HD = 128
SPAN = 64
KEYS = 256
F32 = jnp.float32
BF16 = jnp.bfloat16


def dot(a, b, contract):
    return lax.dot_general(a, b, (contract, ((), ())), preferred_element_type=F32)


def shift(value, axis, step=1):
    stride = 2 if axis == "dp" else 1
    size = lax.axis_size(axis)
    return lax.ppermute(value, axis, [(i, (i + step * stride) % size) for i in range(size)])


def swap(value):
    return lax.ppermute(value, "dp", [(i, i ^ 1) for i in range(lax.axis_size("dp"))])


def after(value, *others):
    return lax.optimization_barrier((value, *others))[0]


def reaches(size, far_up):
    up = size // 2 if far_up else (size - 1) // 2
    return up, size - 1 - up


def gather_ring(block, axis, size, rounds=None):
    blocks = [block] + [None] * (size - 1)
    for m in range(1, (size // 2 if rounds is None else rounds) + 1):
        came = {}
        for sign, count in zip((1, -1), reaches(size, True)):
            if m <= count:
                came[(sign * m) % size] = shift(blocks[(sign * (m - 1)) % size], axis, sign)
        for k, value in zip(came, lax.optimization_barrier(tuple(came.values()))):
            blocks[k] = value
    return blocks


def reduce_rings(streams, axis):
    size = len(streams[0][0])
    found = [[blocks[0]] for blocks, _ in streams]
    came = {}
    for m in range(1, size // 2 + 1):
        sent = {}
        for s, (blocks, far_up) in enumerate(streams):
            for sign, count in zip((1, -1), reaches(size, far_up)):
                if m <= count:
                    block = blocks[(-sign * (count - m + 1)) % size]
                    if m > 1:
                        block = came[s, sign].astype(F32) + block.astype(F32)
                    sent[s, sign] = shift(block.astype(BF16), axis, sign)
        came = dict(zip(sent, lax.optimization_barrier(tuple(sent.values()))))
        for (s, sign), block in came.items():
            if m == reaches(size, streams[s][1])[0 if sign == 1 else 1]:
                found[s].append(block)
    return found


def total(values):
    return functools.reduce(lambda a, b: a + b, [value.astype(F32) for value in values])


def product_kernel(count, start, table_ref, *refs):
    blocks, weight_ref, out_ref = refs[:count], refs[count], refs[count + 1]
    tile = min(256, out_ref.shape[1])
    for at in range(0, out_ref.shape[1], tile):
        total = None
        for k in range(count):
            weight = weight_ref[table_ref[k], :, start + at:start + at + tile]
            part = dot(blocks[k][...], weight, ((1,), (0,)))
            total = part if total is None else total + part
        out_ref[:, at:at + tile] = total


def product(blocks, weights, table, start, width):
    count, (rows, depth) = len(blocks), blocks[0].shape
    return pl.pallas_call(
        functools.partial(product_kernel, count, start),
        out_shape=jax.ShapeDtypeStruct((rows, width), F32),
        in_specs=[pl.BlockSpec(memory_space=pltpu.SMEM)]
        + [pl.BlockSpec(memory_space=pltpu.VMEM)] * (count + 1),
        out_specs=pl.BlockSpec(memory_space=pltpu.VMEM),
        compiler_params=pltpu.CompilerParams(vmem_limit_bytes=16 * 1024 * 1024),
        cost_estimate=pl.CostEstimate(
            flops=2 * rows * count * depth * width,
            bytes_accessed=2 * count * depth * (rows + width) + 4 * rows * width,
            transcendentals=0,
        ),
    )(table, *blocks, weights)


def attend_block(q_ref, g_ref, kv_ref, live_ref, dq_ref, grad_ref):
    pairs = q_ref.shape[-1] // HD // 2
    scale = HD ** (-0.5)
    live = live_ref[...].astype(F32) > 0.5
    zero = jnp.zeros((SPAN, HD), BF16)

    def diagonal(ref, start):
        one = ref[:, start:start + HD]
        two = ref[:, start + HD:start + 2 * HD]
        return jnp.concatenate(
            [jnp.concatenate([one, zero], axis=1), jnp.concatenate([zero, two], axis=1)], axis=0
        )

    def first(pair):
        start = pair * 2 * HD
        columns = slice(start, start + 2 * HD)
        scores = dot(kv_ref[0, :, columns], diagonal(q_ref, start), ((1,), (1,)))
        prob_grad = dot(kv_ref[1, :, columns], diagonal(g_ref, start), ((1,), (1,)))
        return scores, prob_grad

    ahead = first(0)
    for pair in range(pairs):
        scores, prob_grad = ahead
        if pair + 1 < pairs:
            ahead = first(pair + 1)
        start = pair * 2 * HD
        columns = slice(start, start + 2 * HD)
        scores = jnp.where(live, scores * scale, -1e30)
        expo = jnp.exp(scores - jnp.max(scores, axis=0, keepdims=True))
        probs = expo * (1.0 / jnp.sum(expo, axis=0, keepdims=True))
        center = jnp.sum(probs * prob_grad, axis=0, keepdims=True)
        score_grad = (probs * (prob_grad - center) * scale).astype(BF16)
        value_grad = dot(probs.astype(BF16), diagonal(g_ref, start), ((1,), (0,)))
        key_grad = dot(score_grad, diagonal(q_ref, start), ((1,), (0,)))
        both = dot(score_grad, kv_ref[0, :, columns], ((0,), (0,)))
        grad_ref[1, :, columns] = value_grad.astype(BF16)
        grad_ref[0, :, columns] = key_grad.astype(BF16)
        dq_ref[:, columns] = jnp.concatenate([both[:SPAN, :HD], both[SPAN:, HD:]], axis=1).astype(
            BF16
        )


def attend_kernel(part, table_ref, q_ref, g_ref, live_ref, kv_ref, *rest):
    dq_ref, grad_ref, kv_buf, grad_buf, in_sem, out_sem = rest[-6:]
    count, _, width = q_ref.shape
    keys = kv_buf.shape[2]
    columns = pl.ds(part * width, width)
    pieces = [(i, h) for i in range(2) for h in range(2)]

    def copies(r, back):
        found = []
        for n, (i, h) in enumerate(pieces):
            some = pl.ds(h * (keys // 2), keys // 2)
            if back:
                far = grad_ref.at[table_ref[r], i, some, columns]
                copy = pltpu.make_async_copy(grad_buf.at[r, i, some], far, out_sem.at[r, n])
            else:
                far = kv_ref.at[table_ref[r], i, some, columns]
                copy = pltpu.make_async_copy(far, kv_buf.at[r, i, some], in_sem.at[r, n])
            found.append(copy)
        return found

    @pl.loop(0, count)
    def _(r):
        @pl.when(table_ref[count + r] != 0)
        def _():
            for copy in copies(r, False):
                copy.start()

    @pl.loop(0, count)
    def _(r):
        @pl.when(table_ref[count + r] == 0)
        def _():
            dq_ref[r] = jnp.zeros(dq_ref.shape[1:], BF16)
            grad_buf[r] = jnp.zeros(grad_buf.shape[1:], BF16)

        @pl.when(table_ref[count + r] != 0)
        def _():
            for copy in copies(r, False):
                copy.wait()
            attend_block(
                q_ref.at[r],
                g_ref.at[r, :, columns],
                kv_buf.at[r],
                live_ref.at[table_ref[r]],
                dq_ref.at[r],
                grad_buf.at[r],
            )

        for copy in copies(r, True):
            copy.start()

    @pl.loop(0, count)
    def _(r):
        for copy in copies(r, True):
            copy.wait()


def attend(slots, named, queries, grads, kv, live, part, before):
    count, _, width = queries.shape
    keys = kv.shape[2]
    heads = width // HD
    table = jnp.concatenate([slots, named]).astype(jnp.int32)
    inside = pl.BlockSpec(memory_space=pltpu.VMEM)
    outside = pl.BlockSpec(memory_space=pl.ANY)
    in_specs = [pl.BlockSpec(memory_space=pltpu.SMEM), inside, inside, inside, outside]
    operands = [table, queries, grads, live, kv]
    aliases = {}
    if before is not None:
        in_specs.append(outside)
        operands.append(before)
        aliases = {len(operands) - 1: 1}
    return pl.pallas_call(
        functools.partial(attend_kernel, part),
        in_specs=in_specs,
        out_specs=[inside, outside],
        out_shape=[
            jax.ShapeDtypeStruct(queries.shape, BF16),
            jax.ShapeDtypeStruct(kv.shape, BF16),
        ],
        scratch_shapes=[
            pltpu.VMEM((count, 2, keys, width), BF16),
            pltpu.VMEM((count, 2, keys, width), BF16),
            pltpu.SemaphoreType.DMA((count, 4)),
            pltpu.SemaphoreType.DMA((count, 4)),
        ],
        input_output_aliases=aliases,
        compiler_params=pltpu.CompilerParams(vmem_limit_bytes=54 * 1024 * 1024),
        cost_estimate=pl.CostEstimate(
            flops=count * heads * 5 * 2 * SPAN * keys * HD * 4,
            bytes_accessed=count * 4 * keys * width * 2,
            transcendentals=count * heads * SPAN * keys,
        ),
    )(*operands)


def total_kernel(tile, *refs):
    out_ref, buf, sem = refs[-3:]
    copies = []
    for n in range(sem.shape[0]):
        some = pl.ds(n * tile, tile)
        buf[some] = total([ref[some] for ref in refs[:-3]])
        copies.append(pltpu.make_async_copy(buf.at[some], out_ref.at[some], sem.at[n]))
        copies[-1].start()
    for copy in copies:
        copy.wait()


def summed(values):
    rows, columns = values[0].shape
    tile = min(64, rows)
    return pl.pallas_call(
        functools.partial(total_kernel, tile),
        in_specs=[pl.BlockSpec(memory_space=pltpu.VMEM)] * len(values),
        out_specs=pl.BlockSpec(memory_space=pl.ANY),
        out_shape=jax.ShapeDtypeStruct((rows, columns), F32),
        scratch_shapes=[
            pltpu.VMEM((rows, columns), F32),
            pltpu.SemaphoreType.DMA((rows // tile,)),
        ],
        compiler_params=pltpu.CompilerParams(vmem_limit_bytes=16 * 1024 * 1024),
        cost_estimate=pl.CostEstimate(
            flops=len(values) * rows * columns,
            bytes_accessed=(2 * len(values) + 4) * rows * columns,
            transcendentals=0,
        ),
    )(*values)


def assemble_kernel(depth, core_ref, own_ref, up_ref, down_ref, arrived_ref, out_ref):
    kept = own_ref[...].astype(F32) + up_ref[...].astype(F32) + down_ref[...].astype(F32)
    kept = kept.astype(BF16)
    for p in range(kept.shape[1] // depth):
        columns = slice(p * depth, (p + 1) * depth)
        mine, other = 2 * p + core_ref[0], 2 * p + 1 - core_ref[0]
        out_ref[:, pl.ds(pl.multiple_of(mine * depth, depth), depth)] = kept[:, columns]
        out_ref[:, pl.ds(pl.multiple_of(other * depth, depth), depth)] = arrived_ref[:, columns]


def assemble(core, own, up, down, arrived, depth):
    rows, columns = arrived.shape
    tile = min(64, rows)
    block = pl.BlockSpec((tile, columns), lambda r: (r, 0))
    return pl.pallas_call(
        functools.partial(assemble_kernel, depth),
        grid=(rows // tile,),
        in_specs=[pl.BlockSpec(memory_space=pltpu.SMEM)] + [block] * 4,
        out_specs=pl.BlockSpec((tile, 2 * columns), lambda r: (r, 0)),
        out_shape=jax.ShapeDtypeStruct((rows, 2 * columns), BF16),
        compiler_params=pltpu.CompilerParams(vmem_limit_bytes=16 * 1024 * 1024),
        cost_estimate=pl.CostEstimate(
            flops=2 * rows * columns, bytes_accessed=12 * rows * columns, transcendentals=0
        ),
    )(jnp.reshape(core, (1,)).astype(jnp.int32), own, up, down, arrived)


def on_device(span_act, q_weight, out_grad, neighbour_kv, neighbour_ids, owner):
    rows, width = out_grad.shape
    depth = q_weight.shape[0]
    seq_count = lax.axis_size("seq")
    dp_count = lax.axis_size("dp")
    tensor_count = lax.axis_size("tensor")
    couples = dp_count // 2
    seq_at = lax.axis_index("seq")
    dp_at = lax.axis_index("dp")
    tensor_at = lax.axis_index("tensor")
    core = dp_at % 2
    spans = rows // SPAN
    capacity = neighbour_kv.shape[0]
    pairs = capacity // seq_count
    whole_blocks = pairs == spans
    per = span_act.shape[1] // depth // 2
    half = width // 2
    opposite = tensor_count // 2

    raw = gather_ring(span_act, "tensor", tensor_count, opposite - 1)
    along_seq = gather_ring(q_weight, "seq", seq_count)
    along_dp = gather_ring(q_weight, "dp", couples)

    groups = owner.reshape(seq_count, dp_count, spans)
    groups = lax.dynamic_index_in_dim(groups, dp_at, 1, keepdims=False)
    mine = lax.dynamic_index_in_dim(groups, seq_at, 0, keepdims=False)

    def order(group, target):
        names = group == target
        at = jnp.arange(spans)
        ahead = (names[None, :] & ~names[:, None]) | (
            (names[None, :] == names[:, None]) & (at[None, :] < at[:, None])
        )
        return jnp.sum(ahead.astype(jnp.int32), axis=1), names.astype(jnp.int32)

    def message(target):
        place, names = order(mine, target)
        hit = place[None, :] == jnp.arange(pairs)[:, None]
        return hit & (names[None, :] == 1)

    def to_owner(value, step):
        value = value.reshape(spans, SPAN, -1)
        if not whole_blocks:
            hit = message((seq_at + step) % seq_count)
            value = jnp.sum(
                jnp.where(hit[:, :, None, None], value[None], jnp.zeros((), BF16)), axis=1
            )
        return shift(value, "seq", step) if step else value

    cut = width * 5 // 8 // HD * HD
    up_from, down_from = raw[opposite - 1][:rows // 2], raw[opposite + 1][rows // 2:]
    left_from = [block[:, :cut] for block in along_seq[1:]]
    right_from = [block[:, cut:] for block in along_dp[1:]]
    left_from, right_from, up_from = lax.optimization_barrier((left_from, right_from, up_from))
    corner_left = [gather_ring(block, "dp", couples) for block in left_from]
    corner_right = [gather_ring(block, "seq", seq_count) for block in right_from]
    up = shift(up_from, "tensor", 1)
    down_from = after(down_from, left_from, right_from)

    def columns_of(block, which):
        return jnp.concatenate(
            [
                lax.dynamic_slice(block, (0, (2 * p + which) * depth), (block.shape[0], depth))
                for p in range(per)
            ],
            axis=1,
        )

    near = [k for k in range(tensor_count) if k != opposite]
    others = [raw[k] for k in near]
    others = after(others, down_from)
    others = swap(jnp.concatenate([columns_of(block, 1 - core) for block in others], axis=0))
    grad_out = after(out_grad, left_from, right_from)
    grads = [to_owner(grad_out, step) for step in range(seq_count)]
    down_from, grads, others = lax.optimization_barrier((down_from, grads, others))
    down = shift(down_from, "tensor", -1)
    raw[opposite] = jnp.concatenate([up, down], axis=0)
    others = {k: others[n * rows:(n + 1) * rows] for n, k in enumerate(near)}
    others[opposite] = swap(columns_of(raw[opposite], 1 - core))
    acts = [
        jnp.concatenate([columns_of(raw[k], core), others[k]], axis=0) for k in range(tensor_count)
    ]
    depth_blocks = [(tensor_at - k) % tensor_count for k in range(tensor_count)]
    table = jnp.stack(depth_blocks).astype(jnp.int32)

    def block_at(i, j):
        block = ((seq_at - i) % seq_count) * dp_count + ((dp_at // 2 - j) % couples) * 2
        return block // (2 * per), (block % (2 * per)) // 2

    places = [(i, j) for i in range(seq_count) for j in range(couples)]
    weights = jnp.zeros((tensor_count, per * depth, width), BF16)
    for i, j in places:
        at, inner = block_at(i, j)
        if j == 0:
            pieces = [(along_seq[i], 0)]
        elif i == 0:
            pieces = [(along_dp[j], 0)]
        else:
            pieces = [(corner_left[i - 1][j], 0), (corner_right[j - 1][i], cut)]
        for piece, start in pieces:
            weights = lax.dynamic_update_slice(weights, piece[None], (at, inner * depth, start))

    def from_owner(value, step):
        value = shift(value, "seq", -step) if step else value
        if not whole_blocks:
            hit = message((seq_at + step) % seq_count)
            value = jnp.sum(
                jnp.where(hit[:, :, None, None], value[:, None], jnp.zeros((), BF16)), axis=0
            )
        return value.reshape(rows, -1)

    def slots_of(step):
        group = lax.dynamic_index_in_dim(groups, (seq_at - step) % seq_count, 0, keepdims=False)
        place, names = order(group, seq_at)
        if not whole_blocks:
            place = jnp.arange(pairs)
            names = (place < jnp.sum(names)).astype(jnp.int32)
        return (seq_at - step) % seq_count * pairs + place, names

    live = jnp.broadcast_to((neighbour_ids != 0).astype(BF16)[:, :, None], (capacity, KEYS, HD))
    slots = [slots_of(step) for step in range(seq_count)]

    queries = []
    for part in range(2):
        partial = product(acts, weights, table, part * half, half)
        arrived = swap(partial[rows:])
        queries.append((partial[:rows] + arrived).astype(BF16))
    asked = [[to_owner(value, step) for step in range(seq_count)] for value in queries]
    asked[0][0] = after(asked[0][0], queries[1])

    stacked = jnp.stack(after(acts, queries[1]))

    def act_block(i, j):
        at, inner = block_at(i, j)
        k = (tensor_at - at) % tensor_count
        return lax.dynamic_slice(stacked, (k, 0, inner * depth), (1, 2 * rows, depth))[0]

    def weight_product(i, j, grad):
        found = dot(act_block(i, j), grad, ((0,), (0,)))
        return lax.optimization_barrier(found.astype(BF16))

    kv_grad = None
    both_grads, corners = [], []
    corner_places = [(i, j) for i in range(1, seq_count) for j in range(1, couples)]
    for part in range(2):
        answers = []
        for step in range(seq_count):
            answer, kv_grad = attend(
                *slots[step],
                asked[part][step],
                grads[step],
                neighbour_kv,
                live,
                part,
                kv_grad,
            )
            answers.append(from_owner(answer, step))
        if part:
            answers[-1] = after(answers[-1], corners[0][corner_places[-1]])
        grad = sum(answers[1:], answers[0])
        both_grads.append(jnp.concatenate([grad, swap(grad)], axis=0))
        if part == 0:
            corners.append({at: weight_product(*at, both_grads[0]) for at in corner_places[::-1]})
    both_grad = jnp.concatenate(both_grads, axis=1)

    def act_product(k):
        block = lax.dynamic_index_in_dim(weights, depth_blocks[k], 0, keepdims=False)
        return lax.optimization_barrier(dot(both_grad, block, ((1,), (1,))).astype(BF16))

    far = act_product(opposite)
    up, down = shift(far[:rows], "tensor", 1), shift(far[rows:], "tensor", -1)

    late_grad = after(both_grads[1], far)
    corners.append({at: weight_product(*at, late_grad) for at in corner_places[::-1]})
    left = [
        reduce_rings([([None] + [corners[0][i, j] for j in range(1, couples)], True)], "dp")[0][1:]
        for i in range(1, seq_count)
    ]
    right = [
        reduce_rings([([None] + [corners[1][i, j] for i in range(1, seq_count)], True)], "seq")[0][1:]
        for j in range(1, couples)
    ]
    act_parts = {k: act_product(k) for k in range(tensor_count) if k != opposite}
    own = weight_product(0, 0, both_grad)
    beside_seq = [weight_product(i, 0, both_grad) for i in range(1, seq_count)]
    beside_dp = [weight_product(0, j, both_grad) for j in range(1, couples)]
    up, down, left, right, act_parts, own, beside_seq, beside_dp = lax.optimization_barrier(
        (up, down, left, right, act_parts, own, beside_seq, beside_dp)
    )

    beside_seq = [
        lax.dynamic_update_slice(block, total([block[:, :half]] + came).astype(BF16), (0, 0))
        for block, came in zip(beside_seq, left)
    ]
    from_seq = reduce_rings([([None] + beside_seq, True)], "seq")[0][1:]
    for m in range(opposite - 1, 0, -1):
        block = act_parts[tensor_count - m]
        if up.shape[0] == rows:
            up = lax.dynamic_update_slice(block, total([block[:rows], up]).astype(BF16), (0, 0))
        else:
            up = total([block, up]).astype(BF16)
        block = act_parts[m]
        if down.shape[0] == rows:
            down = lax.dynamic_update_slice(
                block, total([block[rows:], down]).astype(BF16), (rows, 0)
            )
        else:
            down = total([block, down]).astype(BF16)
        up, down = shift(up, "tensor", 1), shift(down, "tensor", -1)
    beside_dp = [
        lax.dynamic_update_slice(block, total([block[:, half:]] + came).astype(BF16), (0, half))
        for block, came in zip(beside_dp, right)
    ]
    from_dp = reduce_rings([([None] + beside_dp, True)], "dp")[0][1:]

    arrived = swap(total([part[rows:] for part in (act_parts[0], up, down)]).astype(BF16))
    act_grad = assemble(core, act_parts[0], up, down, arrived, depth)
    weight_grad = summed([own] + from_seq + from_dp)
    return (act_grad, weight_grad, kv_grad)


def solution(mesh):
    in_specs = (
        P(("seq", "dp"), "tensor"),
        P(("seq", "dp"), "tensor"),
        P(("seq", "dp"), "tensor"),
        P(("seq", "dp"), None, None, "tensor"),
        P(("seq", "dp"), None),
        P(),
    )
    out_specs = (
        P(("seq", "dp"), "tensor"),
        P(("seq", "dp"), "tensor"),
        P(("seq", "dp"), None, None, "tensor"),
    )
    return jax.shard_map(
        on_device, mesh=mesh, in_specs=in_specs, out_specs=out_specs, check_vma=False
    )
```

```python
import functools

import jax
import jax.numpy as jnp
from jax import lax
from jax.experimental import pallas as pl
from jax.experimental.pallas import tpu as pltpu
from jax.sharding import PartitionSpec as P

HD = 128
SPAN = 64
KEYS = 256
F32 = jnp.float32
BF16 = jnp.bfloat16


def dot(a, b, contract):
    return lax.dot_general(a, b, (contract, ((), ())), preferred_element_type=F32)


def shift(value, axis, step=1):
    stride = 2 if axis == "dp" else 1
    size = lax.axis_size(axis)
    return lax.ppermute(value, axis, [(i, (i + step * stride) % size) for i in range(size)])


def swap(value):
    return lax.ppermute(value, "dp", [(i, i ^ 1) for i in range(lax.axis_size("dp"))])


def after(value, *others):
    return lax.optimization_barrier((value, *others))[0]


def reaches(size, far_up):
    up = size // 2 if far_up else (size - 1) // 2
    return up, size - 1 - up


def gather_ring(block, axis, size, rounds=None):
    blocks = [block] + [None] * (size - 1)
    for m in range(1, (size // 2 if rounds is None else rounds) + 1):
        came = {}
        for sign, count in zip((1, -1), reaches(size, True)):
            if m <= count:
                came[(sign * m) % size] = shift(blocks[(sign * (m - 1)) % size], axis, sign)
        for k, value in zip(came, lax.optimization_barrier(tuple(came.values()))):
            blocks[k] = value
    return blocks


def reduce_rings(streams, axis):
    size = len(streams[0][0])
    found = [[blocks[0]] for blocks, _ in streams]
    came = {}
    for m in range(1, size // 2 + 1):
        sent = {}
        for s, (blocks, far_up) in enumerate(streams):
            for sign, count in zip((1, -1), reaches(size, far_up)):
                if m <= count:
                    block = blocks[(-sign * (count - m + 1)) % size]
                    if m > 1:
                        block = came[s, sign].astype(F32) + block.astype(F32)
                    sent[s, sign] = shift(block.astype(BF16), axis, sign)
        came = dict(zip(sent, lax.optimization_barrier(tuple(sent.values()))))
        for (s, sign), block in came.items():
            if m == reaches(size, streams[s][1])[0 if sign == 1 else 1]:
                found[s].append(block)
    return found


def total(values):
    return functools.reduce(lambda a, b: a + b, [value.astype(F32) for value in values])


def product_kernel(count, start, table_ref, *refs):
    blocks, weight_ref, out_ref = refs[:count], refs[count], refs[count + 1]
    tile = min(256, out_ref.shape[1])
    for at in range(0, out_ref.shape[1], tile):
        total = None
        for k in range(count):
            weight = weight_ref[table_ref[k], :, start + at:start + at + tile]
            part = dot(blocks[k][...], weight, ((1,), (0,)))
            total = part if total is None else total + part
        out_ref[:, at:at + tile] = total


def product(blocks, weights, table, start, width):
    count, (rows, depth) = len(blocks), blocks[0].shape
    return pl.pallas_call(
        functools.partial(product_kernel, count, start),
        out_shape=jax.ShapeDtypeStruct((rows, width), F32),
        in_specs=[pl.BlockSpec(memory_space=pltpu.SMEM)]
        + [pl.BlockSpec(memory_space=pltpu.VMEM)] * (count + 1),
        out_specs=pl.BlockSpec(memory_space=pltpu.VMEM),
        compiler_params=pltpu.CompilerParams(vmem_limit_bytes=16 * 1024 * 1024),
        cost_estimate=pl.CostEstimate(
            flops=2 * rows * count * depth * width,
            bytes_accessed=2 * count * depth * (rows + width) + 4 * rows * width,
            transcendentals=0,
        ),
    )(table, *blocks, weights)


def attend_block(q_ref, g_ref, kv_ref, live_ref, dq_ref, grad_ref):
    pairs = q_ref.shape[-1] // HD // 2
    scale = HD ** (-0.5)
    live = live_ref[...] > 0.5
    zero = jnp.zeros((SPAN, HD), BF16)

    def diagonal(ref, start):
        one = ref[:, start:start + HD]
        two = ref[:, start + HD:start + 2 * HD]
        return jnp.concatenate(
            [jnp.concatenate([one, zero], axis=1), jnp.concatenate([zero, two], axis=1)], axis=0
        )

    def first(pair):
        start = pair * 2 * HD
        columns = slice(start, start + 2 * HD)
        scores = dot(kv_ref[0, :, columns], diagonal(q_ref, start), ((1,), (1,)))
        prob_grad = dot(kv_ref[1, :, columns], diagonal(g_ref, start), ((1,), (1,)))
        return scores, prob_grad

    ahead = first(0)
    for pair in range(pairs):
        scores, prob_grad = ahead
        if pair + 1 < pairs:
            ahead = first(pair + 1)
        start = pair * 2 * HD
        columns = slice(start, start + 2 * HD)
        scores = jnp.where(live, scores * scale, -1e30)
        expo = jnp.exp(scores - jnp.max(scores, axis=0, keepdims=True))
        probs = expo * (1.0 / jnp.sum(expo, axis=0, keepdims=True))
        center = jnp.sum(probs * prob_grad, axis=0, keepdims=True)
        score_grad = (probs * (prob_grad - center) * scale).astype(BF16)
        value_grad = dot(probs.astype(BF16), diagonal(g_ref, start), ((1,), (0,)))
        key_grad = dot(score_grad, diagonal(q_ref, start), ((1,), (0,)))
        both = dot(score_grad, kv_ref[0, :, columns], ((0,), (0,)))
        grad_ref[1, :, columns] = value_grad.astype(BF16)
        grad_ref[0, :, columns] = key_grad.astype(BF16)
        dq_ref[:, columns] = jnp.concatenate([both[:SPAN, :HD], both[SPAN:, HD:]], axis=1).astype(
            BF16
        )


def attend_kernel(table_ref, q_ref, g_ref, live_ref, kv_ref, *rest):
    dq_ref, grad_ref = rest[-2:]
    named = table_ref[pl.num_programs(0) + pl.program_id(0)]

    @pl.when(named == 0)
    def _():
        dq_ref[...] = jnp.zeros_like(dq_ref)
        grad_ref[...] = jnp.zeros_like(grad_ref)

    @pl.when(named != 0)
    def _():
        refs = (q_ref, g_ref, kv_ref, live_ref, dq_ref, grad_ref)
        attend_block(*(ref.at[0] for ref in refs))


def attend(place, named, source, queries, grads, kv, live, part, before):
    count, _, width = queries.shape
    capacity, keys, _ = live.shape
    heads = width // HD
    table = jnp.concatenate([place, named, source * count + place]).astype(jnp.int32)
    span_block = pl.BlockSpec((1, SPAN, width), lambda r, t: (r, 0, 0))
    part_block = pl.BlockSpec((1, SPAN, width), lambda r, t: (r, 0, part))
    live_block = pl.BlockSpec((1, keys, HD), lambda r, t: (t[2 * count + r], 0, 0))
    kv_block = pl.BlockSpec((1, 2, keys, width), lambda r, t: (t[r], 0, 0, 0))
    grad_block = pl.BlockSpec((1, 2, keys, width), lambda r, t: (t[2 * count + r], 0, 0, part))
    in_specs = [span_block, part_block, live_block, kv_block]
    operands = [table, queries, grads, live, kv]
    aliases = {}
    if before is not None:
        in_specs.append(pl.BlockSpec(memory_space=pl.ANY))
        operands.append(before)
        aliases = {len(operands) - 1: 1}
    return pl.pallas_call(
        attend_kernel,
        grid_spec=pltpu.PrefetchScalarGridSpec(
            num_scalar_prefetch=1,
            grid=(count,),
            in_specs=in_specs,
            out_specs=[span_block, grad_block],
        ),
        out_shape=[
            jax.ShapeDtypeStruct(queries.shape, BF16),
            jax.ShapeDtypeStruct((capacity, 2, keys, 2 * width), BF16),
        ],
        input_output_aliases=aliases,
        compiler_params=pltpu.CompilerParams(vmem_limit_bytes=12 * 1024 * 1024),
        cost_estimate=pl.CostEstimate(
            flops=count * heads * 5 * 2 * SPAN * keys * HD * 4,
            bytes_accessed=count * 4 * keys * width * 2,
            transcendentals=count * heads * SPAN * keys,
        ),
    )(*operands)


def stage_kernel(source_ref, kv_ref, left_ref, right_ref):
    width = left_ref.shape[-1]
    left_ref[...] = kv_ref[:, :, :, :width]
    right_ref[...] = kv_ref[:, :, :, width:]


def stage(kv, source, count):
    _, _, keys, width = kv.shape
    half_block = pl.BlockSpec((1, 2, keys, width // 2), lambda r, t: (r, 0, 0, 0))
    half_shape = jax.ShapeDtypeStruct((count, 2, keys, width // 2), kv.dtype)
    return pl.pallas_call(
        stage_kernel,
        grid_spec=pltpu.PrefetchScalarGridSpec(
            num_scalar_prefetch=1,
            grid=(count,),
            in_specs=[
                pl.BlockSpec((1, 2, keys, width), lambda r, t: (t[0] * count + r, 0, 0, 0))
            ],
            out_specs=[half_block, half_block],
        ),
        out_shape=[half_shape, half_shape],
        compiler_params=pltpu.CompilerParams(vmem_limit_bytes=12 * 1024 * 1024),
        cost_estimate=pl.CostEstimate(
            flops=0, bytes_accessed=8 * count * keys * width, transcendentals=0
        ),
    )(jnp.reshape(source, (1,)).astype(jnp.int32), kv)


def total_kernel(tile, *refs):
    out_ref, buf, sem = refs[-3:]
    copies = []
    for n in range(sem.shape[0]):
        some = pl.ds(n * tile, tile)
        buf[some] = total([ref[some] for ref in refs[:-3]])
        copies.append(pltpu.make_async_copy(buf.at[some], out_ref.at[some], sem.at[n]))
        copies[-1].start()
    for copy in copies:
        copy.wait()


def summed(values):
    rows, columns = values[0].shape
    tile = min(64, rows)
    return pl.pallas_call(
        functools.partial(total_kernel, tile),
        in_specs=[pl.BlockSpec(memory_space=pltpu.VMEM)] * len(values),
        out_specs=pl.BlockSpec(memory_space=pl.ANY),
        out_shape=jax.ShapeDtypeStruct((rows, columns), F32),
        scratch_shapes=[
            pltpu.VMEM((rows, columns), F32),
            pltpu.SemaphoreType.DMA((rows // tile,)),
        ],
        compiler_params=pltpu.CompilerParams(vmem_limit_bytes=16 * 1024 * 1024),
        cost_estimate=pl.CostEstimate(
            flops=len(values) * rows * columns,
            bytes_accessed=(2 * len(values) + 4) * rows * columns,
            transcendentals=0,
        ),
    )(*values)


def assemble_kernel(depth, core_ref, own_ref, up_ref, down_ref, arrived_ref, out_ref):
    kept = own_ref[...].astype(F32) + up_ref[...].astype(F32) + down_ref[...].astype(F32)
    kept = kept.astype(BF16)
    for p in range(kept.shape[1] // depth):
        columns = slice(p * depth, (p + 1) * depth)
        mine, other = 2 * p + core_ref[0], 2 * p + 1 - core_ref[0]
        out_ref[:, pl.ds(pl.multiple_of(mine * depth, depth), depth)] = kept[:, columns]
        out_ref[:, pl.ds(pl.multiple_of(other * depth, depth), depth)] = arrived_ref[:, columns]


def assemble(core, own, up, down, arrived, depth):
    rows, columns = arrived.shape
    tile = min(64, rows)
    block = pl.BlockSpec((tile, columns), lambda r: (r, 0))
    return pl.pallas_call(
        functools.partial(assemble_kernel, depth),
        grid=(rows // tile,),
        in_specs=[pl.BlockSpec(memory_space=pltpu.SMEM)] + [block] * 4,
        out_specs=pl.BlockSpec((tile, 2 * columns), lambda r: (r, 0)),
        out_shape=jax.ShapeDtypeStruct((rows, 2 * columns), BF16),
        compiler_params=pltpu.CompilerParams(vmem_limit_bytes=16 * 1024 * 1024),
        cost_estimate=pl.CostEstimate(
            flops=2 * rows * columns, bytes_accessed=12 * rows * columns, transcendentals=0
        ),
    )(jnp.reshape(core, (1,)).astype(jnp.int32), own, up, down, arrived)


def on_device(span_act, q_weight, out_grad, neighbour_kv, neighbour_ids, owner):
    rows, width = out_grad.shape
    depth = q_weight.shape[0]
    seq_count = lax.axis_size("seq")
    dp_count = lax.axis_size("dp")
    tensor_count = lax.axis_size("tensor")
    couples = dp_count // 2
    seq_at = lax.axis_index("seq")
    dp_at = lax.axis_index("dp")
    tensor_at = lax.axis_index("tensor")
    core = dp_at % 2
    spans = rows // SPAN
    capacity = neighbour_kv.shape[0]
    pairs = capacity // seq_count
    whole_blocks = pairs == spans
    per = span_act.shape[1] // depth // 2
    half = width // 2
    opposite = tensor_count // 2

    raw = gather_ring(span_act, "tensor", tensor_count, opposite - 1)
    along_seq = gather_ring(q_weight, "seq", seq_count)
    along_dp = gather_ring(q_weight, "dp", couples)

    groups = owner.reshape(seq_count, dp_count, spans)
    groups = lax.dynamic_index_in_dim(groups, dp_at, 1, keepdims=False)
    mine = lax.dynamic_index_in_dim(groups, seq_at, 0, keepdims=False)

    def order(group, target):
        names = group == target
        at = jnp.arange(spans)
        ahead = (names[None, :] & ~names[:, None]) | (
            (names[None, :] == names[:, None]) & (at[None, :] < at[:, None])
        )
        return jnp.sum(ahead.astype(jnp.int32), axis=1), names.astype(jnp.int32)

    def message(target):
        place, names = order(mine, target)
        hit = place[None, :] == jnp.arange(pairs)[:, None]
        return hit & (names[None, :] == 1)

    def to_owner(value, step):
        value = value.reshape(spans, SPAN, -1)
        if not whole_blocks:
            hit = message((seq_at + step) % seq_count)
            value = jnp.sum(
                jnp.where(hit[:, :, None, None], value[None], jnp.zeros((), BF16)), axis=1
            )
        return shift(value, "seq", step) if step else value

    sources = [(seq_at - step) % seq_count for step in range(seq_count)]
    staged = [stage(neighbour_kv, source, pairs) for source in sources]
    near = [k for k in range(tensor_count) if k != opposite]
    raw, along_seq, along_dp, staged, grad_out = lax.optimization_barrier(
        ([raw[k] for k in near], along_seq, along_dp, staged, out_grad)
    )
    raw = dict(zip(near, raw))

    cut = width * 5 // 8 // HD * HD
    left_from = [block[:, :cut] for block in along_seq[1:]]
    right_from = [block[:, cut:] for block in along_dp[1:]]
    left_from, right_from = lax.optimization_barrier((left_from, right_from))
    corner_left = [gather_ring(block, "dp", couples) for block in left_from]
    corner_right = [gather_ring(block, "seq", seq_count) for block in right_from]
    grads = [to_owner(grad_out, step) for step in range(seq_count)]
    up_from, down_from = raw[opposite - 1][:rows // 2], raw[opposite + 1][rows // 2:]
    up_from, down_from = lax.optimization_barrier((up_from, down_from, left_from, right_from))[:2]
    raw[opposite] = jnp.concatenate(
        [shift(up_from, "tensor", 1), shift(down_from, "tensor", -1)], axis=0
    )

    def columns_of(block, which):
        return jnp.concatenate(
            [
                lax.dynamic_slice(block, (0, (2 * p + which) * depth), (block.shape[0], depth))
                for p in range(per)
            ],
            axis=1,
        )

    others = lax.optimization_barrier(([raw[k] for k in near], down_from, grads))[0]
    others = swap(jnp.concatenate([columns_of(block, 1 - core) for block in others], axis=0))
    others = {k: others[n * rows:(n + 1) * rows] for n, k in enumerate(near)}
    others[opposite] = swap(columns_of(raw[opposite], 1 - core))
    acts = [
        jnp.concatenate([columns_of(raw[k], core), others[k]], axis=0) for k in range(tensor_count)
    ]
    depth_blocks = [(tensor_at - k) % tensor_count for k in range(tensor_count)]
    table = jnp.stack(depth_blocks).astype(jnp.int32)

    def block_at(i, j):
        block = ((seq_at - i) % seq_count) * dp_count + ((dp_at // 2 - j) % couples) * 2
        return block // (2 * per), (block % (2 * per)) // 2

    places = [(i, j) for i in range(seq_count) for j in range(couples)]
    weights = jnp.zeros((tensor_count, per * depth, width), BF16)
    for i, j in places:
        at, inner = block_at(i, j)
        if j == 0:
            pieces = [(along_seq[i], 0)]
        elif i == 0:
            pieces = [(along_dp[j], 0)]
        else:
            pieces = [(corner_left[i - 1][j], 0), (corner_right[j - 1][i], cut)]
        for piece, start in pieces:
            weights = lax.dynamic_update_slice(weights, piece[None], (at, inner * depth, start))

    def from_owner(value, step):
        value = shift(value, "seq", -step) if step else value
        if not whole_blocks:
            hit = message((seq_at + step) % seq_count)
            value = jnp.sum(
                jnp.where(hit[:, :, None, None], value[:, None], jnp.zeros((), BF16)), axis=0
            )
        return value.reshape(rows, -1)

    def slots_of(step):
        group = lax.dynamic_index_in_dim(groups, sources[step], 0, keepdims=False)
        place, names = order(group, seq_at)
        if not whole_blocks:
            place = jnp.arange(pairs)
            names = (place < jnp.sum(names)).astype(jnp.int32)
        return place, names, sources[step]

    live = jnp.broadcast_to((neighbour_ids != 0).astype(F32)[:, :, None], (capacity, KEYS, HD))
    slots = [slots_of(step) for step in range(seq_count)]

    queries = []
    for part in range(2):
        partial = product(acts, weights, table, part * half, half)
        arrived = swap(partial[rows:])
        queries.append((partial[:rows] + arrived).astype(BF16))
    asked = [[to_owner(value, step) for step in range(seq_count)] for value in queries]
    asked[0][0] = after(asked[0][0], queries[1])

    stacked = jnp.stack(after(acts, queries[1]))

    def act_block(i, j):
        at, inner = block_at(i, j)
        k = (tensor_at - at) % tensor_count
        return lax.dynamic_slice(stacked, (k, 0, inner * depth), (1, 2 * rows, depth))[0]

    def weight_product(i, j, grad):
        found = dot(act_block(i, j), grad, ((0,), (0,)))
        return lax.optimization_barrier(found.astype(BF16))

    kv_grad = None
    answers = [[None] * seq_count for _ in range(2)]
    calls = [(0, 0), (1, 0)] + [(part, step) for part in range(2) for step in range(1, seq_count)]
    for part, step in calls:
        answer, kv_grad = attend(
            *slots[step],
            asked[part][step],
            grads[step],
            staged[step][part],
            live,
            part,
            kv_grad,
        )
        answers[part][step] = from_owner(answer, step)

    far_weights = lax.dynamic_index_in_dim(weights, depth_blocks[opposite], 0, keepdims=False)
    far_weights = after(far_weights, queries[1])
    both_grads, corners = [], []
    corner_places = [(i, j) for i in range(1, seq_count) for j in range(1, couples)]
    for part in range(2):
        if part:
            answers[1][-1] = after(answers[1][-1], corners[0][corner_places[-1]])
        grad = sum(answers[part][1:], answers[part][0])
        both_grads.append(jnp.concatenate([grad, swap(grad)], axis=0))
        if part == 0:
            corners.append({at: weight_product(*at, both_grads[0]) for at in corner_places[::-1]})
    both_grad = jnp.concatenate(both_grads, axis=1)

    def act_product(k, block=None):
        if block is None:
            block = lax.dynamic_index_in_dim(weights, depth_blocks[k], 0, keepdims=False)
        return lax.optimization_barrier(dot(both_grad, block, ((1,), (1,))).astype(BF16))

    far = act_product(opposite, far_weights)
    up, down = shift(far[:rows], "tensor", 1), shift(far[rows:], "tensor", -1)

    late_grad = after(both_grads[1], far)
    corners.append({at: weight_product(*at, late_grad) for at in corner_places[::-1]})
    left = [
        reduce_rings([([None] + [corners[0][i, j] for j in range(1, couples)], True)], "dp")[0][1:]
        for i in range(1, seq_count)
    ]
    right = [
        reduce_rings([([None] + [corners[1][i, j] for i in range(1, seq_count)], True)], "seq")[0][1:]
        for j in range(1, couples)
    ]
    act_parts = {k: act_product(k) for k in range(tensor_count) if k != opposite}
    own = weight_product(0, 0, both_grad)
    beside_seq = [weight_product(i, 0, both_grad) for i in range(1, seq_count)]
    beside_dp = [weight_product(0, j, both_grad) for j in range(1, couples)]
    up, down, left, right, act_parts, own, beside_seq, beside_dp = lax.optimization_barrier(
        (up, down, left, right, act_parts, own, beside_seq, beside_dp)
    )

    beside_seq = [
        lax.dynamic_update_slice(block, total([block[:, :half]] + came).astype(BF16), (0, 0))
        for block, came in zip(beside_seq, left)
    ]
    from_seq = reduce_rings([([None] + beside_seq, True)], "seq")[0][1:]
    for m in range(opposite - 1, 0, -1):
        block = act_parts[tensor_count - m]
        if up.shape[0] == rows:
            up = lax.dynamic_update_slice(block, total([block[:rows], up]).astype(BF16), (0, 0))
        else:
            up = total([block, up]).astype(BF16)
        block = act_parts[m]
        if down.shape[0] == rows:
            down = lax.dynamic_update_slice(
                block, total([block[rows:], down]).astype(BF16), (rows, 0)
            )
        else:
            down = total([block, down]).astype(BF16)
        up, down = shift(up, "tensor", 1), shift(down, "tensor", -1)
    beside_dp = [
        lax.dynamic_update_slice(block, total([block[:, half:]] + came).astype(BF16), (0, half))
        for block, came in zip(beside_dp, right)
    ]
    from_dp = reduce_rings([([None] + beside_dp, True)], "dp")[0][1:]

    arrived = swap(total([part[rows:] for part in (act_parts[0], up, down)]).astype(BF16))
    act_grad = assemble(core, act_parts[0], up, down, arrived, depth)
    weight_grad = summed([own] + from_seq + from_dp)
    return (act_grad, weight_grad, kv_grad)


def solution(mesh):
    in_specs = (
        P(("seq", "dp"), "tensor"),
        P(("seq", "dp"), "tensor"),
        P(("seq", "dp"), "tensor"),
        P(("seq", "dp"), None, None, "tensor"),
        P(("seq", "dp"), None),
        P(),
    )
    out_specs = (
        P(("seq", "dp"), "tensor"),
        P(("seq", "dp"), "tensor"),
        P(("seq", "dp"), None, None, "tensor"),
    )
    return jax.shard_map(
        on_device, mesh=mesh, in_specs=in_specs, out_specs=out_specs, check_vma=False
    )
```

```python
import functools

import jax
import jax.numpy as jnp
from jax import lax
from jax.experimental import pallas as pl
from jax.experimental.pallas import tpu as pltpu
from jax.sharding import PartitionSpec as P

HD = 128
SPAN = 64
KEYS = 256
F32 = jnp.float32
BF16 = jnp.bfloat16


def dot(a, b, contract):
    return lax.dot_general(a, b, (contract, ((), ())), preferred_element_type=F32)


def shift(value, axis, step=1):
    stride = 2 if axis == "dp" else 1
    size = lax.axis_size(axis)
    return lax.ppermute(value, axis, [(i, (i + step * stride) % size) for i in range(size)])


def swap(value):
    return lax.ppermute(value, "dp", [(i, i ^ 1) for i in range(lax.axis_size("dp"))])


def after(value, *others):
    return lax.optimization_barrier((value, *others))[0]


def reaches(size, far_up):
    up = size // 2 if far_up else (size - 1) // 2
    return up, size - 1 - up


def gather_ring(block, axis, size, rounds=None):
    blocks = [block] + [None] * (size - 1)
    for m in range(1, (size // 2 if rounds is None else rounds) + 1):
        came = {}
        for sign, count in zip((1, -1), reaches(size, True)):
            if m <= count:
                came[(sign * m) % size] = shift(blocks[(sign * (m - 1)) % size], axis, sign)
        for k, value in zip(came, lax.optimization_barrier(tuple(came.values()))):
            blocks[k] = value
    return blocks


def reduce_rings(streams, axis):
    size = len(streams[0][0])
    found = [[blocks[0]] for blocks, _ in streams]
    came = {}
    for m in range(1, size // 2 + 1):
        sent = {}
        for s, (blocks, far_up) in enumerate(streams):
            for sign, count in zip((1, -1), reaches(size, far_up)):
                if m <= count:
                    block = blocks[(-sign * (count - m + 1)) % size]
                    if m > 1:
                        block = came[s, sign].astype(F32) + block.astype(F32)
                    sent[s, sign] = shift(block.astype(BF16), axis, sign)
        came = dict(zip(sent, lax.optimization_barrier(tuple(sent.values()))))
        for (s, sign), block in came.items():
            if m == reaches(size, streams[s][1])[0 if sign == 1 else 1]:
                found[s].append(block)
    return found


def total(values):
    return functools.reduce(lambda a, b: a + b, [value.astype(F32) for value in values])


def product_kernel(count, start, table_ref, *refs):
    blocks, weight_ref, out_ref = refs[:count], refs[count], refs[count + 1]
    tile = min(256, out_ref.shape[1])
    for at in range(0, out_ref.shape[1], tile):
        total = None
        for k in range(count):
            weight = weight_ref[table_ref[k], :, start + at:start + at + tile]
            part = dot(blocks[k][...], weight, ((1,), (0,)))
            total = part if total is None else total + part
        out_ref[:, at:at + tile] = total


def product(blocks, weights, table, start, width):
    count, (rows, depth) = len(blocks), blocks[0].shape
    return pl.pallas_call(
        functools.partial(product_kernel, count, start),
        out_shape=jax.ShapeDtypeStruct((rows, width), F32),
        in_specs=[pl.BlockSpec(memory_space=pltpu.SMEM)]
        + [pl.BlockSpec(memory_space=pltpu.VMEM)] * (count + 1),
        out_specs=pl.BlockSpec(memory_space=pltpu.VMEM),
        compiler_params=pltpu.CompilerParams(vmem_limit_bytes=16 * 1024 * 1024),
        cost_estimate=pl.CostEstimate(
            flops=2 * rows * count * depth * width,
            bytes_accessed=2 * count * depth * (rows + width) + 4 * rows * width,
            transcendentals=0,
        ),
    )(table, *blocks, weights)


def attend_block(q_ref, g_ref, kv_ref, live_ref, dq_ref, grad_ref):
    pairs = q_ref.shape[-1] // HD // 2
    scale = HD ** (-0.5)
    live = live_ref[...] > 0.5
    zero = jnp.zeros((SPAN, HD), BF16)

    def diagonal(ref, start):
        one = ref[:, start:start + HD]
        two = ref[:, start + HD:start + 2 * HD]
        return jnp.concatenate(
            [jnp.concatenate([one, zero], axis=1), jnp.concatenate([zero, two], axis=1)], axis=0
        )

    def first(pair):
        start = pair * 2 * HD
        columns = slice(start, start + 2 * HD)
        scores = dot(kv_ref[0, :, columns], diagonal(q_ref, start), ((1,), (1,)))
        prob_grad = dot(kv_ref[1, :, columns], diagonal(g_ref, start), ((1,), (1,)))
        return scores, prob_grad

    ahead = first(0)
    for pair in range(pairs):
        scores, prob_grad = ahead
        if pair + 1 < pairs:
            ahead = first(pair + 1)
        start = pair * 2 * HD
        columns = slice(start, start + 2 * HD)
        scores = jnp.where(live, scores * scale, -1e30)
        expo = jnp.exp(scores - jnp.max(scores, axis=0, keepdims=True))
        probs = expo * (1.0 / jnp.sum(expo, axis=0, keepdims=True))
        center = jnp.sum(probs * prob_grad, axis=0, keepdims=True)
        score_grad = (probs * (prob_grad - center) * scale).astype(BF16)
        value_grad = dot(probs.astype(BF16), diagonal(g_ref, start), ((1,), (0,)))
        key_grad = dot(score_grad, diagonal(q_ref, start), ((1,), (0,)))
        both = dot(score_grad, kv_ref[0, :, columns], ((0,), (0,)))
        grad_ref[1, :, columns] = value_grad.astype(BF16)
        grad_ref[0, :, columns] = key_grad.astype(BF16)
        dq_ref[:, columns] = jnp.concatenate([both[:SPAN, :HD], both[SPAN:, HD:]], axis=1).astype(
            BF16
        )


def attend_kernel(table_ref, q_ref, g_ref, live_ref, kv_ref, *rest):
    dq_ref, grad_ref = rest[-2:]
    named = table_ref[pl.num_programs(0) + pl.program_id(0)]

    @pl.when(named == 0)
    def _():
        dq_ref[...] = jnp.zeros_like(dq_ref)
        grad_ref[...] = jnp.zeros_like(grad_ref)

    @pl.when(named != 0)
    def _():
        refs = (q_ref, g_ref, kv_ref, live_ref, dq_ref, grad_ref)
        attend_block(*(ref.at[0] for ref in refs))


def attend(place, named, source, queries, grads, kv, live, part, before):
    count, _, width = queries.shape
    capacity, keys, _ = live.shape
    heads = width // HD
    table = jnp.concatenate([place, named, source * count + place]).astype(jnp.int32)
    span_block = pl.BlockSpec((1, SPAN, width), lambda r, t: (r, 0, 0))
    part_block = pl.BlockSpec((1, SPAN, width), lambda r, t: (r, 0, part))
    live_block = pl.BlockSpec((1, keys, HD), lambda r, t: (t[2 * count + r], 0, 0))
    kv_block = pl.BlockSpec((1, 2, keys, width), lambda r, t: (t[r], 0, 0, 0))
    grad_block = pl.BlockSpec((1, 2, keys, width), lambda r, t: (t[2 * count + r], 0, 0, part))
    in_specs = [span_block, part_block, live_block, kv_block]
    operands = [table, queries, grads, live, kv]
    aliases = {}
    if before is not None:
        in_specs.append(pl.BlockSpec(memory_space=pl.ANY))
        operands.append(before)
        aliases = {len(operands) - 1: 1}
    return pl.pallas_call(
        attend_kernel,
        grid_spec=pltpu.PrefetchScalarGridSpec(
            num_scalar_prefetch=1,
            grid=(count,),
            in_specs=in_specs,
            out_specs=[span_block, grad_block],
        ),
        out_shape=[
            jax.ShapeDtypeStruct(queries.shape, BF16),
            jax.ShapeDtypeStruct((capacity, 2, keys, 2 * width), BF16),
        ],
        input_output_aliases=aliases,
        compiler_params=pltpu.CompilerParams(vmem_limit_bytes=12 * 1024 * 1024),
        cost_estimate=pl.CostEstimate(
            flops=count * heads * 5 * 2 * SPAN * keys * HD * 4,
            bytes_accessed=count * 4 * keys * width * 2,
            transcendentals=count * heads * SPAN * keys,
        ),
    )(*operands)


def stage_kernel(source_ref, kv_ref, left_ref, right_ref):
    width = left_ref.shape[-1]
    left_ref[...] = kv_ref[:, :, :, :width]
    right_ref[...] = kv_ref[:, :, :, width:]


def stage(kv, source, count):
    _, _, keys, width = kv.shape
    half_block = pl.BlockSpec((1, 2, keys, width // 2), lambda r, t: (r, 0, 0, 0))
    half_shape = jax.ShapeDtypeStruct((count, 2, keys, width // 2), kv.dtype)
    return pl.pallas_call(
        stage_kernel,
        grid_spec=pltpu.PrefetchScalarGridSpec(
            num_scalar_prefetch=1,
            grid=(count,),
            in_specs=[
                pl.BlockSpec((1, 2, keys, width), lambda r, t: (t[0] * count + r, 0, 0, 0))
            ],
            out_specs=[half_block, half_block],
        ),
        out_shape=[half_shape, half_shape],
        compiler_params=pltpu.CompilerParams(vmem_limit_bytes=12 * 1024 * 1024),
        cost_estimate=pl.CostEstimate(
            flops=0, bytes_accessed=8 * count * keys * width, transcendentals=0
        ),
    )(jnp.reshape(source, (1,)).astype(jnp.int32), kv)


def pick_kernel(depth, which_ref, *refs):
    out_ref = refs[-1]
    rows = refs[0].shape[0]
    for n, ref in enumerate(refs[:-1]):
        for p in range(out_ref.shape[1] // depth):
            start = pl.multiple_of((2 * p + which_ref[0]) * depth, depth)
            out_ref[n * rows:(n + 1) * rows, p * depth:(p + 1) * depth] = ref[:, pl.ds(start, depth)]


def picked(blocks, which, depth):
    rows, columns = blocks[0].shape
    shape = (len(blocks) * rows, columns // 2)
    return pl.pallas_call(
        functools.partial(pick_kernel, depth),
        in_specs=[pl.BlockSpec(memory_space=pltpu.SMEM)]
        + [pl.BlockSpec(memory_space=pltpu.VMEM)] * len(blocks),
        out_specs=pl.BlockSpec(memory_space=pltpu.VMEM),
        out_shape=jax.ShapeDtypeStruct(shape, BF16),
        compiler_params=pltpu.CompilerParams(vmem_limit_bytes=16 * 1024 * 1024),
        cost_estimate=pl.CostEstimate(
            flops=0, bytes_accessed=4 * shape[0] * shape[1], transcendentals=0
        ),
    )(jnp.reshape(which, (1,)).astype(jnp.int32), *blocks)


def total_kernel(tile, *refs):
    out_ref, buf, sem = refs[-3:]
    copies = []
    for n in range(sem.shape[0]):
        some = pl.ds(n * tile, tile)
        buf[some] = total([ref[some] for ref in refs[:-3]])
        copies.append(pltpu.make_async_copy(buf.at[some], out_ref.at[some], sem.at[n]))
        copies[-1].start()
    for copy in copies:
        copy.wait()


def summed(values):
    rows, columns = values[0].shape
    tile = min(64, rows)
    return pl.pallas_call(
        functools.partial(total_kernel, tile),
        in_specs=[pl.BlockSpec(memory_space=pltpu.VMEM)] * len(values),
        out_specs=pl.BlockSpec(memory_space=pl.ANY),
        out_shape=jax.ShapeDtypeStruct((rows, columns), F32),
        scratch_shapes=[
            pltpu.VMEM((rows, columns), F32),
            pltpu.SemaphoreType.DMA((rows // tile,)),
        ],
        compiler_params=pltpu.CompilerParams(vmem_limit_bytes=16 * 1024 * 1024),
        cost_estimate=pl.CostEstimate(
            flops=len(values) * rows * columns,
            bytes_accessed=(2 * len(values) + 4) * rows * columns,
            transcendentals=0,
        ),
    )(*values)


def assemble_kernel(depth, core_ref, own_ref, up_ref, down_ref, arrived_ref, out_ref):
    kept = own_ref[...].astype(F32) + up_ref[...].astype(F32) + down_ref[...].astype(F32)
    kept = kept.astype(BF16)
    for p in range(kept.shape[1] // depth):
        columns = slice(p * depth, (p + 1) * depth)
        mine, other = 2 * p + core_ref[0], 2 * p + 1 - core_ref[0]
        out_ref[:, pl.ds(pl.multiple_of(mine * depth, depth), depth)] = kept[:, columns]
        out_ref[:, pl.ds(pl.multiple_of(other * depth, depth), depth)] = arrived_ref[:, columns]


def assemble(core, own, up, down, arrived, depth):
    rows, columns = arrived.shape
    tile = min(64, rows)
    block = pl.BlockSpec((tile, columns), lambda r: (r, 0))
    return pl.pallas_call(
        functools.partial(assemble_kernel, depth),
        grid=(rows // tile,),
        in_specs=[pl.BlockSpec(memory_space=pltpu.SMEM)] + [block] * 4,
        out_specs=pl.BlockSpec((tile, 2 * columns), lambda r: (r, 0)),
        out_shape=jax.ShapeDtypeStruct((rows, 2 * columns), BF16),
        compiler_params=pltpu.CompilerParams(vmem_limit_bytes=16 * 1024 * 1024),
        cost_estimate=pl.CostEstimate(
            flops=2 * rows * columns, bytes_accessed=12 * rows * columns, transcendentals=0
        ),
    )(jnp.reshape(core, (1,)).astype(jnp.int32), own, up, down, arrived)


def on_device(span_act, q_weight, out_grad, neighbour_kv, neighbour_ids, owner):
    rows, width = out_grad.shape
    depth = q_weight.shape[0]
    seq_count = lax.axis_size("seq")
    dp_count = lax.axis_size("dp")
    tensor_count = lax.axis_size("tensor")
    couples = dp_count // 2
    seq_at = lax.axis_index("seq")
    dp_at = lax.axis_index("dp")
    tensor_at = lax.axis_index("tensor")
    core = dp_at % 2
    spans = rows // SPAN
    capacity = neighbour_kv.shape[0]
    pairs = capacity // seq_count
    whole_blocks = pairs == spans
    per = span_act.shape[1] // depth // 2
    half = width // 2
    opposite = tensor_count // 2

    raw = gather_ring(span_act, "tensor", tensor_count, opposite - 1)
    along_seq = gather_ring(q_weight, "seq", seq_count)
    along_dp = gather_ring(q_weight, "dp", couples)

    groups = owner.reshape(seq_count, dp_count, spans)
    groups = lax.dynamic_index_in_dim(groups, dp_at, 1, keepdims=False)
    mine = lax.dynamic_index_in_dim(groups, seq_at, 0, keepdims=False)

    def order(group, target):
        names = group == target
        at = jnp.arange(spans)
        ahead = (names[None, :] & ~names[:, None]) | (
            (names[None, :] == names[:, None]) & (at[None, :] < at[:, None])
        )
        return jnp.sum(ahead.astype(jnp.int32), axis=1), names.astype(jnp.int32)

    def message(target):
        place, names = order(mine, target)
        hit = place[None, :] == jnp.arange(pairs)[:, None]
        return hit & (names[None, :] == 1)

    def to_owner(value, step):
        value = value.reshape(spans, SPAN, -1)
        if not whole_blocks:
            hit = message((seq_at + step) % seq_count)
            value = jnp.sum(
                jnp.where(hit[:, :, None, None], value[None], jnp.zeros((), BF16)), axis=1
            )
        return shift(value, "seq", step) if step else value

    sources = [(seq_at - step) % seq_count for step in range(seq_count)]
    staged = [stage(neighbour_kv, source, pairs) for source in sources]
    near = [k for k in range(tensor_count) if k != opposite]
    cut = width * 5 // 8 // HD * HD
    left_from = [block[:, :cut] for block in along_seq[1:]]
    right_from = [block[:, cut:] for block in along_dp[1:]]
    left_from, right_from, raw, staged = lax.optimization_barrier(
        (left_from, right_from, [raw[k] for k in near], staged)
    )
    raw = dict(zip(near, raw))

    corner_left = [gather_ring(block, "dp", couples) for block in left_from]
    corner_right = [gather_ring(block, "seq", seq_count) for block in right_from]
    up = shift(raw[opposite - 1][:rows // 2], "tensor", 1)
    down = shift(raw[opposite + 1][rows // 2:], "tensor", -1)
    grad_out = after(out_grad, corner_right)
    grads = [to_owner(grad_out, step) for step in range(seq_count)]

    def columns_of(block, which):
        return jnp.concatenate(
            [
                lax.dynamic_slice(block, (0, (2 * p + which) * depth), (block.shape[0], depth))
                for p in range(per)
            ],
            axis=1,
        )

    others = swap(picked([raw[k] for k in near], 1 - core, depth))
    up, down, others = lax.optimization_barrier((up, down, others))
    raw[opposite] = jnp.concatenate([up, down], axis=0)
    others = {k: others[n * rows:(n + 1) * rows] for n, k in enumerate(near)}
    others[opposite] = swap(columns_of(raw[opposite], 1 - core))
    acts = [
        jnp.concatenate([columns_of(raw[k], core), others[k]], axis=0) for k in range(tensor_count)
    ]
    depth_blocks = [(tensor_at - k) % tensor_count for k in range(tensor_count)]
    table = jnp.stack(depth_blocks).astype(jnp.int32)

    def block_at(i, j):
        block = ((seq_at - i) % seq_count) * dp_count + ((dp_at // 2 - j) % couples) * 2
        return block // (2 * per), (block % (2 * per)) // 2

    places = [(i, j) for i in range(seq_count) for j in range(couples)]
    weights = jnp.zeros((tensor_count, per * depth, width), BF16)
    for i, j in places:
        at, inner = block_at(i, j)
        if j == 0:
            pieces = [(along_seq[i], 0)]
        elif i == 0:
            pieces = [(along_dp[j], 0)]
        else:
            pieces = [(corner_left[i - 1][j], 0), (corner_right[j - 1][i], cut)]
        for piece, start in pieces:
            weights = lax.dynamic_update_slice(weights, piece[None], (at, inner * depth, start))

    def from_owner(value, step):
        value = shift(value, "seq", -step) if step else value
        if not whole_blocks:
            hit = message((seq_at + step) % seq_count)
            value = jnp.sum(
                jnp.where(hit[:, :, None, None], value[:, None], jnp.zeros((), BF16)), axis=0
            )
        return value.reshape(rows, -1)

    def slots_of(step):
        group = lax.dynamic_index_in_dim(groups, sources[step], 0, keepdims=False)
        place, names = order(group, seq_at)
        if not whole_blocks:
            place = jnp.arange(pairs)
            names = (place < jnp.sum(names)).astype(jnp.int32)
        return place, names, sources[step]

    live = jnp.broadcast_to((neighbour_ids != 0).astype(F32)[:, :, None], (capacity, KEYS, HD))
    slots = [slots_of(step) for step in range(seq_count)]

    queries = []
    for part in range(2):
        partial = product(acts, weights, table, part * half, half)
        arrived = swap(partial[rows:])
        if part:
            partial = after(partial, grads)
        queries.append((partial[:rows] + arrived).astype(BF16))
    asked = [[to_owner(value, step) for step in range(seq_count)] for value in queries]
    asked[0][0] = after(asked[0][0], queries[1])

    stacked = jnp.stack(after(acts, queries[1]))

    def act_block(i, j):
        at, inner = block_at(i, j)
        k = (tensor_at - at) % tensor_count
        return lax.dynamic_slice(stacked, (k, 0, inner * depth), (1, 2 * rows, depth))[0]

    def weight_product(i, j, grad):
        found = dot(act_block(i, j), grad, ((0,), (0,)))
        return lax.optimization_barrier(found.astype(BF16))

    kv_grad = None
    answers = [[None] * seq_count for _ in range(2)]
    calls = [(0, 0), (1, 0)] + [(part, step) for part in range(2) for step in range(1, seq_count)]
    for part, step in calls:
        answer, kv_grad = attend(
            *slots[step],
            asked[part][step],
            grads[step],
            staged[step][part],
            live,
            part,
            kv_grad,
        )
        answers[part][step] = from_owner(answer, step)

    far_weights = lax.dynamic_index_in_dim(weights, depth_blocks[opposite], 0, keepdims=False)
    far_weights = after(far_weights, queries[1])
    both_grads, corners = [], []
    corner_places = [(i, j) for i in range(1, seq_count) for j in range(1, couples)]
    for part in range(2):
        ahead = corners[0][corner_places[-1]] if part else far_weights
        answers[part][-1] = after(answers[part][-1], ahead)
        grad = sum(answers[part][1:], answers[part][0])
        both_grads.append(jnp.concatenate([grad, swap(grad)], axis=0))
        if part == 0:
            corners.append({at: weight_product(*at, both_grads[0]) for at in corner_places[::-1]})
    both_grad = jnp.concatenate(both_grads, axis=1)

    def act_product(k, block=None):
        if block is None:
            block = lax.dynamic_index_in_dim(weights, depth_blocks[k], 0, keepdims=False)
        return lax.optimization_barrier(dot(both_grad, block, ((1,), (1,))).astype(BF16))

    far = act_product(opposite, far_weights)
    up, down = shift(far[:rows], "tensor", 1), shift(far[rows:], "tensor", -1)

    late_grad = after(both_grads[1], far)
    corners.append({at: weight_product(*at, late_grad) for at in corner_places[::-1]})
    left = [
        reduce_rings([([None] + [corners[0][i, j] for j in range(1, couples)], True)], "dp")[0][1:]
        for i in range(1, seq_count)
    ]
    right = [
        reduce_rings([([None] + [corners[1][i, j] for i in range(1, seq_count)], True)], "seq")[0][1:]
        for j in range(1, couples)
    ]
    act_parts = {k: act_product(k) for k in range(tensor_count) if k != opposite}
    own = weight_product(0, 0, both_grad)
    beside_seq = [weight_product(i, 0, both_grad) for i in range(1, seq_count)]
    beside_dp = [weight_product(0, j, both_grad) for j in range(1, couples)]
    up, down, left, right, act_parts, own, beside_seq, beside_dp = lax.optimization_barrier(
        (up, down, left, right, act_parts, own, beside_seq, beside_dp)
    )

    beside_seq = [
        lax.dynamic_update_slice(block, total([block[:, :half]] + came).astype(BF16), (0, 0))
        for block, came in zip(beside_seq, left)
    ]
    from_seq = reduce_rings([([None] + beside_seq, True)], "seq")[0][1:]
    for m in range(opposite - 1, 0, -1):
        block = act_parts[tensor_count - m]
        if up.shape[0] == rows:
            up = lax.dynamic_update_slice(block, total([block[:rows], up]).astype(BF16), (0, 0))
        else:
            up = total([block, up]).astype(BF16)
        block = act_parts[m]
        if down.shape[0] == rows:
            down = lax.dynamic_update_slice(
                block, total([block[rows:], down]).astype(BF16), (rows, 0)
            )
        else:
            down = total([block, down]).astype(BF16)
        up, down = shift(up, "tensor", 1), shift(down, "tensor", -1)
    beside_dp = [
        lax.dynamic_update_slice(block, total([block[:, half:]] + came).astype(BF16), (0, half))
        for block, came in zip(beside_dp, right)
    ]
    from_dp = reduce_rings([([None] + beside_dp, True)], "dp")[0][1:]

    weight_grad = summed([own] + from_seq + from_dp)
    others = after([part[rows:] for part in (act_parts[0], up, down)], weight_grad)
    arrived = swap(total(others).astype(BF16))
    act_grad = assemble(core, act_parts[0], up, down, arrived, depth)
    return (act_grad, weight_grad, kv_grad)


def solution(mesh):
    in_specs = (
        P(("seq", "dp"), "tensor"),
        P(("seq", "dp"), "tensor"),
        P(("seq", "dp"), "tensor"),
        P(("seq", "dp"), None, None, "tensor"),
        P(("seq", "dp"), None),
        P(),
    )
    out_specs = (
        P(("seq", "dp"), "tensor"),
        P(("seq", "dp"), "tensor"),
        P(("seq", "dp"), None, None, "tensor"),
    )
    return jax.shard_map(
        on_device, mesh=mesh, in_specs=in_specs, out_specs=out_specs, check_vma=False
    )
```

```python
import functools

import jax
import jax.numpy as jnp
from jax import lax
from jax.experimental import pallas as pl
from jax.experimental.pallas import tpu as pltpu
from jax.sharding import PartitionSpec as P

HD = 128
SPAN = 64
KEYS = 256
F32 = jnp.float32
BF16 = jnp.bfloat16


def dot(a, b, contract):
    return lax.dot_general(a, b, (contract, ((), ())), preferred_element_type=F32)


def shift(value, axis, step=1):
    stride = 2 if axis == "dp" else 1
    size = lax.axis_size(axis)
    return lax.ppermute(value, axis, [(i, (i + step * stride) % size) for i in range(size)])


def swap(value):
    return lax.ppermute(value, "dp", [(i, i ^ 1) for i in range(lax.axis_size("dp"))])


def after(value, *others):
    return lax.optimization_barrier((value, *others))[0]


def reaches(size, far_up):
    up = size // 2 if far_up else (size - 1) // 2
    return up, size - 1 - up


def gather_ring(block, axis, size, rounds=None):
    blocks = [block] + [None] * (size - 1)
    for m in range(1, (size // 2 if rounds is None else rounds) + 1):
        came = {}
        for sign, count in zip((1, -1), reaches(size, True)):
            if m <= count:
                came[(sign * m) % size] = shift(blocks[(sign * (m - 1)) % size], axis, sign)
        for k, value in zip(came, lax.optimization_barrier(tuple(came.values()))):
            blocks[k] = value
    return blocks


def reduce_rings(streams, axis):
    size = len(streams[0][0])
    found = [[blocks[0]] for blocks, _ in streams]
    came = {}
    for m in range(1, size // 2 + 1):
        sent = {}
        for s, (blocks, far_up) in enumerate(streams):
            for sign, count in zip((1, -1), reaches(size, far_up)):
                if m <= count:
                    block = blocks[(-sign * (count - m + 1)) % size]
                    if m > 1:
                        block = came[s, sign].astype(F32) + block.astype(F32)
                    sent[s, sign] = shift(block.astype(BF16), axis, sign)
        came = dict(zip(sent, lax.optimization_barrier(tuple(sent.values()))))
        for (s, sign), block in came.items():
            if m == reaches(size, streams[s][1])[0 if sign == 1 else 1]:
                found[s].append(block)
    return found


def total(values):
    return functools.reduce(lambda a, b: a + b, [value.astype(F32) for value in values])


def product_kernel(count, start, table_ref, *refs):
    blocks, weight_ref, out_ref = refs[:count], refs[count], refs[count + 1]
    tile = min(256, out_ref.shape[1])
    for at in range(0, out_ref.shape[1], tile):
        total = None
        for k in range(count):
            weight = weight_ref[table_ref[k], :, start + at:start + at + tile]
            part = dot(blocks[k][...], weight, ((1,), (0,)))
            total = part if total is None else total + part
        out_ref[:, at:at + tile] = total


def product(blocks, weights, table, start, width):
    count, (rows, depth) = len(blocks), blocks[0].shape
    return pl.pallas_call(
        functools.partial(product_kernel, count, start),
        out_shape=jax.ShapeDtypeStruct((rows, width), F32),
        in_specs=[pl.BlockSpec(memory_space=pltpu.SMEM)]
        + [pl.BlockSpec(memory_space=pltpu.VMEM)] * (count + 1),
        out_specs=pl.BlockSpec(memory_space=pltpu.VMEM),
        compiler_params=pltpu.CompilerParams(vmem_limit_bytes=4 * 1024 * 1024),
        cost_estimate=pl.CostEstimate(
            flops=2 * rows * count * depth * width,
            bytes_accessed=2 * count * depth * (rows + width) + 4 * rows * width,
            transcendentals=0,
        ),
    )(table, *blocks, weights)


def attend_block(q_ref, g_ref, kv_ref, live_ref, dq_ref, grad_ref):
    pairs = q_ref.shape[-1] // HD // 2
    scale = HD ** (-0.5)
    live = live_ref[...] > 0.5
    zero = jnp.zeros((SPAN, HD), BF16)

    def diagonal(ref, start):
        one = ref[:, start:start + HD]
        two = ref[:, start + HD:start + 2 * HD]
        return jnp.concatenate(
            [jnp.concatenate([one, zero], axis=1), jnp.concatenate([zero, two], axis=1)], axis=0
        )

    def first(pair):
        start = pair * 2 * HD
        columns = slice(start, start + 2 * HD)
        scores = dot(kv_ref[0, :, columns], diagonal(q_ref, start), ((1,), (1,)))
        prob_grad = dot(kv_ref[1, :, columns], diagonal(g_ref, start), ((1,), (1,)))
        return scores, prob_grad

    ahead = first(0)
    for pair in range(pairs):
        scores, prob_grad = ahead
        if pair + 1 < pairs:
            ahead = first(pair + 1)
        start = pair * 2 * HD
        columns = slice(start, start + 2 * HD)
        scores = jnp.where(live, scores * scale, -1e30)
        expo = jnp.exp(scores - jnp.max(scores, axis=0, keepdims=True))
        probs = expo * (1.0 / jnp.sum(expo, axis=0, keepdims=True))
        center = jnp.sum(probs * prob_grad, axis=0, keepdims=True)
        score_grad = (probs * (prob_grad - center) * scale).astype(BF16)
        value_grad = dot(probs.astype(BF16), diagonal(g_ref, start), ((1,), (0,)))
        key_grad = dot(score_grad, diagonal(q_ref, start), ((1,), (0,)))
        both = dot(score_grad, kv_ref[0, :, columns], ((0,), (0,)))
        grad_ref[1, :, columns] = value_grad.astype(BF16)
        grad_ref[0, :, columns] = key_grad.astype(BF16)
        dq_ref[:, columns] = jnp.concatenate([both[:SPAN, :HD], both[SPAN:, HD:]], axis=1).astype(
            BF16
        )


def attend_kernel(table_ref, q_ref, g_ref, live_ref, kv_ref, *rest):
    dq_ref, grad_ref = rest[-2:]
    named = table_ref[pl.num_programs(0) + pl.program_id(0)]

    @pl.when(named == 0)
    def _():
        dq_ref[...] = jnp.zeros_like(dq_ref)
        grad_ref[...] = jnp.zeros_like(grad_ref)

    @pl.when(named != 0)
    def _():
        refs = (q_ref, g_ref, kv_ref, live_ref, dq_ref, grad_ref)
        attend_block(*(ref.at[0] for ref in refs))


def attend(place, named, source, queries, grads, kv, live, part, before):
    count, _, width = queries.shape
    capacity, keys, _ = live.shape
    heads = width // HD
    table = jnp.concatenate([place, named, source * count + place]).astype(jnp.int32)
    span_block = pl.BlockSpec((1, SPAN, width), lambda r, t: (r, 0, 0))
    part_block = pl.BlockSpec((1, SPAN, width), lambda r, t: (r, 0, part))
    live_block = pl.BlockSpec((1, keys, HD), lambda r, t: (t[2 * count + r], 0, 0))
    kv_block = pl.BlockSpec((1, 2, keys, width), lambda r, t: (t[r], 0, 0, 0))
    grad_block = pl.BlockSpec((1, 2, keys, width), lambda r, t: (t[2 * count + r], 0, 0, part))
    in_specs = [span_block, part_block, live_block, kv_block]
    operands = [table, queries, grads, live, kv]
    aliases = {}
    if before is not None:
        in_specs.append(pl.BlockSpec(memory_space=pl.ANY))
        operands.append(before)
        aliases = {len(operands) - 1: 1}
    return pl.pallas_call(
        attend_kernel,
        grid_spec=pltpu.PrefetchScalarGridSpec(
            num_scalar_prefetch=1,
            grid=(count,),
            in_specs=in_specs,
            out_specs=[span_block, grad_block],
        ),
        out_shape=[
            jax.ShapeDtypeStruct(queries.shape, BF16),
            jax.ShapeDtypeStruct((capacity, 2, keys, 2 * width), BF16),
        ],
        input_output_aliases=aliases,
        compiler_params=pltpu.CompilerParams(vmem_limit_bytes=6 * 1024 * 1024),
        cost_estimate=pl.CostEstimate(
            flops=count * heads * 5 * 2 * SPAN * keys * HD * 4,
            bytes_accessed=count * 4 * keys * width * 2,
            transcendentals=count * heads * SPAN * keys,
        ),
    )(*operands)


def stage_kernel(source_ref, kv_ref, left_ref, right_ref):
    width = left_ref.shape[-1]
    left_ref[...] = kv_ref[:, :, :, :width]
    right_ref[...] = kv_ref[:, :, :, width:]


def stage(kv, source, count):
    _, _, keys, width = kv.shape
    half_block = pl.BlockSpec((1, 2, keys, width // 2), lambda r, t: (r, 0, 0, 0))
    half_shape = jax.ShapeDtypeStruct((count, 2, keys, width // 2), kv.dtype)
    return pl.pallas_call(
        stage_kernel,
        grid_spec=pltpu.PrefetchScalarGridSpec(
            num_scalar_prefetch=1,
            grid=(count,),
            in_specs=[
                pl.BlockSpec((1, 2, keys, width), lambda r, t: (t[0] * count + r, 0, 0, 0))
            ],
            out_specs=[half_block, half_block],
        ),
        out_shape=[half_shape, half_shape],
        compiler_params=pltpu.CompilerParams(vmem_limit_bytes=8 * 1024 * 1024),
        cost_estimate=pl.CostEstimate(
            flops=0, bytes_accessed=8 * count * keys * width, transcendentals=0
        ),
    )(jnp.reshape(source, (1,)).astype(jnp.int32), kv)


def total_kernel(tile, *refs):
    out_ref, buf, sem = refs[-3:]
    copies = []
    for n in range(sem.shape[0]):
        some = pl.ds(n * tile, tile)
        buf[some] = total([ref[some] for ref in refs[:-3]])
        copies.append(pltpu.make_async_copy(buf.at[some], out_ref.at[some], sem.at[n]))
        copies[-1].start()
    for copy in copies:
        copy.wait()


def summed(values):
    rows, columns = values[0].shape
    tile = min(64, rows)
    return pl.pallas_call(
        functools.partial(total_kernel, tile),
        in_specs=[pl.BlockSpec(memory_space=pltpu.VMEM)] * len(values),
        out_specs=pl.BlockSpec(memory_space=pl.ANY),
        out_shape=jax.ShapeDtypeStruct((rows, columns), F32),
        scratch_shapes=[
            pltpu.VMEM((rows, columns), F32),
            pltpu.SemaphoreType.DMA((rows // tile,)),
        ],
        compiler_params=pltpu.CompilerParams(vmem_limit_bytes=6 * 1024 * 1024),
        cost_estimate=pl.CostEstimate(
            flops=len(values) * rows * columns,
            bytes_accessed=(2 * len(values) + 4) * rows * columns,
            transcendentals=0,
        ),
    )(*values)


def assemble_kernel(depth, core_ref, own_ref, up_ref, down_ref, arrived_ref, out_ref):
    kept = own_ref[...].astype(F32) + up_ref[...].astype(F32) + down_ref[...].astype(F32)
    kept = kept.astype(BF16)
    for p in range(kept.shape[1] // depth):
        columns = slice(p * depth, (p + 1) * depth)
        mine, other = 2 * p + core_ref[0], 2 * p + 1 - core_ref[0]
        out_ref[:, pl.ds(pl.multiple_of(mine * depth, depth), depth)] = kept[:, columns]
        out_ref[:, pl.ds(pl.multiple_of(other * depth, depth), depth)] = arrived_ref[:, columns]


def assemble(core, own, up, down, arrived, depth):
    rows, columns = arrived.shape
    tile = min(64, rows)
    block = pl.BlockSpec((tile, columns), lambda r: (r, 0))
    return pl.pallas_call(
        functools.partial(assemble_kernel, depth),
        grid=(rows // tile,),
        in_specs=[pl.BlockSpec(memory_space=pltpu.SMEM)] + [block] * 4,
        out_specs=pl.BlockSpec((tile, 2 * columns), lambda r: (r, 0)),
        out_shape=jax.ShapeDtypeStruct((rows, 2 * columns), BF16),
        compiler_params=pltpu.CompilerParams(vmem_limit_bytes=4 * 1024 * 1024),
        cost_estimate=pl.CostEstimate(
            flops=2 * rows * columns, bytes_accessed=12 * rows * columns, transcendentals=0
        ),
    )(jnp.reshape(core, (1,)).astype(jnp.int32), own, up, down, arrived)


def on_device(span_act, q_weight, out_grad, neighbour_kv, neighbour_ids, owner):
    rows, width = out_grad.shape
    depth = q_weight.shape[0]
    seq_count = lax.axis_size("seq")
    dp_count = lax.axis_size("dp")
    tensor_count = lax.axis_size("tensor")
    couples = dp_count // 2
    seq_at = lax.axis_index("seq")
    dp_at = lax.axis_index("dp")
    tensor_at = lax.axis_index("tensor")
    core = dp_at % 2
    spans = rows // SPAN
    capacity = neighbour_kv.shape[0]
    pairs = capacity // seq_count
    whole_blocks = pairs == spans
    per = span_act.shape[1] // depth // 2
    half = width // 2
    opposite = tensor_count // 2

    raw = gather_ring(span_act, "tensor", tensor_count, opposite - 1)
    along_seq = gather_ring(q_weight, "seq", seq_count)
    along_dp = gather_ring(q_weight, "dp", couples)

    groups = owner.reshape(seq_count, dp_count, spans)
    groups = lax.dynamic_index_in_dim(groups, dp_at, 1, keepdims=False)
    mine = lax.dynamic_index_in_dim(groups, seq_at, 0, keepdims=False)

    def order(group, target):
        names = group == target
        at = jnp.arange(spans)
        ahead = (names[None, :] & ~names[:, None]) | (
            (names[None, :] == names[:, None]) & (at[None, :] < at[:, None])
        )
        return jnp.sum(ahead.astype(jnp.int32), axis=1), names.astype(jnp.int32)

    def message(target):
        place, names = order(mine, target)
        hit = place[None, :] == jnp.arange(pairs)[:, None]
        return hit & (names[None, :] == 1)

    def to_owner(value, step):
        value = value.reshape(spans, SPAN, -1)
        if not whole_blocks:
            hit = message((seq_at + step) % seq_count)
            value = jnp.sum(
                jnp.where(hit[:, :, None, None], value[None], jnp.zeros((), BF16)), axis=1
            )
        return shift(value, "seq", step) if step else value

    sources = [(seq_at - step) % seq_count for step in range(seq_count)]
    staged = [stage(neighbour_kv, source, pairs) for source in sources]
    near = [k for k in range(tensor_count) if k != opposite]
    cut = width * 5 // 8 // HD * HD
    left_from = [block[:, :cut] for block in along_seq[1:]]
    right_from = [block[:, cut:] for block in along_dp[1:]]
    left_from, right_from, raw, staged = lax.optimization_barrier(
        (left_from, right_from, [raw[k] for k in near], staged)
    )
    raw = dict(zip(near, raw))

    corner_left = [gather_ring(block, "dp", couples) for block in left_from]
    corner_right = [gather_ring(block, "seq", seq_count) for block in right_from]
    up = shift(raw[opposite - 1][:rows // 2], "tensor", 1)
    down = shift(raw[opposite + 1][rows // 2:], "tensor", -1)
    grad_out = after(out_grad, corner_right)
    grads = [to_owner(grad_out, step) for step in range(seq_count)]

    def columns_of(block, which):
        return jnp.concatenate(
            [
                lax.dynamic_slice(block, (0, (2 * p + which) * depth), (block.shape[0], depth))
                for p in range(per)
            ],
            axis=1,
        )

    others = swap(jnp.concatenate([columns_of(raw[k], 1 - core) for k in near], axis=0))
    up, down, others = lax.optimization_barrier((up, down, others))
    raw[opposite] = jnp.concatenate([up, down], axis=0)
    others = {k: others[n * rows:(n + 1) * rows] for n, k in enumerate(near)}
    others[opposite] = swap(columns_of(raw[opposite], 1 - core))
    acts = [
        jnp.concatenate([columns_of(raw[k], core), others[k]], axis=0) for k in range(tensor_count)
    ]
    depth_blocks = [(tensor_at - k) % tensor_count for k in range(tensor_count)]
    table = jnp.stack(depth_blocks).astype(jnp.int32)

    def block_at(i, j):
        block = ((seq_at - i) % seq_count) * dp_count + ((dp_at // 2 - j) % couples) * 2
        return block // (2 * per), (block % (2 * per)) // 2

    places = [(i, j) for i in range(seq_count) for j in range(couples)]
    weights = jnp.zeros((tensor_count, per * depth, width), BF16)
    for i, j in places:
        at, inner = block_at(i, j)
        if j == 0:
            pieces = [(along_seq[i], 0)]
        elif i == 0:
            pieces = [(along_dp[j], 0)]
        else:
            pieces = [(corner_left[i - 1][j], 0), (corner_right[j - 1][i], cut)]
        for piece, start in pieces:
            weights = lax.dynamic_update_slice(weights, piece[None], (at, inner * depth, start))

    def from_owner(value, step):
        value = shift(value, "seq", -step) if step else value
        if not whole_blocks:
            hit = message((seq_at + step) % seq_count)
            value = jnp.sum(
                jnp.where(hit[:, :, None, None], value[:, None], jnp.zeros((), BF16)), axis=0
            )
        return value.reshape(rows, -1)

    def slots_of(step):
        group = lax.dynamic_index_in_dim(groups, sources[step], 0, keepdims=False)
        place, names = order(group, seq_at)
        if not whole_blocks:
            place = jnp.arange(pairs)
            names = (place < jnp.sum(names)).astype(jnp.int32)
        return place, names, sources[step]

    live = jnp.broadcast_to((neighbour_ids != 0).astype(F32)[:, :, None], (capacity, KEYS, HD))
    slots = [slots_of(step) for step in range(seq_count)]

    queries = []
    for part in range(2):
        partial = product(acts, weights, table, part * half, half)
        arrived = swap(partial[rows:])
        if part:
            partial = after(partial, grads)
        queries.append((partial[:rows] + arrived).astype(BF16))
    asked = [[to_owner(value, step) for step in range(seq_count)] for value in queries]
    asked[0][0] = after(asked[0][0], queries[1])

    stacked = jnp.stack(after(acts, queries[1]))

    def act_block(i, j):
        at, inner = block_at(i, j)
        k = (tensor_at - at) % tensor_count
        return lax.dynamic_slice(stacked, (k, 0, inner * depth), (1, 2 * rows, depth))[0]

    def weight_product(i, j, grad):
        found = dot(act_block(i, j), grad, ((0,), (0,)))
        return lax.optimization_barrier(found.astype(BF16))

    kv_grad = None
    answers = [[None] * seq_count for _ in range(2)]
    calls = [(0, 0), (1, 0)] + [(part, step) for part in range(2) for step in range(1, seq_count)]
    for part, step in calls:
        answer, kv_grad = attend(
            *slots[step],
            asked[part][step],
            grads[step],
            staged[step][part],
            live,
            part,
            kv_grad,
        )
        answers[part][step] = from_owner(answer, step)

    far_weights = lax.dynamic_index_in_dim(weights, depth_blocks[opposite], 0, keepdims=False)
    far_weights = after(far_weights, queries[1])
    both_grads, corners = [], []
    corner_places = [(i, j) for i in range(1, seq_count) for j in range(1, couples)]
    for part in range(2):
        if part:
            answers[1][-1] = after(answers[1][-1], corners[0][corner_places[-1]])
        grad = sum(answers[part][1:], answers[part][0])
        both_grads.append(jnp.concatenate([grad, swap(grad)], axis=0))
        if part == 0:
            corners.append({at: weight_product(*at, both_grads[0]) for at in corner_places[::-1]})
    both_grad = jnp.concatenate(both_grads, axis=1)

    def act_product(k, block=None):
        if block is None:
            block = lax.dynamic_index_in_dim(weights, depth_blocks[k], 0, keepdims=False)
        return lax.optimization_barrier(dot(both_grad, block, ((1,), (1,))).astype(BF16))

    far = act_product(opposite, far_weights)
    up, down = shift(far[:rows], "tensor", 1), shift(far[rows:], "tensor", -1)

    late_grad = after(both_grads[1], far)
    corners.append({at: weight_product(*at, late_grad) for at in corner_places[::-1]})
    left = [
        reduce_rings([([None] + [corners[0][i, j] for j in range(1, couples)], True)], "dp")[0][1:]
        for i in range(1, seq_count)
    ]
    right = [
        reduce_rings([([None] + [corners[1][i, j] for i in range(1, seq_count)], True)], "seq")[0][1:]
        for j in range(1, couples)
    ]
    act_parts = {k: act_product(k) for k in range(tensor_count) if k != opposite}
    own = weight_product(0, 0, both_grad)
    beside_seq = [weight_product(i, 0, both_grad) for i in range(1, seq_count)]
    beside_dp = [weight_product(0, j, both_grad) for j in range(1, couples)]
    up, down, left, right, act_parts, own, beside_seq, beside_dp = lax.optimization_barrier(
        (up, down, left, right, act_parts, own, beside_seq, beside_dp)
    )

    beside_seq = [
        lax.dynamic_update_slice(block, total([block[:, :half]] + came).astype(BF16), (0, 0))
        for block, came in zip(beside_seq, left)
    ]
    from_seq = reduce_rings([([None] + beside_seq, True)], "seq")[0][1:]
    for m in range(opposite - 1, 0, -1):
        block = act_parts[tensor_count - m]
        if up.shape[0] == rows:
            up = lax.dynamic_update_slice(block, total([block[:rows], up]).astype(BF16), (0, 0))
        else:
            up = total([block, up]).astype(BF16)
        block = act_parts[m]
        if down.shape[0] == rows:
            down = lax.dynamic_update_slice(
                block, total([block[rows:], down]).astype(BF16), (rows, 0)
            )
        else:
            down = total([block, down]).astype(BF16)
        up, down = shift(up, "tensor", 1), shift(down, "tensor", -1)
    beside_dp = [
        lax.dynamic_update_slice(block, total([block[:, half:]] + came).astype(BF16), (0, half))
        for block, came in zip(beside_dp, right)
    ]
    from_dp = reduce_rings([([None] + beside_dp, True)], "dp")[0][1:]

    weight_grad = summed([own] + from_seq + from_dp)
    others = after([part[rows:] for part in (act_parts[0], up, down)], weight_grad)
    arrived = swap(total(others).astype(BF16))
    act_grad = assemble(core, act_parts[0], up, down, arrived, depth)
    return (act_grad, weight_grad, kv_grad)


def solution(mesh):
    in_specs = (
        P(("seq", "dp"), "tensor"),
        P(("seq", "dp"), "tensor"),
        P(("seq", "dp"), "tensor"),
        P(("seq", "dp"), None, None, "tensor"),
        P(("seq", "dp"), None),
        P(),
    )
    out_specs = (
        P(("seq", "dp"), "tensor"),
        P(("seq", "dp"), "tensor"),
        P(("seq", "dp"), None, None, "tensor"),
    )
    return jax.shard_map(
        on_device, mesh=mesh, in_specs=in_specs, out_specs=out_specs, check_vma=False
    )
```

```python
import functools

import jax
import jax.numpy as jnp
from jax import lax
from jax.experimental import pallas as pl
from jax.experimental.pallas import tpu as pltpu
from jax.sharding import PartitionSpec as P

HD = 128
SPAN = 64
KEYS = 256
F32 = jnp.float32
BF16 = jnp.bfloat16


def dot(a, b, contract):
    return lax.dot_general(a, b, (contract, ((), ())), preferred_element_type=F32)


def shift(value, axis, step=1):
    stride = 2 if axis == "dp" else 1
    size = lax.axis_size(axis)
    return lax.ppermute(value, axis, [(i, (i + step * stride) % size) for i in range(size)])


def swap(value):
    return lax.ppermute(value, "dp", [(i, i ^ 1) for i in range(lax.axis_size("dp"))])


def after(value, *others):
    return lax.optimization_barrier((value, *others))[0]


def reaches(size, far_up):
    up = size // 2 if far_up else (size - 1) // 2
    return up, size - 1 - up


def gather_ring(block, axis, size, rounds=None):
    blocks = [block] + [None] * (size - 1)
    for m in range(1, (size // 2 if rounds is None else rounds) + 1):
        came = {}
        for sign, count in zip((1, -1), reaches(size, True)):
            if m <= count:
                came[(sign * m) % size] = shift(blocks[(sign * (m - 1)) % size], axis, sign)
        for k, value in zip(came, lax.optimization_barrier(tuple(came.values()))):
            blocks[k] = value
    return blocks


def reduce_rings(streams, axis):
    size = len(streams[0][0])
    found = [[blocks[0]] for blocks, _ in streams]
    came = {}
    for m in range(1, size // 2 + 1):
        sent = {}
        for s, (blocks, far_up) in enumerate(streams):
            for sign, count in zip((1, -1), reaches(size, far_up)):
                if m <= count:
                    block = blocks[(-sign * (count - m + 1)) % size]
                    if m > 1:
                        block = came[s, sign].astype(F32) + block.astype(F32)
                    sent[s, sign] = shift(block.astype(BF16), axis, sign)
        came = dict(zip(sent, lax.optimization_barrier(tuple(sent.values()))))
        for (s, sign), block in came.items():
            if m == reaches(size, streams[s][1])[0 if sign == 1 else 1]:
                found[s].append(block)
    return found


def total(values):
    return functools.reduce(lambda a, b: a + b, [value.astype(F32) for value in values])


def product_kernel(count, depth, part, table_ref, act_ref, *refs):
    out_ref = refs[-1]
    tile = min(256, out_ref.shape[1])
    for at in range(0, out_ref.shape[1], tile):
        found = None
        for n, weight_ref in enumerate(refs[:-1]):
            inner = pl.ds(pl.multiple_of(table_ref[count + n] * depth, depth), depth)
            act = act_ref[table_ref[n], :, inner]
            start = at + (part * out_ref.shape[1] if weight_ref.shape[1] > out_ref.shape[1] else 0)
            more = dot(act, weight_ref[:, start:start + tile], ((1,), (0,)))
            found = more if found is None else found + more
        out_ref[:, at:at + tile] = found


def product(acts, weights, table, part):
    count, rows = len(weights), acts.shape[1]
    depth, width = weights[0].shape[0], min(block.shape[1] for block in weights)
    return pl.pallas_call(
        functools.partial(product_kernel, count, depth, part),
        out_shape=jax.ShapeDtypeStruct((rows, width), F32),
        in_specs=[pl.BlockSpec(memory_space=pltpu.SMEM)]
        + [pl.BlockSpec(memory_space=pltpu.VMEM)] * (count + 1),
        out_specs=pl.BlockSpec(memory_space=pltpu.VMEM),
        compiler_params=pltpu.CompilerParams(vmem_limit_bytes=4 * 1024 * 1024),
        cost_estimate=pl.CostEstimate(
            flops=2 * rows * count * depth * width,
            bytes_accessed=2 * count * depth * (rows + width) + 4 * rows * width,
            transcendentals=0,
        ),
    )(table, acts, *weights)


def attend_block(q_ref, g_ref, kv_ref, live_ref, dq_ref, grad_ref):
    pairs = q_ref.shape[-1] // HD // 2
    scale = HD ** (-0.5)
    live = live_ref[...] > 0.5
    zero = jnp.zeros((SPAN, HD), BF16)

    def diagonal(ref, start):
        one = ref[:, start:start + HD]
        two = ref[:, start + HD:start + 2 * HD]
        return jnp.concatenate(
            [jnp.concatenate([one, zero], axis=1), jnp.concatenate([zero, two], axis=1)], axis=0
        )

    def first(pair):
        start = pair * 2 * HD
        columns = slice(start, start + 2 * HD)
        scores = dot(kv_ref[0, :, columns], diagonal(q_ref, start), ((1,), (1,)))
        prob_grad = dot(kv_ref[1, :, columns], diagonal(g_ref, start), ((1,), (1,)))
        return scores, prob_grad

    ahead = first(0)
    for pair in range(pairs):
        scores, prob_grad = ahead
        if pair + 1 < pairs:
            ahead = first(pair + 1)
        start = pair * 2 * HD
        columns = slice(start, start + 2 * HD)
        scores = jnp.where(live, scores * scale, -1e30)
        expo = jnp.exp(scores - jnp.max(scores, axis=0, keepdims=True))
        probs = expo * (1.0 / jnp.sum(expo, axis=0, keepdims=True))
        center = jnp.sum(probs * prob_grad, axis=0, keepdims=True)
        score_grad = (probs * (prob_grad - center) * scale).astype(BF16)
        value_grad = dot(probs.astype(BF16), diagonal(g_ref, start), ((1,), (0,)))
        key_grad = dot(score_grad, diagonal(q_ref, start), ((1,), (0,)))
        both = dot(score_grad, kv_ref[0, :, columns], ((0,), (0,)))
        grad_ref[1, :, columns] = value_grad.astype(BF16)
        grad_ref[0, :, columns] = key_grad.astype(BF16)
        dq_ref[:, columns] = jnp.concatenate([both[:SPAN, :HD], both[SPAN:, HD:]], axis=1).astype(
            BF16
        )


def attend_kernel(table_ref, q_ref, g_ref, live_ref, kv_ref, *rest):
    dq_ref, grad_ref = rest[-2:]
    named = table_ref[pl.num_programs(0) + pl.program_id(0)]

    @pl.when(named == 0)
    def _():
        dq_ref[...] = jnp.zeros_like(dq_ref)
        grad_ref[...] = jnp.zeros_like(grad_ref)

    @pl.when(named != 0)
    def _():
        refs = (q_ref, g_ref, kv_ref, live_ref, dq_ref, grad_ref)
        attend_block(*(ref.at[0] for ref in refs))


def attend(place, named, source, queries, grads, kv, live, part, before):
    count, _, width = queries.shape
    capacity, keys, _ = live.shape
    heads = width // HD
    table = jnp.concatenate([place, named, source * count + place]).astype(jnp.int32)
    span_block = pl.BlockSpec((1, SPAN, width), lambda r, t: (r, 0, 0))
    part_block = pl.BlockSpec((1, SPAN, width), lambda r, t: (r, 0, part))
    live_block = pl.BlockSpec((1, keys, HD), lambda r, t: (t[2 * count + r], 0, 0))
    kv_block = pl.BlockSpec((1, 2, keys, width), lambda r, t: (t[r], 0, 0, 0))
    grad_block = pl.BlockSpec((1, 2, keys, width), lambda r, t: (t[2 * count + r], 0, 0, part))
    in_specs = [span_block, part_block, live_block, kv_block]
    operands = [table, queries, grads, live, kv]
    aliases = {}
    if before is not None:
        in_specs.append(pl.BlockSpec(memory_space=pl.ANY))
        operands.append(before)
        aliases = {len(operands) - 1: 1}
    return pl.pallas_call(
        attend_kernel,
        grid_spec=pltpu.PrefetchScalarGridSpec(
            num_scalar_prefetch=1,
            grid=(count,),
            in_specs=in_specs,
            out_specs=[span_block, grad_block],
        ),
        out_shape=[
            jax.ShapeDtypeStruct(queries.shape, BF16),
            jax.ShapeDtypeStruct((capacity, 2, keys, 2 * width), BF16),
        ],
        input_output_aliases=aliases,
        compiler_params=pltpu.CompilerParams(vmem_limit_bytes=6 * 1024 * 1024),
        cost_estimate=pl.CostEstimate(
            flops=count * heads * 5 * 2 * SPAN * keys * HD * 4,
            bytes_accessed=count * 4 * keys * width * 2,
            transcendentals=count * heads * SPAN * keys,
        ),
    )(*operands)


def stage_kernel(source_ref, kv_ref, left_ref, right_ref):
    width = left_ref.shape[-1]
    left_ref[...] = kv_ref[:, :, :, :width]
    right_ref[...] = kv_ref[:, :, :, width:]


def stage(kv, source, count):
    _, _, keys, width = kv.shape
    half_block = pl.BlockSpec((1, 2, keys, width // 2), lambda r, t: (r, 0, 0, 0))
    half_shape = jax.ShapeDtypeStruct((count, 2, keys, width // 2), kv.dtype)
    return pl.pallas_call(
        stage_kernel,
        grid_spec=pltpu.PrefetchScalarGridSpec(
            num_scalar_prefetch=1,
            grid=(count,),
            in_specs=[
                pl.BlockSpec((1, 2, keys, width), lambda r, t: (t[0] * count + r, 0, 0, 0))
            ],
            out_specs=[half_block, half_block],
        ),
        out_shape=[half_shape, half_shape],
        compiler_params=pltpu.CompilerParams(vmem_limit_bytes=8 * 1024 * 1024),
        cost_estimate=pl.CostEstimate(
            flops=0, bytes_accessed=8 * count * keys * width, transcendentals=0
        ),
    )(jnp.reshape(source, (1,)).astype(jnp.int32), kv)


def total_kernel(tile, *refs):
    out_ref, buf, sem = refs[-3:]
    copies = []
    for n in range(sem.shape[0]):
        some = pl.ds(n * tile, tile)
        buf[some] = total([ref[some] for ref in refs[:-3]])
        copies.append(pltpu.make_async_copy(buf.at[some], out_ref.at[some], sem.at[n]))
        copies[-1].start()
    for copy in copies:
        copy.wait()


def summed(values):
    rows, columns = values[0].shape
    tile = min(64, rows)
    return pl.pallas_call(
        functools.partial(total_kernel, tile),
        in_specs=[pl.BlockSpec(memory_space=pltpu.VMEM)] * len(values),
        out_specs=pl.BlockSpec(memory_space=pl.ANY),
        out_shape=jax.ShapeDtypeStruct((rows, columns), F32),
        scratch_shapes=[
            pltpu.VMEM((rows, columns), F32),
            pltpu.SemaphoreType.DMA((rows // tile,)),
        ],
        compiler_params=pltpu.CompilerParams(vmem_limit_bytes=6 * 1024 * 1024),
        cost_estimate=pl.CostEstimate(
            flops=len(values) * rows * columns,
            bytes_accessed=(2 * len(values) + 4) * rows * columns,
            transcendentals=0,
        ),
    )(*values)


def assemble_kernel(depth, core_ref, own_ref, up_ref, down_ref, arrived_ref, out_ref):
    kept = own_ref[...].astype(F32) + up_ref[...].astype(F32) + down_ref[...].astype(F32)
    kept = kept.astype(BF16)
    for p in range(kept.shape[1] // depth):
        columns = slice(p * depth, (p + 1) * depth)
        mine, other = 2 * p + core_ref[0], 2 * p + 1 - core_ref[0]
        out_ref[:, pl.ds(pl.multiple_of(mine * depth, depth), depth)] = kept[:, columns]
        out_ref[:, pl.ds(pl.multiple_of(other * depth, depth), depth)] = arrived_ref[:, columns]


def assemble(core, own, up, down, arrived, depth):
    rows, columns = arrived.shape
    tile = min(64, rows)
    block = pl.BlockSpec((tile, columns), lambda r: (r, 0))
    return pl.pallas_call(
        functools.partial(assemble_kernel, depth),
        grid=(rows // tile,),
        in_specs=[pl.BlockSpec(memory_space=pltpu.SMEM)] + [block] * 4,
        out_specs=pl.BlockSpec((tile, 2 * columns), lambda r: (r, 0)),
        out_shape=jax.ShapeDtypeStruct((rows, 2 * columns), BF16),
        compiler_params=pltpu.CompilerParams(vmem_limit_bytes=4 * 1024 * 1024),
        cost_estimate=pl.CostEstimate(
            flops=2 * rows * columns, bytes_accessed=12 * rows * columns, transcendentals=0
        ),
    )(jnp.reshape(core, (1,)).astype(jnp.int32), own, up, down, arrived)


def on_device(span_act, q_weight, out_grad, neighbour_kv, neighbour_ids, owner):
    rows, width = out_grad.shape
    depth = q_weight.shape[0]
    seq_count = lax.axis_size("seq")
    dp_count = lax.axis_size("dp")
    tensor_count = lax.axis_size("tensor")
    couples = dp_count // 2
    seq_at = lax.axis_index("seq")
    dp_at = lax.axis_index("dp")
    tensor_at = lax.axis_index("tensor")
    core = dp_at % 2
    spans = rows // SPAN
    capacity = neighbour_kv.shape[0]
    pairs = capacity // seq_count
    whole_blocks = pairs == spans
    per = span_act.shape[1] // depth // 2
    half = width // 2
    opposite = tensor_count // 2

    raw = gather_ring(span_act, "tensor", tensor_count, opposite - 1)
    along_seq = gather_ring(q_weight, "seq", seq_count)
    along_dp = gather_ring(q_weight, "dp", couples)

    groups = owner.reshape(seq_count, dp_count, spans)
    groups = lax.dynamic_index_in_dim(groups, dp_at, 1, keepdims=False)
    mine = lax.dynamic_index_in_dim(groups, seq_at, 0, keepdims=False)

    def order(group, target):
        names = group == target
        at = jnp.arange(spans)
        ahead = (names[None, :] & ~names[:, None]) | (
            (names[None, :] == names[:, None]) & (at[None, :] < at[:, None])
        )
        return jnp.sum(ahead.astype(jnp.int32), axis=1), names.astype(jnp.int32)

    def message(target):
        place, names = order(mine, target)
        hit = place[None, :] == jnp.arange(pairs)[:, None]
        return hit & (names[None, :] == 1)

    def to_owner(value, step):
        value = value.reshape(spans, SPAN, -1)
        if not whole_blocks:
            hit = message((seq_at + step) % seq_count)
            value = jnp.sum(
                jnp.where(hit[:, :, None, None], value[None], jnp.zeros((), BF16)), axis=1
            )
        return shift(value, "seq", step) if step else value

    sources = [(seq_at - step) % seq_count for step in range(seq_count)]
    staged = [stage(neighbour_kv, source, pairs) for source in sources]
    near = [k for k in range(tensor_count) if k != opposite]
    left_from = [block[:, :half] for block in along_seq[1:]]
    right_from = [block[:, half:] for block in along_dp[1:]]
    left_from, right_from, raw, staged = lax.optimization_barrier(
        (left_from, right_from, [raw[k] for k in near], staged)
    )
    raw = dict(zip(near, raw))

    corner_left = [gather_ring(block, "dp", couples) for block in left_from]
    corner_right = [gather_ring(block, "seq", seq_count) for block in right_from]
    up = shift(raw[opposite - 1][:rows // 2], "tensor", 1)
    down = shift(raw[opposite + 1][rows // 2:], "tensor", -1)
    def columns_of(block, which):
        return jnp.concatenate(
            [
                lax.dynamic_slice(block, (0, (2 * p + which) * depth), (block.shape[0], depth))
                for p in range(per)
            ],
            axis=1,
        )

    others = swap(jnp.concatenate([columns_of(raw[k], 1 - core) for k in near], axis=0))
    grad_out, others = lax.optimization_barrier((out_grad, others, corner_right))[:2]
    grads = [to_owner(grad_out, step) for step in range(seq_count)]
    others = {k: others[n * rows:(n + 1) * rows] for n, k in enumerate(near)}
    depth_blocks = [(tensor_at - k) % tensor_count for k in range(tensor_count)]

    def block_at(i, j):
        block = ((seq_at - i) % seq_count) * dp_count + ((dp_at // 2 - j) % couples) * 2
        return (tensor_at - block // (2 * per)) % tensor_count, (block % (2 * per)) // 2

    places = [(i, j) for i in range(seq_count) for j in range(couples)]
    table = [block_at(i, j) for i, j in places]
    table = jnp.stack([k for k, _ in table] + [inner for _, inner in table]).astype(jnp.int32)

    acts = jnp.zeros((tensor_count, 2 * rows, per * depth), BF16)
    for k in near:
        block = jnp.concatenate([columns_of(raw[k], core), others[k]], axis=0)
        acts = lax.dynamic_update_slice(acts, block[None], (k, 0, 0))

    def placed(weights, piece, i, j, column):
        k, inner = block_at(i, j)
        at = ((tensor_at - k) % tensor_count, inner * depth, column)
        return lax.dynamic_update_slice(weights, piece[None], at)

    by_depth = jnp.zeros((tensor_count, per * depth, width), BF16)
    for i, j in places:
        if i == 0 or j == 0:
            by_depth = placed(by_depth, along_seq[i] if j == 0 else along_dp[j], i, j, 0)

    acts, by_depth, up, down = lax.optimization_barrier((acts, by_depth, up, down))
    for n, which in enumerate((core, 1 - core)):
        block = jnp.concatenate([columns_of(block, which) for block in (up, down)], axis=0)
        block = swap(block) if n else block
        acts = lax.dynamic_update_slice(acts, block[None], (opposite, n * rows, 0))

    def weight_pieces(i, j):
        if j == 0:
            return [along_seq[i]]
        if i == 0:
            return [along_dp[j]]
        return [corner_left[i - 1][j], corner_right[j - 1][i]]

    def from_owner(value, step):
        value = shift(value, "seq", -step) if step else value
        if not whole_blocks:
            hit = message((seq_at + step) % seq_count)
            value = jnp.sum(
                jnp.where(hit[:, :, None, None], value[:, None], jnp.zeros((), BF16)), axis=0
            )
        return value.reshape(rows, -1)

    def slots_of(step):
        group = lax.dynamic_index_in_dim(groups, sources[step], 0, keepdims=False)
        place, names = order(group, seq_at)
        if not whole_blocks:
            place = jnp.arange(pairs)
            names = (place < jnp.sum(names)).astype(jnp.int32)
        return place, names, sources[step]

    live = jnp.broadcast_to((neighbour_ids != 0).astype(F32)[:, :, None], (capacity, KEYS, HD))
    slots = [slots_of(step) for step in range(seq_count)]

    queries = []
    for part in range(2):
        weights = [weight_pieces(i, j)[part if i and j else 0] for i, j in places]
        partial = product(acts, weights, table, part)
        arrived = swap(partial[rows:])
        if part:
            partial = after(partial, grads)
        queries.append((partial[:rows] + arrived).astype(BF16))
    asked = [[to_owner(value, step) for step in range(seq_count)] for value in queries]
    asked[0][0] = after(asked[0][0], queries[1])

    weights = by_depth
    for i, j in places:
        if i and j:
            for n, piece in enumerate(after(weight_pieces(i, j), queries[1])):
                weights = placed(weights, piece, i, j, n * half)

    def act_block(i, j):
        k, inner = block_at(i, j)
        return lax.dynamic_slice(acts, (k, 0, inner * depth), (1, 2 * rows, depth))[0]

    def weight_product(i, j, grad):
        found = dot(act_block(i, j), grad, ((0,), (0,)))
        return lax.optimization_barrier(found.astype(BF16))

    kv_grad = None
    answers = [[None] * seq_count for _ in range(2)]
    calls = [(0, 0), (1, 0)] + [(part, step) for part in range(2) for step in range(1, seq_count)]
    for part, step in calls:
        answer, kv_grad = attend(
            *slots[step],
            asked[part][step],
            grads[step],
            staged[step][part],
            live,
            part,
            kv_grad,
        )
        answers[part][step] = from_owner(answer, step)

    far_weights = lax.dynamic_index_in_dim(weights, depth_blocks[opposite], 0, keepdims=False)
    far_weights = after(far_weights, queries[1])
    both_grads, corners = [], []
    corner_places = [(i, j) for i in range(1, seq_count) for j in range(1, couples)]
    for part in range(2):
        if part:
            answers[1][-1] = after(answers[1][-1], corners[0][corner_places[-1]])
        grad = sum(answers[part][1:], answers[part][0])
        both_grads.append(jnp.concatenate([grad, swap(grad)], axis=0))
        if part == 0:
            corners.append({at: weight_product(*at, both_grads[0]) for at in corner_places[::-1]})
    both_grad = jnp.concatenate(both_grads, axis=1)

    def act_product(k, block=None):
        if block is None:
            block = lax.dynamic_index_in_dim(weights, depth_blocks[k], 0, keepdims=False)
        return lax.optimization_barrier(dot(both_grad, block, ((1,), (1,))).astype(BF16))

    far = act_product(opposite, far_weights)
    up, down = shift(far[:rows], "tensor", 1), shift(far[rows:], "tensor", -1)

    late_grad = after(both_grads[1], far)
    corners.append({at: weight_product(*at, late_grad) for at in corner_places[::-1]})
    left = [
        reduce_rings([([None] + [corners[0][i, j] for j in range(1, couples)], True)], "dp")[0][1:]
        for i in range(1, seq_count)
    ]
    right = [
        reduce_rings([([None] + [corners[1][i, j] for i in range(1, seq_count)], True)], "seq")[0][1:]
        for j in range(1, couples)
    ]
    act_parts = {k: act_product(k) for k in range(tensor_count) if k != opposite}
    own = weight_product(0, 0, both_grad)
    beside_seq = [weight_product(i, 0, both_grad) for i in range(1, seq_count)]
    beside_dp = [weight_product(0, j, both_grad) for j in range(1, couples)]
    up, down, left, right, act_parts, own, beside_seq, beside_dp = lax.optimization_barrier(
        (up, down, left, right, act_parts, own, beside_seq, beside_dp)
    )

    beside_seq = [
        lax.dynamic_update_slice(block, total([block[:, :half]] + came).astype(BF16), (0, 0))
        for block, came in zip(beside_seq, left)
    ]
    from_seq = reduce_rings([([None] + beside_seq, True)], "seq")[0][1:]
    for m in range(opposite - 1, 0, -1):
        block = act_parts[tensor_count - m]
        if up.shape[0] == rows:
            up = lax.dynamic_update_slice(block, total([block[:rows], up]).astype(BF16), (0, 0))
        else:
            up = total([block, up]).astype(BF16)
        block = act_parts[m]
        if down.shape[0] == rows:
            down = lax.dynamic_update_slice(
                block, total([block[rows:], down]).astype(BF16), (rows, 0)
            )
        else:
            down = total([block, down]).astype(BF16)
        up, down = shift(up, "tensor", 1), shift(down, "tensor", -1)
    beside_dp = [
        lax.dynamic_update_slice(block, total([block[:, half:]] + came).astype(BF16), (0, half))
        for block, came in zip(beside_dp, right)
    ]
    from_dp = reduce_rings([([None] + beside_dp, True)], "dp")[0][1:]

    weight_grad = summed([own] + from_seq + from_dp)
    arrived = swap(total([part[rows:] for part in (act_parts[0], up, down)]).astype(BF16))
    act_grad = assemble(after(core, weight_grad), act_parts[0], up, down, arrived, depth)
    return (act_grad, weight_grad, kv_grad)


def solution(mesh):
    in_specs = (
        P(("seq", "dp"), "tensor"),
        P(("seq", "dp"), "tensor"),
        P(("seq", "dp"), "tensor"),
        P(("seq", "dp"), None, None, "tensor"),
        P(("seq", "dp"), None),
        P(),
    )
    out_specs = (
        P(("seq", "dp"), "tensor"),
        P(("seq", "dp"), "tensor"),
        P(("seq", "dp"), None, None, "tensor"),
    )
    return jax.shard_map(
        on_device, mesh=mesh, in_specs=in_specs, out_specs=out_specs, check_vma=False
    )
```

```python
import functools

import jax
import jax.numpy as jnp
from jax import lax
from jax.experimental import pallas as pl
from jax.experimental.pallas import tpu as pltpu
from jax.sharding import PartitionSpec as P

HD = 128
SPAN = 64
KEYS = 256
F32 = jnp.float32
BF16 = jnp.bfloat16


def dot(a, b, contract):
    return lax.dot_general(a, b, (contract, ((), ())), preferred_element_type=F32)


def shift(value, axis, step=1):
    stride = 2 if axis == "dp" else 1
    size = lax.axis_size(axis)
    return lax.ppermute(value, axis, [(i, (i + step * stride) % size) for i in range(size)])


def swap(value):
    return lax.ppermute(value, "dp", [(i, i ^ 1) for i in range(lax.axis_size("dp"))])


def after(value, *others):
    return lax.optimization_barrier((value, *others))[0]


def reaches(size, far_up):
    up = size // 2 if far_up else (size - 1) // 2
    return up, size - 1 - up


def gather_ring(block, axis, size, rounds=None):
    blocks = [block] + [None] * (size - 1)
    for m in range(1, (size // 2 if rounds is None else rounds) + 1):
        came = {}
        for sign, count in zip((1, -1), reaches(size, True)):
            if m <= count:
                came[(sign * m) % size] = shift(blocks[(sign * (m - 1)) % size], axis, sign)
        for k, value in zip(came, lax.optimization_barrier(tuple(came.values()))):
            blocks[k] = value
    return blocks


def reduce_rings(streams, axis):
    size = len(streams[0][0])
    found = [[blocks[0]] for blocks, _ in streams]
    came = {}
    for m in range(1, size // 2 + 1):
        sent = {}
        for s, (blocks, far_up) in enumerate(streams):
            for sign, count in zip((1, -1), reaches(size, far_up)):
                if m <= count:
                    block = blocks[(-sign * (count - m + 1)) % size]
                    if m > 1:
                        block = came[s, sign].astype(F32) + block.astype(F32)
                    sent[s, sign] = shift(block.astype(BF16), axis, sign)
        came = dict(zip(sent, lax.optimization_barrier(tuple(sent.values()))))
        for (s, sign), block in came.items():
            if m == reaches(size, streams[s][1])[0 if sign == 1 else 1]:
                found[s].append(block)
    return found


def total(values):
    return functools.reduce(lambda a, b: a + b, [value.astype(F32) for value in values])


def product_kernel(count, start, table_ref, *refs):
    blocks, weight_ref, out_ref = refs[:count], refs[count], refs[count + 1]
    tile = min(256, out_ref.shape[1])
    for at in range(0, out_ref.shape[1], tile):
        total = None
        for k in range(count):
            weight = weight_ref[table_ref[k], :, start + at:start + at + tile]
            part = dot(blocks[k][...], weight, ((1,), (0,)))
            total = part if total is None else total + part
        out_ref[:, at:at + tile] = total


def product(blocks, weights, table, start, width):
    count, (rows, depth) = len(blocks), blocks[0].shape
    return pl.pallas_call(
        functools.partial(product_kernel, count, start),
        out_shape=jax.ShapeDtypeStruct((rows, width), F32),
        in_specs=[pl.BlockSpec(memory_space=pltpu.SMEM)]
        + [pl.BlockSpec(memory_space=pltpu.VMEM)] * (count + 1),
        out_specs=pl.BlockSpec(memory_space=pltpu.VMEM),
        compiler_params=pltpu.CompilerParams(vmem_limit_bytes=4 * 1024 * 1024),
        cost_estimate=pl.CostEstimate(
            flops=2 * rows * count * depth * width,
            bytes_accessed=2 * count * depth * (rows + width) + 4 * rows * width,
            transcendentals=0,
        ),
    )(table, *blocks, weights)


def attend_block(q_ref, g_ref, kv_ref, live_ref, dq_ref, grad_ref):
    pairs = q_ref.shape[-1] // HD // 2
    scale = HD ** (-0.5)
    live = live_ref[...] > 0.5
    zero = jnp.zeros((SPAN, HD), BF16)

    def diagonal(ref, start):
        one = ref[:, start:start + HD]
        two = ref[:, start + HD:start + 2 * HD]
        return jnp.concatenate(
            [jnp.concatenate([one, zero], axis=1), jnp.concatenate([zero, two], axis=1)], axis=0
        )

    def first(pair):
        start = pair * 2 * HD
        columns = slice(start, start + 2 * HD)
        scores = dot(kv_ref[0, :, columns], diagonal(q_ref, start), ((1,), (1,)))
        prob_grad = dot(kv_ref[1, :, columns], diagonal(g_ref, start), ((1,), (1,)))
        return scores, prob_grad

    ahead = first(0)
    for pair in range(pairs):
        scores, prob_grad = ahead
        if pair + 1 < pairs:
            ahead = first(pair + 1)
        start = pair * 2 * HD
        columns = slice(start, start + 2 * HD)
        scores = jnp.where(live, scores * scale, -1e30)
        expo = jnp.exp(scores - jnp.max(scores, axis=0, keepdims=True))
        probs = expo * (1.0 / jnp.sum(expo, axis=0, keepdims=True))
        center = jnp.sum(probs * prob_grad, axis=0, keepdims=True)
        score_grad = (probs * (prob_grad - center) * scale).astype(BF16)
        value_grad = dot(probs.astype(BF16), diagonal(g_ref, start), ((1,), (0,)))
        key_grad = dot(score_grad, diagonal(q_ref, start), ((1,), (0,)))
        both = dot(score_grad, kv_ref[0, :, columns], ((0,), (0,)))
        grad_ref[1, :, columns] = value_grad.astype(BF16)
        grad_ref[0, :, columns] = key_grad.astype(BF16)
        dq_ref[:, columns] = jnp.concatenate([both[:SPAN, :HD], both[SPAN:, HD:]], axis=1).astype(
            BF16
        )


def attend_kernel(table_ref, q_ref, g_ref, live_ref, kv_ref, *rest):
    dq_ref, grad_ref = rest[-2:]
    named = table_ref[pl.num_programs(0) + pl.program_id(0)]

    @pl.when(named == 0)
    def _():
        dq_ref[...] = jnp.zeros_like(dq_ref)
        grad_ref[...] = jnp.zeros_like(grad_ref)

    @pl.when(named != 0)
    def _():
        refs = (q_ref, g_ref, kv_ref, live_ref, dq_ref, grad_ref)
        attend_block(*(ref.at[0] for ref in refs))


def attend(place, named, source, queries, grads, kv, live, part, before):
    count, _, width = queries.shape
    capacity, keys, _ = live.shape
    heads = width // HD
    table = jnp.concatenate([place, named, source * count + place]).astype(jnp.int32)
    span_block = pl.BlockSpec((1, SPAN, width), lambda r, t: (r, 0, 0))
    part_block = pl.BlockSpec((1, SPAN, width), lambda r, t: (r, 0, part))
    live_block = pl.BlockSpec((1, keys, HD), lambda r, t: (t[2 * count + r], 0, 0))
    kv_block = pl.BlockSpec((1, 2, keys, width), lambda r, t: (t[r], 0, 0, 0))
    grad_block = pl.BlockSpec((1, 2, keys, width), lambda r, t: (t[2 * count + r], 0, 0, part))
    in_specs = [span_block, part_block, live_block, kv_block]
    operands = [table, queries, grads, live, kv]
    aliases = {}
    if before is not None:
        in_specs.append(pl.BlockSpec(memory_space=pl.ANY))
        operands.append(before)
        aliases = {len(operands) - 1: 1}
    return pl.pallas_call(
        attend_kernel,
        grid_spec=pltpu.PrefetchScalarGridSpec(
            num_scalar_prefetch=1,
            grid=(count,),
            in_specs=in_specs,
            out_specs=[span_block, grad_block],
        ),
        out_shape=[
            jax.ShapeDtypeStruct(queries.shape, BF16),
            jax.ShapeDtypeStruct((capacity, 2, keys, 2 * width), BF16),
        ],
        input_output_aliases=aliases,
        compiler_params=pltpu.CompilerParams(vmem_limit_bytes=6 * 1024 * 1024),
        cost_estimate=pl.CostEstimate(
            flops=count * heads * 5 * 2 * SPAN * keys * HD * 4,
            bytes_accessed=count * 4 * keys * width * 2,
            transcendentals=count * heads * SPAN * keys,
        ),
    )(*operands)


def stage_kernel(source_ref, kv_ref, left_ref, right_ref):
    width = left_ref.shape[-1]
    left_ref[...] = kv_ref[:, :, :, :width]
    right_ref[...] = kv_ref[:, :, :, width:]


def stage(kv, source, count):
    _, _, keys, width = kv.shape
    half_block = pl.BlockSpec((1, 2, keys, width // 2), lambda r, t: (r, 0, 0, 0))
    half_shape = jax.ShapeDtypeStruct((count, 2, keys, width // 2), kv.dtype)
    return pl.pallas_call(
        stage_kernel,
        grid_spec=pltpu.PrefetchScalarGridSpec(
            num_scalar_prefetch=1,
            grid=(count,),
            in_specs=[
                pl.BlockSpec((1, 2, keys, width), lambda r, t: (t[0] * count + r, 0, 0, 0))
            ],
            out_specs=[half_block, half_block],
        ),
        out_shape=[half_shape, half_shape],
        compiler_params=pltpu.CompilerParams(vmem_limit_bytes=8 * 1024 * 1024),
        cost_estimate=pl.CostEstimate(
            flops=0, bytes_accessed=8 * count * keys * width, transcendentals=0
        ),
    )(jnp.reshape(source, (1,)).astype(jnp.int32), kv)


def total_kernel(tile, *refs):
    out_ref, buf, sem = refs[-3:]
    copies = []
    for n in range(sem.shape[0]):
        some = pl.ds(n * tile, tile)
        buf[some] = total([ref[some] for ref in refs[:-3]])
        copies.append(pltpu.make_async_copy(buf.at[some], out_ref.at[some], sem.at[n]))
        copies[-1].start()
    for copy in copies:
        copy.wait()


def summed(values):
    rows, columns = values[0].shape
    tile = min(64, rows)
    return pl.pallas_call(
        functools.partial(total_kernel, tile),
        in_specs=[pl.BlockSpec(memory_space=pltpu.VMEM)] * len(values),
        out_specs=pl.BlockSpec(memory_space=pl.ANY),
        out_shape=jax.ShapeDtypeStruct((rows, columns), F32),
        scratch_shapes=[
            pltpu.VMEM((rows, columns), F32),
            pltpu.SemaphoreType.DMA((rows // tile,)),
        ],
        compiler_params=pltpu.CompilerParams(vmem_limit_bytes=6 * 1024 * 1024),
        cost_estimate=pl.CostEstimate(
            flops=len(values) * rows * columns,
            bytes_accessed=(2 * len(values) + 4) * rows * columns,
            transcendentals=0,
        ),
    )(*values)


def assemble_kernel(depth, core_ref, own_ref, up_ref, down_ref, arrived_ref, out_ref):
    kept = own_ref[...].astype(F32) + up_ref[...].astype(F32) + down_ref[...].astype(F32)
    kept = kept.astype(BF16)
    for p in range(kept.shape[1] // depth):
        columns = slice(p * depth, (p + 1) * depth)
        mine, other = 2 * p + core_ref[0], 2 * p + 1 - core_ref[0]
        out_ref[:, pl.ds(pl.multiple_of(mine * depth, depth), depth)] = kept[:, columns]
        out_ref[:, pl.ds(pl.multiple_of(other * depth, depth), depth)] = arrived_ref[:, columns]


def assemble(core, own, up, down, arrived, depth):
    rows, columns = arrived.shape
    tile = min(64, rows)
    block = pl.BlockSpec((tile, columns), lambda r: (r, 0))
    return pl.pallas_call(
        functools.partial(assemble_kernel, depth),
        grid=(rows // tile,),
        in_specs=[pl.BlockSpec(memory_space=pltpu.SMEM)] + [block] * 4,
        out_specs=pl.BlockSpec((tile, 2 * columns), lambda r: (r, 0)),
        out_shape=jax.ShapeDtypeStruct((rows, 2 * columns), BF16),
        compiler_params=pltpu.CompilerParams(vmem_limit_bytes=4 * 1024 * 1024),
        cost_estimate=pl.CostEstimate(
            flops=2 * rows * columns, bytes_accessed=12 * rows * columns, transcendentals=0
        ),
    )(jnp.reshape(core, (1,)).astype(jnp.int32), own, up, down, arrived)


def on_device(span_act, q_weight, out_grad, neighbour_kv, neighbour_ids, owner):
    rows, width = out_grad.shape
    depth = q_weight.shape[0]
    seq_count = lax.axis_size("seq")
    dp_count = lax.axis_size("dp")
    tensor_count = lax.axis_size("tensor")
    couples = dp_count // 2
    seq_at = lax.axis_index("seq")
    dp_at = lax.axis_index("dp")
    tensor_at = lax.axis_index("tensor")
    core = dp_at % 2
    spans = rows // SPAN
    capacity = neighbour_kv.shape[0]
    pairs = capacity // seq_count
    whole_blocks = pairs == spans
    per = span_act.shape[1] // depth // 2
    half = width // 2
    opposite = tensor_count // 2

    def columns_of(which):
        return jnp.concatenate(
            [
                lax.dynamic_slice(span_act, (0, (2 * p + which) * depth), (rows, depth))
                for p in range(per)
            ],
            axis=1,
        )

    act_both = jnp.concatenate([columns_of(core), swap(columns_of(1 - core))], axis=0)

    act_both, q_weight = lax.optimization_barrier((act_both, q_weight))
    acts = gather_ring(act_both, "tensor", tensor_count, opposite - 1)
    along_seq = gather_ring(q_weight, "seq", seq_count)
    along_dp = gather_ring(q_weight, "dp", couples)

    groups = owner.reshape(seq_count, dp_count, spans)
    groups = lax.dynamic_index_in_dim(groups, dp_at, 1, keepdims=False)
    mine = lax.dynamic_index_in_dim(groups, seq_at, 0, keepdims=False)

    def order(group, target):
        names = group == target
        at = jnp.arange(spans)
        ahead = (names[None, :] & ~names[:, None]) | (
            (names[None, :] == names[:, None]) & (at[None, :] < at[:, None])
        )
        return jnp.sum(ahead.astype(jnp.int32), axis=1), names.astype(jnp.int32)

    def message(target):
        place, names = order(mine, target)
        hit = place[None, :] == jnp.arange(pairs)[:, None]
        return hit & (names[None, :] == 1)

    def to_owner(value, step):
        value = value.reshape(spans, SPAN, -1)
        if not whole_blocks:
            hit = message((seq_at + step) % seq_count)
            value = jnp.sum(
                jnp.where(hit[:, :, None, None], value[None], jnp.zeros((), BF16)), axis=1
            )
        return shift(value, "seq", step) if step else value

    sources = [(seq_at - step) % seq_count for step in range(seq_count)]
    staged = [stage(neighbour_kv, source, pairs) for source in sources]
    near = [k for k in range(tensor_count) if k != opposite]
    cut = width * 5 // 8 // HD * HD
    left_from = [block[:, :cut] for block in along_seq[1:]]
    right_from = [block[:, cut:] for block in along_dp[1:]]
    left_from, right_from, found, staged = lax.optimization_barrier(
        (left_from, right_from, [acts[k] for k in near], staged)
    )
    acts = found[:opposite] + [None] + found[opposite:]

    corner_left = [gather_ring(block, "dp", couples) for block in left_from]
    corner_right = [gather_ring(block, "seq", seq_count) for block in right_from]
    up = shift(acts[opposite - 1][:rows], "tensor", 1)
    down = shift(acts[opposite + 1][rows:], "tensor", -1)
    acts[opposite] = jnp.concatenate([up, down], axis=0)
    grad_out = after(out_grad, corner_right)
    grads = [to_owner(grad_out, step) for step in range(seq_count)]
    depth_blocks = [(tensor_at - k) % tensor_count for k in range(tensor_count)]
    table = jnp.stack(depth_blocks).astype(jnp.int32)

    def block_at(i, j):
        block = ((seq_at - i) % seq_count) * dp_count + ((dp_at // 2 - j) % couples) * 2
        return block // (2 * per), (block % (2 * per)) // 2

    places = [(i, j) for i in range(seq_count) for j in range(couples)]
    weights = jnp.zeros((tensor_count, per * depth, width), BF16)
    for i, j in places:
        at, inner = block_at(i, j)
        if j == 0:
            pieces = [(along_seq[i], 0)]
        elif i == 0:
            pieces = [(along_dp[j], 0)]
        else:
            pieces = [(corner_left[i - 1][j], 0), (corner_right[j - 1][i], cut)]
        for piece, start in pieces:
            weights = lax.dynamic_update_slice(weights, piece[None], (at, inner * depth, start))

    def from_owner(value, step):
        value = shift(value, "seq", -step) if step else value
        if not whole_blocks:
            hit = message((seq_at + step) % seq_count)
            value = jnp.sum(
                jnp.where(hit[:, :, None, None], value[:, None], jnp.zeros((), BF16)), axis=0
            )
        return value.reshape(rows, -1)

    def slots_of(step):
        group = lax.dynamic_index_in_dim(groups, sources[step], 0, keepdims=False)
        place, names = order(group, seq_at)
        if not whole_blocks:
            place = jnp.arange(pairs)
            names = (place < jnp.sum(names)).astype(jnp.int32)
        return place, names, sources[step]

    live = jnp.broadcast_to((neighbour_ids != 0).astype(F32)[:, :, None], (capacity, KEYS, HD))
    slots = [slots_of(step) for step in range(seq_count)]

    queries = []
    for part in range(2):
        partial = product(acts, weights, table, part * half, half)
        arrived = swap(partial[rows:])
        if part:
            partial = after(partial, grads)
        queries.append((partial[:rows] + arrived).astype(BF16))
    asked = [[to_owner(value, step) for step in range(seq_count)] for value in queries]
    asked[0][0] = after(asked[0][0], queries[1])

    stacked = jnp.stack(after(acts, queries[1]))

    def act_block(i, j):
        at, inner = block_at(i, j)
        k = (tensor_at - at) % tensor_count
        return lax.dynamic_slice(stacked, (k, 0, inner * depth), (1, 2 * rows, depth))[0]

    def weight_product(i, j, grad):
        found = dot(act_block(i, j), grad, ((0,), (0,)))
        return lax.optimization_barrier(found.astype(BF16))

    kv_grad = None
    answers = [[None] * seq_count for _ in range(2)]
    calls = [(0, 0), (1, 0)] + [(part, step) for part in range(2) for step in range(1, seq_count)]
    for part, step in calls:
        answer, kv_grad = attend(
            *slots[step],
            asked[part][step],
            grads[step],
            staged[step][part],
            live,
            part,
            kv_grad,
        )
        answers[part][step] = from_owner(answer, step)

    far_weights = lax.dynamic_index_in_dim(weights, depth_blocks[opposite], 0, keepdims=False)
    far_weights = after(far_weights, queries[1])
    both_grads, corners = [], []
    corner_places = [(i, j) for i in range(1, seq_count) for j in range(1, couples)]
    for part in range(2):
        if part:
            answers[1][-1] = after(answers[1][-1], corners[0][corner_places[-1]])
        grad = sum(answers[part][1:], answers[part][0])
        both_grads.append(jnp.concatenate([grad, swap(grad)], axis=0))
        if part == 0:
            corners.append({at: weight_product(*at, both_grads[0]) for at in corner_places[::-1]})
    both_grad = jnp.concatenate(both_grads, axis=1)

    def act_product(k, block=None):
        if block is None:
            block = lax.dynamic_index_in_dim(weights, depth_blocks[k], 0, keepdims=False)
        return lax.optimization_barrier(dot(both_grad, block, ((1,), (1,))).astype(BF16))

    far = act_product(opposite, far_weights)
    up, down = shift(far[:rows], "tensor", 1), shift(far[rows:], "tensor", -1)

    late_grad = after(both_grads[1], far)
    corners.append({at: weight_product(*at, late_grad) for at in corner_places[::-1]})
    left = [
        reduce_rings([([None] + [corners[0][i, j] for j in range(1, couples)], True)], "dp")[0][1:]
        for i in range(1, seq_count)
    ]
    right = [
        reduce_rings([([None] + [corners[1][i, j] for i in range(1, seq_count)], True)], "seq")[0][1:]
        for j in range(1, couples)
    ]
    act_parts = {k: act_product(k) for k in range(tensor_count) if k != opposite}
    own = weight_product(0, 0, both_grad)
    beside_seq = [weight_product(i, 0, both_grad) for i in range(1, seq_count)]
    beside_dp = [weight_product(0, j, both_grad) for j in range(1, couples)]
    up, down, left, right, act_parts, own, beside_seq, beside_dp = lax.optimization_barrier(
        (up, down, left, right, act_parts, own, beside_seq, beside_dp)
    )

    beside_seq = [
        lax.dynamic_update_slice(block, total([block[:, :half]] + came).astype(BF16), (0, 0))
        for block, came in zip(beside_seq, left)
    ]
    from_seq = reduce_rings([([None] + beside_seq, True)], "seq")[0][1:]
    for m in range(opposite - 1, 0, -1):
        block = act_parts[tensor_count - m]
        if up.shape[0] == rows:
            up = lax.dynamic_update_slice(block, total([block[:rows], up]).astype(BF16), (0, 0))
        else:
            up = total([block, up]).astype(BF16)
        block = act_parts[m]
        if down.shape[0] == rows:
            down = lax.dynamic_update_slice(
                block, total([block[rows:], down]).astype(BF16), (rows, 0)
            )
        else:
            down = total([block, down]).astype(BF16)
        up, down = shift(up, "tensor", 1), shift(down, "tensor", -1)
    beside_dp = [
        lax.dynamic_update_slice(block, total([block[:, half:]] + came).astype(BF16), (0, half))
        for block, came in zip(beside_dp, right)
    ]
    from_dp = reduce_rings([([None] + beside_dp, True)], "dp")[0][1:]

    weight_grad = summed([own] + from_seq + from_dp)
    arrived = swap(total([part[rows:] for part in (act_parts[0], up, down)]).astype(BF16))
    act_grad = assemble(after(core, weight_grad), act_parts[0], up, down, arrived, depth)
    return (act_grad, weight_grad, kv_grad)


def solution(mesh):
    in_specs = (
        P(("seq", "dp"), "tensor"),
        P(("seq", "dp"), "tensor"),
        P(("seq", "dp"), "tensor"),
        P(("seq", "dp"), None, None, "tensor"),
        P(("seq", "dp"), None),
        P(),
    )
    out_specs = (
        P(("seq", "dp"), "tensor"),
        P(("seq", "dp"), "tensor"),
        P(("seq", "dp"), None, None, "tensor"),
    )
    return jax.shard_map(
        on_device, mesh=mesh, in_specs=in_specs, out_specs=out_specs, check_vma=False
    )
```

```python
import functools

import jax
import jax.numpy as jnp
from jax import lax
from jax.experimental import pallas as pl
from jax.experimental.pallas import tpu as pltpu
from jax.sharding import PartitionSpec as P

HD = 128
SPAN = 64
KEYS = 256
F32 = jnp.float32
BF16 = jnp.bfloat16


def dot(a, b, contract):
    return lax.dot_general(a, b, (contract, ((), ())), preferred_element_type=F32)


def shift(value, axis, step=1):
    stride = 2 if axis == "dp" else 1
    size = lax.axis_size(axis)
    return lax.ppermute(value, axis, [(i, (i + step * stride) % size) for i in range(size)])


def swap(value):
    return lax.ppermute(value, "dp", [(i, i ^ 1) for i in range(lax.axis_size("dp"))])


def after(value, *others):
    return lax.optimization_barrier((value, *others))[0]


def reaches(size, far_up):
    up = size // 2 if far_up else (size - 1) // 2
    return up, size - 1 - up


def gather_ring(block, axis, size, rounds=None):
    blocks = [block] + [None] * (size - 1)
    for m in range(1, (size // 2 if rounds is None else rounds) + 1):
        came = {}
        for sign, count in zip((1, -1), reaches(size, True)):
            if m <= count:
                came[(sign * m) % size] = shift(blocks[(sign * (m - 1)) % size], axis, sign)
        for k, value in zip(came, lax.optimization_barrier(tuple(came.values()))):
            blocks[k] = value
    return blocks


def reduce_rings(streams, axis):
    size = len(streams[0][0])
    found = [[blocks[0]] for blocks, _ in streams]
    came = {}
    for m in range(1, size // 2 + 1):
        sent = {}
        for s, (blocks, far_up) in enumerate(streams):
            for sign, count in zip((1, -1), reaches(size, far_up)):
                if m <= count:
                    block = blocks[(-sign * (count - m + 1)) % size]
                    if m > 1:
                        block = came[s, sign].astype(F32) + block.astype(F32)
                    sent[s, sign] = shift(block.astype(BF16), axis, sign)
        came = dict(zip(sent, lax.optimization_barrier(tuple(sent.values()))))
        for (s, sign), block in came.items():
            if m == reaches(size, streams[s][1])[0 if sign == 1 else 1]:
                found[s].append(block)
    return found


def total(values):
    return functools.reduce(lambda a, b: a + b, [value.astype(F32) for value in values])


def product_kernel(count, start, table_ref, *refs):
    blocks, weight_ref, out_ref = refs[:count], refs[count], refs[count + 1]
    tile = min(256, out_ref.shape[1])
    for at in range(0, out_ref.shape[1], tile):
        total = None
        for k in range(count):
            weight = weight_ref[table_ref[k], :, start + at:start + at + tile]
            part = dot(blocks[k][...], weight, ((1,), (0,)))
            total = part if total is None else total + part
        out_ref[:, at:at + tile] = total


def product(blocks, weights, table, start, width):
    count, (rows, depth) = len(blocks), blocks[0].shape
    return pl.pallas_call(
        functools.partial(product_kernel, count, start),
        out_shape=jax.ShapeDtypeStruct((rows, width), F32),
        in_specs=[pl.BlockSpec(memory_space=pltpu.SMEM)]
        + [pl.BlockSpec(memory_space=pltpu.VMEM)] * (count + 1),
        out_specs=pl.BlockSpec(memory_space=pltpu.VMEM),
        compiler_params=pltpu.CompilerParams(vmem_limit_bytes=4 * 1024 * 1024),
        cost_estimate=pl.CostEstimate(
            flops=2 * rows * count * depth * width,
            bytes_accessed=2 * count * depth * (rows + width) + 4 * rows * width,
            transcendentals=0,
        ),
    )(table, *blocks, weights)


def attend_block(q_ref, g_ref, kv_ref, live_ref, dq_ref, grad_ref):
    pairs = q_ref.shape[-1] // HD // 2
    scale = HD ** (-0.5)
    live = live_ref[...] > 0.5
    zero = jnp.zeros((SPAN, HD), BF16)

    def diagonal(ref, start):
        one = ref[:, start:start + HD]
        two = ref[:, start + HD:start + 2 * HD]
        return jnp.concatenate(
            [jnp.concatenate([one, zero], axis=1), jnp.concatenate([zero, two], axis=1)], axis=0
        )

    def first(pair):
        start = pair * 2 * HD
        columns = slice(start, start + 2 * HD)
        scores = dot(kv_ref[0, :, columns], diagonal(q_ref, start), ((1,), (1,)))
        prob_grad = dot(kv_ref[1, :, columns], diagonal(g_ref, start), ((1,), (1,)))
        return scores, prob_grad

    ahead = first(0)
    for pair in range(pairs):
        scores, prob_grad = ahead
        if pair + 1 < pairs:
            ahead = first(pair + 1)
        start = pair * 2 * HD
        columns = slice(start, start + 2 * HD)
        scores = jnp.where(live, scores * scale, -1e30)
        expo = jnp.exp(scores - jnp.max(scores, axis=0, keepdims=True))
        probs = expo * (1.0 / jnp.sum(expo, axis=0, keepdims=True))
        center = jnp.sum(probs * prob_grad, axis=0, keepdims=True)
        score_grad = (probs * (prob_grad - center) * scale).astype(BF16)
        value_grad = dot(probs.astype(BF16), diagonal(g_ref, start), ((1,), (0,)))
        key_grad = dot(score_grad, diagonal(q_ref, start), ((1,), (0,)))
        both = dot(score_grad, kv_ref[0, :, columns], ((0,), (0,)))
        grad_ref[1, :, columns] = value_grad.astype(BF16)
        grad_ref[0, :, columns] = key_grad.astype(BF16)
        dq_ref[:, columns] = jnp.concatenate([both[:SPAN, :HD], both[SPAN:, HD:]], axis=1).astype(
            BF16
        )


def attend_kernel(table_ref, q_ref, g_ref, live_ref, kv_ref, *rest):
    dq_ref, grad_ref = rest[-2:]
    named = table_ref[pl.num_programs(0) + pl.program_id(0)]

    @pl.when(named == 0)
    def _():
        dq_ref[...] = jnp.zeros_like(dq_ref)
        grad_ref[...] = jnp.zeros_like(grad_ref)

    @pl.when(named != 0)
    def _():
        refs = (q_ref, g_ref, kv_ref, live_ref, dq_ref, grad_ref)
        attend_block(*(ref.at[0] for ref in refs))


def attend(place, named, source, queries, grads, kv, live, part, before):
    count, _, width = queries.shape
    capacity, keys, _ = live.shape
    heads = width // HD
    table = jnp.concatenate([place, named, source * count + place]).astype(jnp.int32)
    span_block = pl.BlockSpec((1, SPAN, width), lambda r, t: (r, 0, 0))
    live_block = pl.BlockSpec((1, keys, HD), lambda r, t: (t[2 * count + r], 0, 0))
    kv_block = pl.BlockSpec((1, 2, keys, width), lambda r, t: (t[r], 0, 0, 0))
    grad_block = pl.BlockSpec((1, 2, keys, width), lambda r, t: (t[2 * count + r], 0, 0, part))
    in_specs = [span_block, span_block, live_block, kv_block]
    operands = [table, queries, grads, live, kv]
    aliases = {}
    if before is not None:
        in_specs.append(pl.BlockSpec(memory_space=pl.ANY))
        operands.append(before)
        aliases = {len(operands) - 1: 1}
    return pl.pallas_call(
        attend_kernel,
        grid_spec=pltpu.PrefetchScalarGridSpec(
            num_scalar_prefetch=1,
            grid=(count,),
            in_specs=in_specs,
            out_specs=[span_block, grad_block],
        ),
        out_shape=[
            jax.ShapeDtypeStruct(queries.shape, BF16),
            jax.ShapeDtypeStruct((capacity, 2, keys, 2 * width), BF16),
        ],
        input_output_aliases=aliases,
        compiler_params=pltpu.CompilerParams(vmem_limit_bytes=6 * 1024 * 1024),
        cost_estimate=pl.CostEstimate(
            flops=count * heads * 5 * 2 * SPAN * keys * HD * 4,
            bytes_accessed=count * 4 * keys * width * 2,
            transcendentals=count * heads * SPAN * keys,
        ),
    )(*operands)


def stage_kernel(source_ref, kv_ref, left_ref, right_ref):
    width = left_ref.shape[-1]
    left_ref[...] = kv_ref[:, :, :, :width]
    right_ref[...] = kv_ref[:, :, :, width:]


def stage(kv, source, count):
    _, _, keys, width = kv.shape
    half_block = pl.BlockSpec((1, 2, keys, width // 2), lambda r, t: (r, 0, 0, 0))
    half_shape = jax.ShapeDtypeStruct((count, 2, keys, width // 2), kv.dtype)
    return pl.pallas_call(
        stage_kernel,
        grid_spec=pltpu.PrefetchScalarGridSpec(
            num_scalar_prefetch=1,
            grid=(count,),
            in_specs=[
                pl.BlockSpec((1, 2, keys, width), lambda r, t: (t[0] * count + r, 0, 0, 0))
            ],
            out_specs=[half_block, half_block],
        ),
        out_shape=[half_shape, half_shape],
        compiler_params=pltpu.CompilerParams(vmem_limit_bytes=8 * 1024 * 1024),
        cost_estimate=pl.CostEstimate(
            flops=0, bytes_accessed=8 * count * keys * width, transcendentals=0
        ),
    )(jnp.reshape(source, (1,)).astype(jnp.int32), kv)


def total_kernel(tile, *refs):
    out_ref, buf, sem = refs[-3:]
    copies = []
    for n in range(sem.shape[0]):
        some = pl.ds(n * tile, tile)
        buf[some] = total([ref[some] for ref in refs[:-3]])
        copies.append(pltpu.make_async_copy(buf.at[some], out_ref.at[some], sem.at[n]))
        copies[-1].start()
    for copy in copies:
        copy.wait()


def summed(values):
    rows, columns = values[0].shape
    tile = min(64, rows)
    return pl.pallas_call(
        functools.partial(total_kernel, tile),
        in_specs=[pl.BlockSpec(memory_space=pltpu.VMEM)] * len(values),
        out_specs=pl.BlockSpec(memory_space=pl.ANY),
        out_shape=jax.ShapeDtypeStruct((rows, columns), F32),
        scratch_shapes=[
            pltpu.VMEM((rows, columns), F32),
            pltpu.SemaphoreType.DMA((rows // tile,)),
        ],
        compiler_params=pltpu.CompilerParams(vmem_limit_bytes=6 * 1024 * 1024),
        cost_estimate=pl.CostEstimate(
            flops=len(values) * rows * columns,
            bytes_accessed=(2 * len(values) + 4) * rows * columns,
            transcendentals=0,
        ),
    )(*values)


def assemble_kernel(depth, core_ref, own_ref, up_ref, down_ref, arrived_ref, out_ref):
    kept = own_ref[...].astype(F32) + up_ref[...].astype(F32) + down_ref[...].astype(F32)
    kept = kept.astype(BF16)
    for p in range(kept.shape[1] // depth):
        columns = slice(p * depth, (p + 1) * depth)
        mine, other = 2 * p + core_ref[0], 2 * p + 1 - core_ref[0]
        out_ref[:, pl.ds(pl.multiple_of(mine * depth, depth), depth)] = kept[:, columns]
        out_ref[:, pl.ds(pl.multiple_of(other * depth, depth), depth)] = arrived_ref[:, columns]


def assemble(core, own, up, down, arrived, depth):
    rows, columns = arrived.shape
    tile = min(64, rows)
    block = pl.BlockSpec((tile, columns), lambda r: (r, 0))
    return pl.pallas_call(
        functools.partial(assemble_kernel, depth),
        grid=(rows // tile,),
        in_specs=[pl.BlockSpec(memory_space=pltpu.SMEM)] + [block] * 4,
        out_specs=pl.BlockSpec((tile, 2 * columns), lambda r: (r, 0)),
        out_shape=jax.ShapeDtypeStruct((rows, 2 * columns), BF16),
        compiler_params=pltpu.CompilerParams(vmem_limit_bytes=4 * 1024 * 1024),
        cost_estimate=pl.CostEstimate(
            flops=2 * rows * columns, bytes_accessed=12 * rows * columns, transcendentals=0
        ),
    )(jnp.reshape(core, (1,)).astype(jnp.int32), own, up, down, arrived)


def on_device(span_act, q_weight, out_grad, neighbour_kv, neighbour_ids, owner):
    rows, width = out_grad.shape
    depth = q_weight.shape[0]
    seq_count = lax.axis_size("seq")
    dp_count = lax.axis_size("dp")
    tensor_count = lax.axis_size("tensor")
    couples = dp_count // 2
    seq_at = lax.axis_index("seq")
    dp_at = lax.axis_index("dp")
    tensor_at = lax.axis_index("tensor")
    core = dp_at % 2
    spans = rows // SPAN
    capacity = neighbour_kv.shape[0]
    pairs = capacity // seq_count
    whole_blocks = pairs == spans
    per = span_act.shape[1] // depth // 2
    half = width // 2
    opposite = tensor_count // 2

    def columns_of(which):
        return jnp.concatenate(
            [
                lax.dynamic_slice(span_act, (0, (2 * p + which) * depth), (rows, depth))
                for p in range(per)
            ],
            axis=1,
        )

    act_both = jnp.concatenate([columns_of(core), swap(columns_of(1 - core))], axis=0)

    act_both, q_weight = lax.optimization_barrier((act_both, q_weight))
    acts = gather_ring(act_both, "tensor", tensor_count, opposite - 1)
    along_seq = gather_ring(q_weight, "seq", seq_count)
    along_dp = gather_ring(q_weight, "dp", couples)

    groups = owner.reshape(seq_count, dp_count, spans)
    groups = lax.dynamic_index_in_dim(groups, dp_at, 1, keepdims=False)
    mine = lax.dynamic_index_in_dim(groups, seq_at, 0, keepdims=False)

    def order(group, target):
        names = group == target
        at = jnp.arange(spans)
        ahead = (names[None, :] & ~names[:, None]) | (
            (names[None, :] == names[:, None]) & (at[None, :] < at[:, None])
        )
        return jnp.sum(ahead.astype(jnp.int32), axis=1), names.astype(jnp.int32)

    def message(target):
        place, names = order(mine, target)
        hit = place[None, :] == jnp.arange(pairs)[:, None]
        return hit & (names[None, :] == 1)

    def to_owner(value, step):
        value = value.reshape(spans, SPAN, -1)
        if not whole_blocks:
            hit = message((seq_at + step) % seq_count)
            value = jnp.sum(
                jnp.where(hit[:, :, None, None], value[None], jnp.zeros((), BF16)), axis=1
            )
        return shift(value, "seq", step) if step else value

    sources = [(seq_at - step) % seq_count for step in range(seq_count)]
    staged = [stage(neighbour_kv, source, pairs) for source in sources]
    near = [k for k in range(tensor_count) if k != opposite]
    cut = width * 5 // 8 // HD * HD
    left_from = [block[:, :cut] for block in along_seq[1:]]
    right_from = [block[:, cut:] for block in along_dp[1:]]
    grads = [[to_owner(out_grad[:, :half], step) for step in range(seq_count)]]
    left_from, right_from, found, staged, grads = lax.optimization_barrier(
        (left_from, right_from, [acts[k] for k in near], staged, grads)
    )
    acts = found[:opposite] + [None] + found[opposite:]

    corner_left = [gather_ring(block, "dp", couples) for block in left_from]
    corner_right = [gather_ring(block, "seq", seq_count) for block in right_from]
    up = shift(acts[opposite - 1][:rows], "tensor", 1)
    down = shift(acts[opposite + 1][rows:], "tensor", -1)
    acts[opposite] = jnp.concatenate([up, down], axis=0)
    grad_out = after(out_grad[:, half:], corner_right)
    grads.append([to_owner(grad_out, step) for step in range(seq_count)])
    depth_blocks = [(tensor_at - k) % tensor_count for k in range(tensor_count)]
    table = jnp.stack(depth_blocks).astype(jnp.int32)

    def block_at(i, j):
        block = ((seq_at - i) % seq_count) * dp_count + ((dp_at // 2 - j) % couples) * 2
        return block // (2 * per), (block % (2 * per)) // 2

    places = [(i, j) for i in range(seq_count) for j in range(couples)]
    weights = jnp.zeros((tensor_count, per * depth, width), BF16)
    for i, j in places:
        at, inner = block_at(i, j)
        if j == 0:
            pieces = [(along_seq[i], 0)]
        elif i == 0:
            pieces = [(along_dp[j], 0)]
        else:
            pieces = [(corner_left[i - 1][j], 0), (corner_right[j - 1][i], cut)]
        for piece, start in pieces:
            weights = lax.dynamic_update_slice(weights, piece[None], (at, inner * depth, start))

    def from_owner(value, step):
        value = shift(value, "seq", -step) if step else value
        if not whole_blocks:
            hit = message((seq_at + step) % seq_count)
            value = jnp.sum(
                jnp.where(hit[:, :, None, None], value[:, None], jnp.zeros((), BF16)), axis=0
            )
        return value.reshape(rows, -1)

    def slots_of(step):
        group = lax.dynamic_index_in_dim(groups, sources[step], 0, keepdims=False)
        place, names = order(group, seq_at)
        if not whole_blocks:
            place = jnp.arange(pairs)
            names = (place < jnp.sum(names)).astype(jnp.int32)
        return place, names, sources[step]

    live = jnp.broadcast_to((neighbour_ids != 0).astype(F32)[:, :, None], (capacity, KEYS, HD))
    slots = [slots_of(step) for step in range(seq_count)]

    queries = []
    for part in range(2):
        partial = product(acts, weights, table, part * half, half)
        arrived = swap(partial[rows:])
        if part:
            partial = after(partial, grads[1])
        queries.append((partial[:rows] + arrived).astype(BF16))
    asked = [[to_owner(value, step) for step in range(seq_count)] for value in queries]
    asked[0][0] = after(asked[0][0], queries[1])

    stacked = jnp.stack(after(acts, queries[1]))

    def act_block(i, j):
        at, inner = block_at(i, j)
        k = (tensor_at - at) % tensor_count
        return lax.dynamic_slice(stacked, (k, 0, inner * depth), (1, 2 * rows, depth))[0]

    def weight_product(i, j, grad):
        found = dot(act_block(i, j), grad, ((0,), (0,)))
        return lax.optimization_barrier(found.astype(BF16))

    kv_grad = None
    answers = [[None] * seq_count for _ in range(2)]
    calls = [(0, 0), (1, 0)] + [(part, step) for part in range(2) for step in range(1, seq_count)]
    for part, step in calls:
        answer, kv_grad = attend(
            *slots[step],
            asked[part][step],
            grads[part][step],
            staged[step][part],
            live,
            part,
            kv_grad,
        )
        answers[part][step] = from_owner(answer, step)

    far_weights = lax.dynamic_index_in_dim(weights, depth_blocks[opposite], 0, keepdims=False)
    far_weights = after(far_weights, queries[1])
    both_grads, corners = [], []
    corner_places = [(i, j) for i in range(1, seq_count) for j in range(1, couples)]
    for part in range(2):
        if part:
            answers[1][-1] = after(answers[1][-1], corners[0][corner_places[-1]])
        grad = sum(answers[part][1:], answers[part][0])
        both_grads.append(jnp.concatenate([grad, swap(grad)], axis=0))
        if part == 0:
            corners.append({at: weight_product(*at, both_grads[0]) for at in corner_places[::-1]})
    both_grad = jnp.concatenate(both_grads, axis=1)

    def act_product(k, block=None):
        if block is None:
            block = lax.dynamic_index_in_dim(weights, depth_blocks[k], 0, keepdims=False)
        return lax.optimization_barrier(dot(both_grad, block, ((1,), (1,))).astype(BF16))

    far = act_product(opposite, far_weights)
    up, down = shift(far[:rows], "tensor", 1), shift(far[rows:], "tensor", -1)

    late_grad = after(both_grads[1], far)
    corners.append({at: weight_product(*at, late_grad) for at in corner_places[::-1]})
    left = [
        reduce_rings([([None] + [corners[0][i, j] for j in range(1, couples)], True)], "dp")[0][1:]
        for i in range(1, seq_count)
    ]
    right = [
        reduce_rings([([None] + [corners[1][i, j] for i in range(1, seq_count)], True)], "seq")[0][1:]
        for j in range(1, couples)
    ]
    act_parts = {k: act_product(k) for k in range(tensor_count) if k != opposite}
    own = weight_product(0, 0, both_grad)
    beside_seq = [weight_product(i, 0, both_grad) for i in range(1, seq_count)]
    beside_dp = [weight_product(0, j, both_grad) for j in range(1, couples)]
    up, down, left, right, act_parts, own, beside_seq, beside_dp = lax.optimization_barrier(
        (up, down, left, right, act_parts, own, beside_seq, beside_dp)
    )

    beside_seq = [
        lax.dynamic_update_slice(block, total([block[:, :half]] + came).astype(BF16), (0, 0))
        for block, came in zip(beside_seq, left)
    ]
    from_seq = reduce_rings([([None] + beside_seq, True)], "seq")[0][1:]
    for m in range(opposite - 1, 0, -1):
        block = act_parts[tensor_count - m]
        if up.shape[0] == rows:
            up = lax.dynamic_update_slice(block, total([block[:rows], up]).astype(BF16), (0, 0))
        else:
            up = total([block, up]).astype(BF16)
        block = act_parts[m]
        if down.shape[0] == rows:
            down = lax.dynamic_update_slice(
                block, total([block[rows:], down]).astype(BF16), (rows, 0)
            )
        else:
            down = total([block, down]).astype(BF16)
        up, down = shift(up, "tensor", 1), shift(down, "tensor", -1)
    beside_dp = [
        lax.dynamic_update_slice(block, total([block[:, half:]] + came).astype(BF16), (0, half))
        for block, came in zip(beside_dp, right)
    ]
    from_dp = reduce_rings([([None] + beside_dp, True)], "dp")[0][1:]

    weight_grad = summed([own] + from_seq + from_dp)
    arrived = swap(total([part[rows:] for part in (act_parts[0], up, down)]).astype(BF16))
    act_grad = assemble(after(core, weight_grad), act_parts[0], up, down, arrived, depth)
    return (act_grad, weight_grad, kv_grad)


def solution(mesh):
    in_specs = (
        P(("seq", "dp"), "tensor"),
        P(("seq", "dp"), "tensor"),
        P(("seq", "dp"), "tensor"),
        P(("seq", "dp"), None, None, "tensor"),
        P(("seq", "dp"), None),
        P(),
    )
    out_specs = (
        P(("seq", "dp"), "tensor"),
        P(("seq", "dp"), "tensor"),
        P(("seq", "dp"), None, None, "tensor"),
    )
    return jax.shard_map(
        on_device, mesh=mesh, in_specs=in_specs, out_specs=out_specs, check_vma=False
    )
```

```python
import functools

import jax
import jax.numpy as jnp
from jax import lax
from jax.experimental import pallas as pl
from jax.experimental.pallas import tpu as pltpu
from jax.sharding import PartitionSpec as P

HD = 128
SPAN = 64
KEYS = 256
F32 = jnp.float32
BF16 = jnp.bfloat16


def dot(a, b, contract):
    return lax.dot_general(a, b, (contract, ((), ())), preferred_element_type=F32)


def shift(value, axis, step=1):
    stride = 2 if axis == "dp" else 1
    size = lax.axis_size(axis)
    return lax.ppermute(value, axis, [(i, (i + step * stride) % size) for i in range(size)])


def swap(value):
    return lax.ppermute(value, "dp", [(i, i ^ 1) for i in range(lax.axis_size("dp"))])


def after(value, *others):
    return lax.optimization_barrier((value, *others))[0]


def reaches(size, far_up):
    up = size // 2 if far_up else (size - 1) // 2
    return up, size - 1 - up


def gather_ring(block, axis, size, rounds=None):
    blocks = [block] + [None] * (size - 1)
    for m in range(1, (size // 2 if rounds is None else rounds) + 1):
        came = {}
        for sign, count in zip((1, -1), reaches(size, True)):
            if m <= count:
                came[(sign * m) % size] = shift(blocks[(sign * (m - 1)) % size], axis, sign)
        for k, value in zip(came, lax.optimization_barrier(tuple(came.values()))):
            blocks[k] = value
    return blocks


def reduce_rings(streams, axis):
    size = len(streams[0][0])
    found = [[blocks[0]] for blocks, _ in streams]
    came = {}
    for m in range(1, size // 2 + 1):
        sent = {}
        for s, (blocks, far_up) in enumerate(streams):
            for sign, count in zip((1, -1), reaches(size, far_up)):
                if m <= count:
                    block = blocks[(-sign * (count - m + 1)) % size]
                    if m > 1:
                        block = came[s, sign].astype(F32) + block.astype(F32)
                    sent[s, sign] = shift(block.astype(BF16), axis, sign)
        came = dict(zip(sent, lax.optimization_barrier(tuple(sent.values()))))
        for (s, sign), block in came.items():
            if m == reaches(size, streams[s][1])[0 if sign == 1 else 1]:
                found[s].append(block)
    return found


def total(values):
    return functools.reduce(lambda a, b: a + b, [value.astype(F32) for value in values])


def product_kernel(count, start, table_ref, *refs):
    blocks, weight_ref, out_ref = refs[:count], refs[count], refs[count + 1]
    tile = min(256, out_ref.shape[1])
    for at in range(0, out_ref.shape[1], tile):
        total = None
        for k in range(count):
            weight = weight_ref[table_ref[k], :, start + at:start + at + tile]
            part = dot(blocks[k][...], weight, ((1,), (0,)))
            total = part if total is None else total + part
        out_ref[:, at:at + tile] = total


def product(blocks, weights, table, start, width):
    count, (rows, depth) = len(blocks), blocks[0].shape
    return pl.pallas_call(
        functools.partial(product_kernel, count, start),
        out_shape=jax.ShapeDtypeStruct((rows, width), F32),
        in_specs=[pl.BlockSpec(memory_space=pltpu.SMEM)]
        + [pl.BlockSpec(memory_space=pltpu.VMEM)] * (count + 1),
        out_specs=pl.BlockSpec(memory_space=pltpu.VMEM),
        compiler_params=pltpu.CompilerParams(vmem_limit_bytes=4 * 1024 * 1024),
        cost_estimate=pl.CostEstimate(
            flops=2 * rows * count * depth * width,
            bytes_accessed=2 * count * depth * (rows + width) + 4 * rows * width,
            transcendentals=0,
        ),
    )(table, *blocks, weights)


def attend_block(q_ref, g_ref, kv_ref, live_ref, dq_ref, grad_ref):
    pairs = q_ref.shape[-1] // HD // 2
    scale = HD ** (-0.5)
    live = live_ref[...] > 0.5
    zero = jnp.zeros((SPAN, HD), BF16)

    def diagonal(ref, start):
        one = ref[:, start:start + HD]
        two = ref[:, start + HD:start + 2 * HD]
        return jnp.concatenate(
            [jnp.concatenate([one, zero], axis=1), jnp.concatenate([zero, two], axis=1)], axis=0
        )

    def first(pair):
        start = pair * 2 * HD
        columns = slice(start, start + 2 * HD)
        scores = dot(kv_ref[0, :, columns], diagonal(q_ref, start), ((1,), (1,)))
        prob_grad = dot(kv_ref[1, :, columns], diagonal(g_ref, start), ((1,), (1,)))
        return scores, prob_grad

    ahead = first(0)
    for pair in range(pairs):
        scores, prob_grad = ahead
        if pair + 1 < pairs:
            ahead = first(pair + 1)
        start = pair * 2 * HD
        columns = slice(start, start + 2 * HD)
        scores = jnp.where(live, scores * scale, -1e30)
        expo = jnp.exp(scores - jnp.max(scores, axis=0, keepdims=True))
        probs = expo * (1.0 / jnp.sum(expo, axis=0, keepdims=True))
        center = jnp.sum(probs * prob_grad, axis=0, keepdims=True)
        score_grad = (probs * (prob_grad - center) * scale).astype(BF16)
        value_grad = dot(probs.astype(BF16), diagonal(g_ref, start), ((1,), (0,)))
        key_grad = dot(score_grad, diagonal(q_ref, start), ((1,), (0,)))
        both = dot(score_grad, kv_ref[0, :, columns], ((0,), (0,)))
        grad_ref[1, :, columns] = value_grad.astype(BF16)
        grad_ref[0, :, columns] = key_grad.astype(BF16)
        dq_ref[:, columns] = jnp.concatenate([both[:SPAN, :HD], both[SPAN:, HD:]], axis=1).astype(
            BF16
        )


def attend_kernel(table_ref, q_ref, g_ref, live_ref, kv_ref, *rest):
    dq_ref, grad_ref = rest[-2:]
    named = table_ref[pl.num_programs(0) + pl.program_id(0)]

    @pl.when(named == 0)
    def _():
        dq_ref[...] = jnp.zeros_like(dq_ref)
        grad_ref[...] = jnp.zeros_like(grad_ref)

    @pl.when(named != 0)
    def _():
        refs = (q_ref, g_ref, kv_ref, live_ref, dq_ref, grad_ref)
        attend_block(*(ref.at[0] for ref in refs))


def attend(place, named, source, queries, grads, kv, live, part, before):
    count, _, width = queries.shape
    capacity, keys, _ = live.shape
    heads = width // HD
    table = jnp.concatenate([place, named, source * count + place]).astype(jnp.int32)
    span_block = pl.BlockSpec((1, SPAN, width), lambda r, t: (r, 0, 0))
    live_block = pl.BlockSpec((1, keys, HD), lambda r, t: (t[2 * count + r], 0, 0))
    kv_block = pl.BlockSpec((1, 2, keys, width), lambda r, t: (t[r], 0, 0, 0))
    grad_block = pl.BlockSpec((1, 2, keys, width), lambda r, t: (t[2 * count + r], 0, 0, part))
    in_specs = [span_block, span_block, live_block, kv_block]
    operands = [table, queries, grads, live, kv]
    aliases = {}
    if before is not None:
        in_specs.append(pl.BlockSpec(memory_space=pl.ANY))
        operands.append(before)
        aliases = {len(operands) - 1: 1}
    return pl.pallas_call(
        attend_kernel,
        grid_spec=pltpu.PrefetchScalarGridSpec(
            num_scalar_prefetch=1,
            grid=(count,),
            in_specs=in_specs,
            out_specs=[span_block, grad_block],
        ),
        out_shape=[
            jax.ShapeDtypeStruct(queries.shape, BF16),
            jax.ShapeDtypeStruct((capacity, 2, keys, 2 * width), BF16),
        ],
        input_output_aliases=aliases,
        compiler_params=pltpu.CompilerParams(vmem_limit_bytes=6 * 1024 * 1024),
        cost_estimate=pl.CostEstimate(
            flops=count * heads * 5 * 2 * SPAN * keys * HD * 4,
            bytes_accessed=count * 4 * keys * width * 2,
            transcendentals=count * heads * SPAN * keys,
        ),
    )(*operands)


def stage_kernel(source_ref, kv_ref, left_ref, right_ref):
    width = left_ref.shape[-1]
    left_ref[...] = kv_ref[:, :, :, :width]
    right_ref[...] = kv_ref[:, :, :, width:]


def stage(kv, source, count):
    _, _, keys, width = kv.shape
    half_block = pl.BlockSpec((1, 2, keys, width // 2), lambda r, t: (r, 0, 0, 0))
    half_shape = jax.ShapeDtypeStruct((count, 2, keys, width // 2), kv.dtype)
    return pl.pallas_call(
        stage_kernel,
        grid_spec=pltpu.PrefetchScalarGridSpec(
            num_scalar_prefetch=1,
            grid=(count,),
            in_specs=[
                pl.BlockSpec((1, 2, keys, width), lambda r, t: (t[0] * count + r, 0, 0, 0))
            ],
            out_specs=[half_block, half_block],
        ),
        out_shape=[half_shape, half_shape],
        compiler_params=pltpu.CompilerParams(vmem_limit_bytes=8 * 1024 * 1024),
        cost_estimate=pl.CostEstimate(
            flops=0, bytes_accessed=8 * count * keys * width, transcendentals=0
        ),
    )(jnp.reshape(source, (1,)).astype(jnp.int32), kv)


def total_kernel(tile, *refs):
    out_ref, buf, sem = refs[-3:]
    copies = []
    for n in range(sem.shape[0]):
        some = pl.ds(n * tile, tile)
        buf[some] = total([ref[some] for ref in refs[:-3]])
        copies.append(pltpu.make_async_copy(buf.at[some], out_ref.at[some], sem.at[n]))
        copies[-1].start()
    for copy in copies:
        copy.wait()


def summed(values):
    rows, columns = values[0].shape
    tile = min(64, rows)
    return pl.pallas_call(
        functools.partial(total_kernel, tile),
        in_specs=[pl.BlockSpec(memory_space=pltpu.VMEM)] * len(values),
        out_specs=pl.BlockSpec(memory_space=pl.ANY),
        out_shape=jax.ShapeDtypeStruct((rows, columns), F32),
        scratch_shapes=[
            pltpu.VMEM((rows, columns), F32),
            pltpu.SemaphoreType.DMA((rows // tile,)),
        ],
        compiler_params=pltpu.CompilerParams(vmem_limit_bytes=6 * 1024 * 1024),
        cost_estimate=pl.CostEstimate(
            flops=len(values) * rows * columns,
            bytes_accessed=(2 * len(values) + 4) * rows * columns,
            transcendentals=0,
        ),
    )(*values)


def assemble_kernel(depth, core_ref, own_ref, up_ref, down_ref, arrived_ref, out_ref):
    kept = own_ref[...].astype(F32) + up_ref[...].astype(F32) + down_ref[...].astype(F32)
    kept = kept.astype(BF16)
    for p in range(kept.shape[1] // depth):
        columns = slice(p * depth, (p + 1) * depth)
        mine, other = 2 * p + core_ref[0], 2 * p + 1 - core_ref[0]
        out_ref[:, pl.ds(pl.multiple_of(mine * depth, depth), depth)] = kept[:, columns]
        out_ref[:, pl.ds(pl.multiple_of(other * depth, depth), depth)] = arrived_ref[:, columns]


def assemble(core, own, up, down, arrived, depth):
    rows, columns = arrived.shape
    tile = min(64, rows)
    block = pl.BlockSpec((tile, columns), lambda r: (r, 0))
    return pl.pallas_call(
        functools.partial(assemble_kernel, depth),
        grid=(rows // tile,),
        in_specs=[pl.BlockSpec(memory_space=pltpu.SMEM)] + [block] * 4,
        out_specs=pl.BlockSpec((tile, 2 * columns), lambda r: (r, 0)),
        out_shape=jax.ShapeDtypeStruct((rows, 2 * columns), BF16),
        compiler_params=pltpu.CompilerParams(vmem_limit_bytes=4 * 1024 * 1024),
        cost_estimate=pl.CostEstimate(
            flops=2 * rows * columns, bytes_accessed=12 * rows * columns, transcendentals=0
        ),
    )(jnp.reshape(core, (1,)).astype(jnp.int32), own, up, down, arrived)


def on_device(span_act, q_weight, out_grad, neighbour_kv, neighbour_ids, owner):
    rows, width = out_grad.shape
    depth = q_weight.shape[0]
    seq_count = lax.axis_size("seq")
    dp_count = lax.axis_size("dp")
    tensor_count = lax.axis_size("tensor")
    couples = dp_count // 2
    seq_at = lax.axis_index("seq")
    dp_at = lax.axis_index("dp")
    tensor_at = lax.axis_index("tensor")
    core = dp_at % 2
    spans = rows // SPAN
    capacity = neighbour_kv.shape[0]
    pairs = capacity // seq_count
    whole_blocks = pairs == spans
    per = span_act.shape[1] // depth // 2
    half = width // 2
    opposite = tensor_count // 2

    def columns_of(which):
        return jnp.concatenate(
            [
                lax.dynamic_slice(span_act, (0, (2 * p + which) * depth), (rows, depth))
                for p in range(per)
            ],
            axis=1,
        )

    act_both = jnp.concatenate([columns_of(core), swap(columns_of(1 - core))], axis=0)

    act_both, q_weight = lax.optimization_barrier((act_both, q_weight))
    acts = gather_ring(act_both, "tensor", tensor_count, opposite - 1)
    along_seq = gather_ring(q_weight, "seq", seq_count)
    along_dp = gather_ring(q_weight, "dp", couples)

    groups = owner.reshape(seq_count, dp_count, spans)
    groups = lax.dynamic_index_in_dim(groups, dp_at, 1, keepdims=False)
    mine = lax.dynamic_index_in_dim(groups, seq_at, 0, keepdims=False)

    def order(group, target):
        names = group == target
        at = jnp.arange(spans)
        ahead = (names[None, :] & ~names[:, None]) | (
            (names[None, :] == names[:, None]) & (at[None, :] < at[:, None])
        )
        return jnp.sum(ahead.astype(jnp.int32), axis=1), names.astype(jnp.int32)

    def message(target):
        place, names = order(mine, target)
        hit = place[None, :] == jnp.arange(pairs)[:, None]
        return hit & (names[None, :] == 1)

    def to_owner(value, step):
        value = value.reshape(spans, SPAN, -1)
        if not whole_blocks:
            hit = message((seq_at + step) % seq_count)
            value = jnp.sum(
                jnp.where(hit[:, :, None, None], value[None], jnp.zeros((), BF16)), axis=1
            )
        return shift(value, "seq", step) if step else value

    sources = [(seq_at - step) % seq_count for step in range(seq_count)]
    staged = [stage(neighbour_kv, source, pairs) for source in sources]
    near = [k for k in range(tensor_count) if k != opposite]
    cut = width * 5 // 8 // HD * HD
    left_from = [block[:, :cut] for block in along_seq[1:]]
    right_from = [block[:, cut:] for block in along_dp[1:]]
    grads = [[to_owner(out_grad[:, :half], step) for step in range(seq_count)]]

    def block_at(i, j):
        block = ((seq_at - i) % seq_count) * dp_count + ((dp_at // 2 - j) % couples) * 2
        return block // (2 * per), (block % (2 * per)) // 2

    def placed(weights, piece, i, j, start):
        at, inner = block_at(i, j)
        return lax.dynamic_update_slice(weights, piece[None], (at, inner * depth, start))

    places = [(i, j) for i in range(seq_count) for j in range(couples)]
    weights = jnp.zeros((tensor_count, per * depth, width), BF16)
    weights = placed(weights, q_weight, 0, 0, 0)
    left_from, right_from, found, staged, grads, weights = lax.optimization_barrier(
        (left_from, right_from, [acts[k] for k in near], staged, grads, weights)
    )
    acts = found[:opposite] + [None] + found[opposite:]

    corner_left = [gather_ring(block, "dp", couples) for block in left_from]
    corner_right = [gather_ring(block, "seq", seq_count) for block in right_from]
    up = shift(acts[opposite - 1][:rows], "tensor", 1)
    down = shift(acts[opposite + 1][rows:], "tensor", -1)
    acts[opposite] = jnp.concatenate([up, down], axis=0)
    grad_out = after(out_grad[:, half:], corner_right)
    grads.append([to_owner(grad_out, step) for step in range(seq_count)])
    depth_blocks = [(tensor_at - k) % tensor_count for k in range(tensor_count)]
    table = jnp.stack(depth_blocks).astype(jnp.int32)

    for i, j in places[1:]:
        if j == 0:
            pieces = [(along_seq[i], 0)]
        elif i == 0:
            pieces = [(along_dp[j], 0)]
        else:
            pieces = [(corner_left[i - 1][j], 0), (corner_right[j - 1][i], cut)]
        for piece, start in pieces:
            weights = placed(weights, piece, i, j, start)

    def from_owner(value, step):
        value = shift(value, "seq", -step) if step else value
        if not whole_blocks:
            hit = message((seq_at + step) % seq_count)
            value = jnp.sum(
                jnp.where(hit[:, :, None, None], value[:, None], jnp.zeros((), BF16)), axis=0
            )
        return value.reshape(rows, -1)

    def slots_of(step):
        group = lax.dynamic_index_in_dim(groups, sources[step], 0, keepdims=False)
        place, names = order(group, seq_at)
        if not whole_blocks:
            place = jnp.arange(pairs)
            names = (place < jnp.sum(names)).astype(jnp.int32)
        return place, names, sources[step]

    live = jnp.broadcast_to((neighbour_ids != 0).astype(F32)[:, :, None], (capacity, KEYS, HD))
    slots = [slots_of(step) for step in range(seq_count)]

    queries = []
    for part in range(2):
        partial = product(acts, weights, table, part * half, half)
        arrived = swap(partial[rows:])
        if part:
            partial = after(partial, grads[1])
        queries.append((partial[:rows] + arrived).astype(BF16))
    asked = [[to_owner(value, step) for step in range(seq_count)] for value in queries]
    asked[0][0] = after(asked[0][0], queries[1])

    stacked = jnp.stack(after(acts, queries[1]))

    def act_block(i, j):
        at, inner = block_at(i, j)
        k = (tensor_at - at) % tensor_count
        return lax.dynamic_slice(stacked, (k, 0, inner * depth), (1, 2 * rows, depth))[0]

    def weight_product(i, j, grad):
        found = dot(act_block(i, j), grad, ((0,), (0,)))
        return lax.optimization_barrier(found.astype(BF16))

    kv_grad = None
    answers = [[None] * seq_count for _ in range(2)]
    calls = [(0, 0), (1, 0)] + [(part, step) for part in range(2) for step in range(1, seq_count)]
    for part, step in calls:
        answer, kv_grad = attend(
            *slots[step],
            asked[part][step],
            grads[part][step],
            staged[step][part],
            live,
            part,
            kv_grad,
        )
        answers[part][step] = from_owner(answer, step)

    far_weights = lax.dynamic_index_in_dim(weights, depth_blocks[opposite], 0, keepdims=False)
    far_weights = after(far_weights, queries[1])
    both_grads, corners = [], []
    corner_places = [(i, j) for i in range(1, seq_count) for j in range(1, couples)]
    for part in range(2):
        if part:
            answers[1][-1] = after(answers[1][-1], corners[0][corner_places[-1]])
        grad = sum(answers[part][1:], answers[part][0])
        both_grads.append(jnp.concatenate([grad, swap(grad)], axis=0))
        if part == 0:
            corners.append({at: weight_product(*at, both_grads[0]) for at in corner_places[::-1]})
    both_grad = jnp.concatenate(both_grads, axis=1)

    def act_product(k, block=None):
        if block is None:
            block = lax.dynamic_index_in_dim(weights, depth_blocks[k], 0, keepdims=False)
        return lax.optimization_barrier(dot(both_grad, block, ((1,), (1,))).astype(BF16))

    far = act_product(opposite, far_weights)
    up, down = shift(far[:rows], "tensor", 1), shift(far[rows:], "tensor", -1)

    late_grad = after(both_grads[1], far)
    corners.append({at: weight_product(*at, late_grad) for at in corner_places[::-1]})
    left = [
        reduce_rings([([None] + [corners[0][i, j] for j in range(1, couples)], True)], "dp")[0][1:]
        for i in range(1, seq_count)
    ]
    right = [
        reduce_rings([([None] + [corners[1][i, j] for i in range(1, seq_count)], True)], "seq")[0][1:]
        for j in range(1, couples)
    ]
    act_parts = {k: act_product(k) for k in range(tensor_count) if k != opposite}
    own = weight_product(0, 0, both_grad)
    beside_seq = [weight_product(i, 0, both_grad) for i in range(1, seq_count)]
    beside_dp = [weight_product(0, j, both_grad) for j in range(1, couples)]
    up, down, left, right, act_parts, own, beside_seq, beside_dp = lax.optimization_barrier(
        (up, down, left, right, act_parts, own, beside_seq, beside_dp)
    )

    beside_seq = [
        lax.dynamic_update_slice(block, total([block[:, :half]] + came).astype(BF16), (0, 0))
        for block, came in zip(beside_seq, left)
    ]
    from_seq = reduce_rings([([None] + beside_seq, True)], "seq")[0][1:]
    for m in range(opposite - 1, 0, -1):
        block = act_parts[tensor_count - m]
        if up.shape[0] == rows:
            up = lax.dynamic_update_slice(block, total([block[:rows], up]).astype(BF16), (0, 0))
        else:
            up = total([block, up]).astype(BF16)
        block = act_parts[m]
        if down.shape[0] == rows:
            down = lax.dynamic_update_slice(
                block, total([block[rows:], down]).astype(BF16), (rows, 0)
            )
        else:
            down = total([block, down]).astype(BF16)
        up, down = shift(up, "tensor", 1), shift(down, "tensor", -1)
    beside_dp = [
        lax.dynamic_update_slice(block, total([block[:, half:]] + came).astype(BF16), (0, half))
        for block, came in zip(beside_dp, right)
    ]
    from_dp = reduce_rings([([None] + beside_dp, True)], "dp")[0][1:]

    weight_grad = summed([own] + from_seq + from_dp)
    arrived = swap(total([part[rows:] for part in (act_parts[0], up, down)]).astype(BF16))
    act_grad = assemble(after(core, weight_grad), act_parts[0], up, down, arrived, depth)
    return (act_grad, weight_grad, kv_grad)


def solution(mesh):
    in_specs = (
        P(("seq", "dp"), "tensor"),
        P(("seq", "dp"), "tensor"),
        P(("seq", "dp"), "tensor"),
        P(("seq", "dp"), None, None, "tensor"),
        P(("seq", "dp"), None),
        P(),
    )
    out_specs = (
        P(("seq", "dp"), "tensor"),
        P(("seq", "dp"), "tensor"),
        P(("seq", "dp"), None, None, "tensor"),
    )
    return jax.shard_map(
        on_device, mesh=mesh, in_specs=in_specs, out_specs=out_specs, check_vma=False
    )
```

```python
import functools

import jax
import jax.numpy as jnp
from jax import lax
from jax.experimental import pallas as pl
from jax.experimental.pallas import tpu as pltpu
from jax.sharding import PartitionSpec as P

HD = 128
SPAN = 64
KEYS = 256
F32 = jnp.float32
BF16 = jnp.bfloat16


def dot(a, b, contract):
    return lax.dot_general(a, b, (contract, ((), ())), preferred_element_type=F32)


def shift(value, axis, step=1):
    stride = 2 if axis == "dp" else 1
    size = lax.axis_size(axis)
    return lax.ppermute(value, axis, [(i, (i + step * stride) % size) for i in range(size)])


def swap(value):
    return lax.ppermute(value, "dp", [(i, i ^ 1) for i in range(lax.axis_size("dp"))])


def after(value, *others):
    return lax.optimization_barrier((value, *others))[0]


def reaches(size, far_up):
    up = size // 2 if far_up else (size - 1) // 2
    return up, size - 1 - up


def gather_ring(block, axis, size, rounds=None):
    blocks = [block] + [None] * (size - 1)
    for m in range(1, (size // 2 if rounds is None else rounds) + 1):
        came = {}
        for sign, count in zip((1, -1), reaches(size, True)):
            if m <= count:
                came[(sign * m) % size] = shift(blocks[(sign * (m - 1)) % size], axis, sign)
        for k, value in zip(came, lax.optimization_barrier(tuple(came.values()))):
            blocks[k] = value
    return blocks


def reduce_rings(streams, axis):
    size = len(streams[0][0])
    found = [[blocks[0]] for blocks, _ in streams]
    came = {}
    for m in range(1, size // 2 + 1):
        sent = {}
        for s, (blocks, far_up) in enumerate(streams):
            for sign, count in zip((1, -1), reaches(size, far_up)):
                if m <= count:
                    block = blocks[(-sign * (count - m + 1)) % size]
                    if m > 1:
                        block = came[s, sign].astype(F32) + block.astype(F32)
                    sent[s, sign] = shift(block.astype(BF16), axis, sign)
        came = dict(zip(sent, lax.optimization_barrier(tuple(sent.values()))))
        for (s, sign), block in came.items():
            if m == reaches(size, streams[s][1])[0 if sign == 1 else 1]:
                found[s].append(block)
    return found


def total(values):
    return functools.reduce(lambda a, b: a + b, [value.astype(F32) for value in values])


def product_kernel(count, start, table_ref, *refs):
    blocks, weight_ref, out_ref = refs[:count], refs[count], refs[count + 1]
    tile = min(256, out_ref.shape[1])
    for at in range(0, out_ref.shape[1], tile):
        total = None
        for k in range(count):
            weight = weight_ref[table_ref[k], :, start + at:start + at + tile]
            part = dot(blocks[k][...], weight, ((1,), (0,)))
            total = part if total is None else total + part
        out_ref[:, at:at + tile] = total


def product(blocks, weights, table, start, width):
    count, (rows, depth) = len(blocks), blocks[0].shape
    return pl.pallas_call(
        functools.partial(product_kernel, count, start),
        out_shape=jax.ShapeDtypeStruct((rows, width), F32),
        in_specs=[pl.BlockSpec(memory_space=pltpu.SMEM)]
        + [pl.BlockSpec(memory_space=pltpu.VMEM)] * (count + 1),
        out_specs=pl.BlockSpec(memory_space=pltpu.VMEM),
        compiler_params=pltpu.CompilerParams(vmem_limit_bytes=4 * 1024 * 1024),
        cost_estimate=pl.CostEstimate(
            flops=2 * rows * count * depth * width,
            bytes_accessed=2 * count * depth * (rows + width) + 4 * rows * width,
            transcendentals=0,
        ),
    )(table, *blocks, weights)


def attend_block(q_ref, g_ref, kv_ref, live_ref, dq_ref, grad_ref):
    pairs = q_ref.shape[-1] // HD // 2
    scale = HD ** (-0.5)
    live = live_ref[...].astype(F32) > 0.5
    zero = jnp.zeros((SPAN, HD), BF16)

    def diagonal(ref, start):
        one = ref[:, start:start + HD]
        two = ref[:, start + HD:start + 2 * HD]
        return jnp.concatenate(
            [jnp.concatenate([one, zero], axis=1), jnp.concatenate([zero, two], axis=1)], axis=0
        )

    def first(pair):
        start = pair * 2 * HD
        columns = slice(start, start + 2 * HD)
        scores = dot(kv_ref[0, :, columns], diagonal(q_ref, start), ((1,), (1,)))
        prob_grad = dot(kv_ref[1, :, columns], diagonal(g_ref, start), ((1,), (1,)))
        return scores, prob_grad

    ahead = first(0)
    for pair in range(pairs):
        scores, prob_grad = ahead
        if pair + 1 < pairs:
            ahead = first(pair + 1)
        start = pair * 2 * HD
        columns = slice(start, start + 2 * HD)
        scores = jnp.where(live, scores * scale, -1e30)
        expo = jnp.exp(scores - jnp.max(scores, axis=0, keepdims=True))
        probs = expo * (1.0 / jnp.sum(expo, axis=0, keepdims=True))
        center = jnp.sum(probs * prob_grad, axis=0, keepdims=True)
        score_grad = (probs * (prob_grad - center) * scale).astype(BF16)
        value_grad = dot(probs.astype(BF16), diagonal(g_ref, start), ((1,), (0,)))
        key_grad = dot(score_grad, diagonal(q_ref, start), ((1,), (0,)))
        both = dot(score_grad, kv_ref[0, :, columns], ((0,), (0,)))
        grad_ref[1, :, columns] = value_grad.astype(BF16)
        grad_ref[0, :, columns] = key_grad.astype(BF16)
        dq_ref[:, columns] = jnp.concatenate([both[:SPAN, :HD], both[SPAN:, HD:]], axis=1).astype(
            BF16
        )


def attend_kernel(table_ref, q_ref, g_ref, live_ref, kv_ref, *rest):
    dq_ref, grad_ref = rest[-2:]
    named = table_ref[pl.num_programs(0) + pl.program_id(0)]

    @pl.when(named == 0)
    def _():
        dq_ref[...] = jnp.zeros_like(dq_ref)
        grad_ref[...] = jnp.zeros_like(grad_ref)

    @pl.when(named != 0)
    def _():
        refs = (q_ref, g_ref, kv_ref, live_ref, dq_ref, grad_ref)
        attend_block(*(ref.at[0] for ref in refs))


def attend(place, named, source, queries, grads, kv, live, part, before):
    count, _, width = queries.shape
    capacity, keys, _ = live.shape
    heads = width // HD
    table = jnp.concatenate([place, named, source * count + place]).astype(jnp.int32)
    span_block = pl.BlockSpec((1, SPAN, width), lambda r, t: (r, 0, 0))
    live_block = pl.BlockSpec((1, keys, HD), lambda r, t: (t[2 * count + r], 0, 0))
    kv_block = pl.BlockSpec((1, 2, keys, width), lambda r, t: (t[r], 0, 0, 0))
    grad_block = pl.BlockSpec((1, 2, keys, width), lambda r, t: (t[2 * count + r], 0, 0, part))
    in_specs = [span_block, span_block, live_block, kv_block]
    operands = [table, queries, grads, live, kv]
    aliases = {}
    if before is not None:
        in_specs.append(pl.BlockSpec(memory_space=pl.ANY))
        operands.append(before)
        aliases = {len(operands) - 1: 1}
    return pl.pallas_call(
        attend_kernel,
        grid_spec=pltpu.PrefetchScalarGridSpec(
            num_scalar_prefetch=1,
            grid=(count,),
            in_specs=in_specs,
            out_specs=[span_block, grad_block],
        ),
        out_shape=[
            jax.ShapeDtypeStruct(queries.shape, BF16),
            jax.ShapeDtypeStruct((capacity, 2, keys, 2 * width), BF16),
        ],
        input_output_aliases=aliases,
        compiler_params=pltpu.CompilerParams(vmem_limit_bytes=6 * 1024 * 1024),
        cost_estimate=pl.CostEstimate(
            flops=count * heads * 5 * 2 * SPAN * keys * HD * 4,
            bytes_accessed=count * 4 * keys * width * 2,
            transcendentals=count * heads * SPAN * keys,
        ),
    )(*operands)


def stage_kernel(source_ref, kv_ref, left_ref, right_ref):
    width = left_ref.shape[-1]
    left_ref[...] = kv_ref[:, :, :, :width]
    right_ref[...] = kv_ref[:, :, :, width:]


def stage(kv, source, count):
    _, _, keys, width = kv.shape
    half_block = pl.BlockSpec((1, 2, keys, width // 2), lambda r, t: (r, 0, 0, 0))
    half_shape = jax.ShapeDtypeStruct((count, 2, keys, width // 2), kv.dtype)
    return pl.pallas_call(
        stage_kernel,
        grid_spec=pltpu.PrefetchScalarGridSpec(
            num_scalar_prefetch=1,
            grid=(count,),
            in_specs=[
                pl.BlockSpec((1, 2, keys, width), lambda r, t: (t[0] * count + r, 0, 0, 0))
            ],
            out_specs=[half_block, half_block],
        ),
        out_shape=[half_shape, half_shape],
        compiler_params=pltpu.CompilerParams(vmem_limit_bytes=8 * 1024 * 1024),
        cost_estimate=pl.CostEstimate(
            flops=0, bytes_accessed=8 * count * keys * width, transcendentals=0
        ),
    )(jnp.reshape(source, (1,)).astype(jnp.int32), kv)


def total_kernel(tile, *refs):
    out_ref, buf, sem = refs[-3:]
    copies = []
    for n in range(sem.shape[0]):
        some = pl.ds(n * tile, tile)
        buf[some] = total([ref[some] for ref in refs[:-3]])
        copies.append(pltpu.make_async_copy(buf.at[some], out_ref.at[some], sem.at[n]))
        copies[-1].start()
    for copy in copies:
        copy.wait()


def summed(values):
    rows, columns = values[0].shape
    tile = min(64, rows)
    return pl.pallas_call(
        functools.partial(total_kernel, tile),
        in_specs=[pl.BlockSpec(memory_space=pltpu.VMEM)] * len(values),
        out_specs=pl.BlockSpec(memory_space=pl.ANY),
        out_shape=jax.ShapeDtypeStruct((rows, columns), F32),
        scratch_shapes=[
            pltpu.VMEM((rows, columns), F32),
            pltpu.SemaphoreType.DMA((rows // tile,)),
        ],
        compiler_params=pltpu.CompilerParams(vmem_limit_bytes=6 * 1024 * 1024),
        cost_estimate=pl.CostEstimate(
            flops=len(values) * rows * columns,
            bytes_accessed=(2 * len(values) + 4) * rows * columns,
            transcendentals=0,
        ),
    )(*values)


def assemble_kernel(depth, core_ref, own_ref, up_ref, down_ref, arrived_ref, out_ref):
    kept = own_ref[...].astype(F32) + up_ref[...].astype(F32) + down_ref[...].astype(F32)
    kept = kept.astype(BF16)
    for p in range(kept.shape[1] // depth):
        columns = slice(p * depth, (p + 1) * depth)
        mine, other = 2 * p + core_ref[0], 2 * p + 1 - core_ref[0]
        out_ref[:, pl.ds(pl.multiple_of(mine * depth, depth), depth)] = kept[:, columns]
        out_ref[:, pl.ds(pl.multiple_of(other * depth, depth), depth)] = arrived_ref[:, columns]


def assemble(core, own, up, down, arrived, depth):
    rows, columns = arrived.shape
    tile = min(64, rows)
    block = pl.BlockSpec((tile, columns), lambda r: (r, 0))
    return pl.pallas_call(
        functools.partial(assemble_kernel, depth),
        grid=(rows // tile,),
        in_specs=[pl.BlockSpec(memory_space=pltpu.SMEM)] + [block] * 4,
        out_specs=pl.BlockSpec((tile, 2 * columns), lambda r: (r, 0)),
        out_shape=jax.ShapeDtypeStruct((rows, 2 * columns), BF16),
        compiler_params=pltpu.CompilerParams(vmem_limit_bytes=4 * 1024 * 1024),
        cost_estimate=pl.CostEstimate(
            flops=2 * rows * columns, bytes_accessed=12 * rows * columns, transcendentals=0
        ),
    )(jnp.reshape(core, (1,)).astype(jnp.int32), own, up, down, arrived)


def on_device(span_act, q_weight, out_grad, neighbour_kv, neighbour_ids, owner):
    rows, width = out_grad.shape
    depth = q_weight.shape[0]
    seq_count = lax.axis_size("seq")
    dp_count = lax.axis_size("dp")
    tensor_count = lax.axis_size("tensor")
    couples = dp_count // 2
    seq_at = lax.axis_index("seq")
    dp_at = lax.axis_index("dp")
    tensor_at = lax.axis_index("tensor")
    core = dp_at % 2
    spans = rows // SPAN
    capacity = neighbour_kv.shape[0]
    pairs = capacity // seq_count
    whole_blocks = pairs == spans
    per = span_act.shape[1] // depth // 2
    half = width // 2
    opposite = tensor_count // 2

    def columns_of(which):
        return jnp.concatenate(
            [
                lax.dynamic_slice(span_act, (0, (2 * p + which) * depth), (rows, depth))
                for p in range(per)
            ],
            axis=1,
        )

    act_both = jnp.concatenate([columns_of(core), swap(columns_of(1 - core))], axis=0)

    act_both, q_weight = lax.optimization_barrier((act_both, q_weight))
    acts = gather_ring(act_both, "tensor", tensor_count, opposite - 1)
    along_seq = gather_ring(q_weight, "seq", seq_count)
    along_dp = gather_ring(q_weight, "dp", couples)

    groups = owner.reshape(seq_count, dp_count, spans)
    groups = lax.dynamic_index_in_dim(groups, dp_at, 1, keepdims=False)
    mine = lax.dynamic_index_in_dim(groups, seq_at, 0, keepdims=False)

    def order(group, target):
        names = group == target
        at = jnp.arange(spans)
        ahead = (names[None, :] & ~names[:, None]) | (
            (names[None, :] == names[:, None]) & (at[None, :] < at[:, None])
        )
        return jnp.sum(ahead.astype(jnp.int32), axis=1), names.astype(jnp.int32)

    def message(target):
        place, names = order(mine, target)
        hit = place[None, :] == jnp.arange(pairs)[:, None]
        return hit & (names[None, :] == 1)

    def to_owner(value, step):
        value = value.reshape(spans, SPAN, -1)
        if not whole_blocks:
            hit = message((seq_at + step) % seq_count)
            value = jnp.sum(
                jnp.where(hit[:, :, None, None], value[None], jnp.zeros((), BF16)), axis=1
            )
        return shift(value, "seq", step) if step else value

    sources = [(seq_at - step) % seq_count for step in range(seq_count)]
    staged = [stage(neighbour_kv, source, pairs) for source in sources]
    near = [k for k in range(tensor_count) if k != opposite]
    cut = width * 5 // 8 // HD * HD
    left_from = [block[:, :cut] for block in along_seq[1:]]
    right_from = [block[:, cut:] for block in along_dp[1:]]
    grads = [[to_owner(out_grad[:, :half], step) for step in range(seq_count)]]

    def block_at(i, j):
        block = ((seq_at - i) % seq_count) * dp_count + ((dp_at // 2 - j) % couples) * 2
        return block // (2 * per), (block % (2 * per)) // 2

    def placed(weights, piece, i, j, start):
        at, inner = block_at(i, j)
        return lax.dynamic_update_slice(weights, piece[None], (at, inner * depth, start))

    places = [(i, j) for i in range(seq_count) for j in range(couples)]
    weights = jnp.zeros((tensor_count, per * depth, width), BF16)
    weights = placed(weights, q_weight, 0, 0, 0)
    left_from, right_from, found, staged, grads, weights = lax.optimization_barrier(
        (left_from, right_from, [acts[k] for k in near], staged, grads, weights)
    )
    acts = found[:opposite] + [None] + found[opposite:]

    corner_left = [gather_ring(block, "dp", couples) for block in left_from]
    corner_right = [gather_ring(block, "seq", seq_count) for block in right_from]
    up = shift(acts[opposite - 1][:rows], "tensor", 1)
    down = shift(acts[opposite + 1][rows:], "tensor", -1)
    acts[opposite] = jnp.concatenate([up, down], axis=0)
    grad_out = after(out_grad[:, half:], corner_right)
    grads.append([to_owner(grad_out, step) for step in range(seq_count)])
    depth_blocks = [(tensor_at - k) % tensor_count for k in range(tensor_count)]
    table = jnp.stack(depth_blocks).astype(jnp.int32)

    for i, j in places[1:]:
        if j == 0:
            pieces = [(along_seq[i], 0)]
        elif i == 0:
            pieces = [(along_dp[j], 0)]
        else:
            pieces = [(corner_left[i - 1][j], 0), (corner_right[j - 1][i], cut)]
        for piece, start in pieces:
            weights = placed(weights, piece, i, j, start)

    def from_owner(value, step):
        value = shift(value, "seq", -step) if step else value
        if not whole_blocks:
            hit = message((seq_at + step) % seq_count)
            value = jnp.sum(
                jnp.where(hit[:, :, None, None], value[:, None], jnp.zeros((), BF16)), axis=0
            )
        return value.reshape(rows, -1)

    def slots_of(step):
        group = lax.dynamic_index_in_dim(groups, sources[step], 0, keepdims=False)
        place, names = order(group, seq_at)
        if not whole_blocks:
            place = jnp.arange(pairs)
            names = (place < jnp.sum(names)).astype(jnp.int32)
        return place, names, sources[step]

    live = jnp.broadcast_to((neighbour_ids != 0).astype(BF16)[:, :, None], (capacity, KEYS, HD))
    slots = [slots_of(step) for step in range(seq_count)]

    queries = []
    for part in range(2):
        partial = product(acts, weights, table, part * half, half)
        arrived = swap(partial[rows:])
        if part:
            partial = after(partial, grads[1])
        queries.append((partial[:rows] + arrived).astype(BF16))
    asked = [[to_owner(value, step) for step in range(seq_count)] for value in queries]
    asked[0][0] = after(asked[0][0], queries[1])

    stacked = jnp.stack(after(acts, queries[1]))

    def act_block(i, j):
        at, inner = block_at(i, j)
        k = (tensor_at - at) % tensor_count
        return lax.dynamic_slice(stacked, (k, 0, inner * depth), (1, 2 * rows, depth))[0]

    def weight_product(i, j, grad):
        found = dot(act_block(i, j), grad, ((0,), (0,)))
        return lax.optimization_barrier(found.astype(BF16))

    kv_grad = None
    answers = [[None] * seq_count for _ in range(2)]
    calls = [(0, 0), (1, 0)] + [(part, step) for part in range(2) for step in range(1, seq_count)]
    for part, step in calls:
        answer, kv_grad = attend(
            *slots[step],
            asked[part][step],
            grads[part][step],
            staged[step][part],
            live,
            part,
            kv_grad,
        )
        answers[part][step] = from_owner(answer, step)

    far_weights = lax.dynamic_index_in_dim(weights, depth_blocks[opposite], 0, keepdims=False)
    far_weights = after(far_weights, queries[1])
    both_grads, corners = [], []
    corner_places = [(i, j) for i in range(1, seq_count) for j in range(1, couples)]
    for part in range(2):
        if part:
            answers[1][-1] = after(answers[1][-1], corners[0][corner_places[-1]])
        grad = sum(answers[part][1:], answers[part][0])
        both_grads.append(jnp.concatenate([grad, swap(grad)], axis=0))
        if part == 0:
            corners.append({at: weight_product(*at, both_grads[0]) for at in corner_places[::-1]})
    both_grad = jnp.concatenate(both_grads, axis=1)

    def act_product(k, block=None):
        if block is None:
            block = lax.dynamic_index_in_dim(weights, depth_blocks[k], 0, keepdims=False)
        return lax.optimization_barrier(dot(both_grad, block, ((1,), (1,))).astype(BF16))

    far = act_product(opposite, far_weights)
    up, down = shift(far[:rows], "tensor", 1), shift(far[rows:], "tensor", -1)

    late_grad = after(both_grads[1], far)
    corners.append({at: weight_product(*at, late_grad) for at in corner_places[::-1]})
    left = [
        reduce_rings([([None] + [corners[0][i, j] for j in range(1, couples)], True)], "dp")[0][1:]
        for i in range(1, seq_count)
    ]
    right = [
        reduce_rings([([None] + [corners[1][i, j] for i in range(1, seq_count)], True)], "seq")[0][1:]
        for j in range(1, couples)
    ]
    act_parts = {k: act_product(k) for k in range(tensor_count) if k != opposite}
    own = weight_product(0, 0, both_grad)
    beside_seq = [weight_product(i, 0, both_grad) for i in range(1, seq_count)]
    beside_dp = [weight_product(0, j, both_grad) for j in range(1, couples)]
    up, down, left, right, act_parts, own, beside_seq, beside_dp = lax.optimization_barrier(
        (up, down, left, right, act_parts, own, beside_seq, beside_dp)
    )

    beside_seq = [
        lax.dynamic_update_slice(block, total([block[:, :half]] + came).astype(BF16), (0, 0))
        for block, came in zip(beside_seq, left)
    ]
    from_seq = reduce_rings([([None] + beside_seq, True)], "seq")[0][1:]
    for m in range(opposite - 1, 0, -1):
        block = act_parts[tensor_count - m]
        if up.shape[0] == rows:
            up = lax.dynamic_update_slice(block, total([block[:rows], up]).astype(BF16), (0, 0))
        else:
            up = total([block, up]).astype(BF16)
        block = act_parts[m]
        if down.shape[0] == rows:
            down = lax.dynamic_update_slice(
                block, total([block[rows:], down]).astype(BF16), (rows, 0)
            )
        else:
            down = total([block, down]).astype(BF16)
        up, down = shift(up, "tensor", 1), shift(down, "tensor", -1)
    beside_dp = [
        lax.dynamic_update_slice(block, total([block[:, half:]] + came).astype(BF16), (0, half))
        for block, came in zip(beside_dp, right)
    ]
    from_dp = reduce_rings([([None] + beside_dp, True)], "dp")[0][1:]

    weight_grad = summed([own] + from_seq + from_dp)
    arrived = swap(total([part[rows:] for part in (act_parts[0], up, down)]).astype(BF16))
    act_grad = assemble(after(core, weight_grad), act_parts[0], up, down, arrived, depth)
    return (act_grad, weight_grad, kv_grad)


def solution(mesh):
    in_specs = (
        P(("seq", "dp"), "tensor"),
        P(("seq", "dp"), "tensor"),
        P(("seq", "dp"), "tensor"),
        P(("seq", "dp"), None, None, "tensor"),
        P(("seq", "dp"), None),
        P(),
    )
    out_specs = (
        P(("seq", "dp"), "tensor"),
        P(("seq", "dp"), "tensor"),
        P(("seq", "dp"), None, None, "tensor"),
    )
    return jax.shard_map(
        on_device, mesh=mesh, in_specs=in_specs, out_specs=out_specs, check_vma=False
    )
```
